32 devices in a mesh: dp: 2 (over core), seq: 4 (over z), mp: 4 (over y, x).
Axes of the slice: x: 2, y: 2, z: 4, core: 2. Of those that a mesh axis runs over, the one named last changes fastest.
Arguments:
- tokens: bfloat16 [2, 4096, 2304], P('dp', 'seq'), may hold values from -27 to 27
- cotangent: bfloat16 [2, 4096, 2304], P('dp', 'seq'), may hold values from -6 to 6
- pre_attn_gain: bfloat16 [2304], P(('dp', 'seq')), may hold values from 0.099609375 to 1.8984375
- w_query: bfloat16 [2304, 2048], P(('dp', 'seq'), 'mp'), may hold values from -4 to 4
- w_key: bfloat16 [2304, 1024], P(('dp', 'seq')), may hold values from -2 to 2
- w_value: bfloat16 [2304, 1024], P(('dp', 'seq')), may hold values from -0.125 to 0.125
- w_out: bfloat16 [2048, 2304], P('mp', ('dp', 'seq')), may hold values from -0.375 to 0.375
- post_attn_gain: bfloat16 [2304], P(('dp', 'seq')), may hold values from 0.099609375 to 1.8984375
- pre_ffw_gain: bfloat16 [2304], P(('dp', 'seq')), may hold values from 0.099609375 to 1.8984375
- w_gate: bfloat16 [2304, 9216], P(('dp', 'seq'), 'mp'), may hold values from -0.125 to 0.125
- w_up: bfloat16 [2304, 9216], P(('dp', 'seq'), 'mp'), may hold values from -0.125 to 0.125
- w_down: bfloat16 [9216, 2304], P('mp', ('dp', 'seq')), may hold values from -0.0625 to 0.0625
- post_ffw_gain: bfloat16 [2304], P(('dp', 'seq')), may hold values from 0.099609375 to 1.8984375
Outputs:
- output: bfloat16 [2, 4096, 2304], P('dp', ('seq', 'mp'))
- tokens_grad: bfloat16 [2, 4096, 2304], P('dp', ('seq', 'mp'))
- pre_attn_gain_grad: float32 [2304], P(('dp', 'seq'))
- w_query_grad: float32 [2304, 2048], P(('dp', 'seq'), 'mp')
- w_key_grad: float32 [2304, 1024], P(('dp', 'seq'))
- w_value_grad: float32 [2304, 1024], P(('dp', 'seq'))
- w_out_grad: float32 [2048, 2304], P('mp', ('dp', 'seq'))
- post_attn_gain_grad: float32 [2304], P(('dp', 'seq'))
- pre_ffw_gain_grad: float32 [2304], P(('dp', 'seq'))
- w_gate_grad: float32 [2304, 9216], P(('dp', 'seq'), 'mp')
- w_up_grad: float32 [2304, 9216], P(('dp', 'seq'), 'mp')
- w_down_grad: float32 [9216, 2304], P('mp', ('dp', 'seq'))
- post_ffw_gain_grad: float32 [2304], P(('dp', 'seq'))
The draws below stay inside these ranges and needn't reach their ends.
All inputs are finite; a program needn't handle non-finite values.
Results may differ from the reference program's by a relative error of at most 0.022.
The reference program's roundings to bfloat16 on the way count: a program that leaves them out, or rounds other values in their place, can miss the bound.
Values may be sent and summed in bfloat16 or wider, within the bound.
A program may use at most 256 MiB of HBM per device.

```python
import jax
import jax.numpy as jnp
from jax import lax

D = 2304
FF = 9216
Q_HEADS = 8
KV_HEADS = 4
HEAD_DIM = 256
WINDOW = 4096
SEQS = 2
LENGTH = 4096


def draw_tokens(key, part):
    key = jax.random.fold_in(key, 11)
    value_key, row_key, column_key = jax.random.split(key, 3)
    entries = jnp.clip(jax.random.normal(value_key, (SEQS, LENGTH, D), jnp.float32), -4.0, 4.0)
    row_scale = jnp.exp(jax.random.uniform(row_key, (SEQS, LENGTH, 1), jnp.float32, -1.2, 1.2))
    column_scale = jnp.exp(jax.random.uniform(column_key, (1, 1, D), jnp.float32, -0.7, 0.7))
    return (entries * row_scale * column_scale).astype(jnp.bfloat16)


def scale_heads(entries, order_key, head_count, top_factor):
    ladder = top_factor ** (jnp.arange(head_count, dtype=jnp.float32) / max(head_count - 1, 1))
    order = jax.random.permutation(order_key, head_count)
    factor = jnp.repeat(ladder[order], HEAD_DIM)
    return (entries * factor[None, :] * D ** (-0.5)).astype(jnp.bfloat16)


def draw_w_query(key, part):
    key = jax.random.fold_in(key, 21)
    entry_key, order_key = jax.random.split(key)
    entries = jnp.clip(jax.random.normal(entry_key, (D, Q_HEADS * HEAD_DIM), jnp.float32), -4.0, 4.0)
    return scale_heads(entries, order_key, Q_HEADS, 8.0)


def draw_w_key(key, part):
    key = jax.random.fold_in(key, 31)
    entry_key, order_key = jax.random.split(key)
    entries = jnp.clip(jax.random.normal(entry_key, (D, KV_HEADS * HEAD_DIM), jnp.float32), -4.0, 4.0)
    return scale_heads(entries, order_key, KV_HEADS, 4.0)


def block_scale(stream_key, dims, cuts, low, largest):
    loudness = 1.0
    for dim, parts in cuts:
        draws = jax.random.uniform(jax.random.fold_in(jax.random.fold_in(stream_key, 6), dim), (parts,), jnp.float32, low / len(cuts), largest / len(cuts))
        loudness = loudness * jnp.repeat(jnp.exp(draws), dims[dim] // parts).reshape((-1,) + (1,) * (len(dims) - 1 - dim))
    return loudness


def gaussian(own_key, dims, scale, reach, cuts=(), held_as=jnp.bfloat16):
    level = block_scale(own_key, dims, cuts, -0.22, 0.18) if cuts else 1.0
    values = jax.random.normal(own_key, dims, jnp.float32) * scale * level
    return jnp.minimum(jnp.maximum(values, -reach), reach).astype(held_as)


def setup_inputs(seed: int = 0) -> dict:
    streams_of = jax.random.split(jax.random.key(seed), 14)
    tokens = draw_tokens(jax.random.fold_in(streams_of[13], 71), 0)
    cotangent = gaussian(streams_of[1], (SEQS, LENGTH, D), 1.0, 6.0, ((0, 2), (1, 4)))
    pre_attn_gain = jnp.clip(1.0 + 0.18 * jax.random.normal(streams_of[2], (D,), jnp.float32), 0.099609375, 1.8984375).astype(jnp.bfloat16)
    w_query = draw_w_query(jax.random.fold_in(streams_of[13], 71), 0)
    w_key = draw_w_key(jax.random.fold_in(streams_of[13], 71), 0)
    w_value = gaussian(streams_of[5], (D, KV_HEADS * HEAD_DIM), D ** -0.5, 0.125, ((0, 8),))
    w_out = gaussian(streams_of[6], (Q_HEADS * HEAD_DIM, D), HEAD_DIM ** -0.5, 0.375, ((0, 4), (1, 8)))
    post_attn_gain = jnp.clip(1.0 + 0.18 * jax.random.normal(streams_of[7], (D,), jnp.float32), 0.099609375, 1.8984375).astype(jnp.bfloat16)
    pre_ffw_gain = jnp.clip(1.0 + 0.18 * jax.random.normal(streams_of[8], (D,), jnp.float32), 0.099609375, 1.8984375).astype(jnp.bfloat16)
    w_gate = gaussian(streams_of[9], (D, FF), D ** -0.5, 0.125, ((0, 8), (1, 4)))
    w_up = gaussian(streams_of[10], (D, FF), D ** -0.5, 0.125, ((0, 8), (1, 4)))
    w_down = gaussian(streams_of[11], (FF, D), FF ** -0.5, 0.0625, ((0, 4), (1, 8)))
    post_ffw_gain = jnp.clip(1.0 + 0.18 * jax.random.normal(streams_of[12], (D,), jnp.float32), 0.099609375, 1.8984375).astype(jnp.bfloat16)
    return dict(tokens=tokens, cotangent=cotangent, pre_attn_gain=pre_attn_gain, w_query=w_query, w_key=w_key, w_value=w_value, w_out=w_out, post_attn_gain=post_attn_gain, pre_ffw_gain=pre_ffw_gain, w_gate=w_gate, w_up=w_up, w_down=w_down, post_ffw_gain=post_ffw_gain)


@jax.custom_vjp
def low(v):
    return lax.optimization_barrier(v.astype(jnp.bfloat16)).astype(jnp.float32)

@jax.custom_vjp
def low_back(v):
    return v

def low_keep(v):
    return (low(v), None)

def low_pass(kept, grad):
    return (grad,)

def back_keep(v):
    return (v, None)

def back_low(kept, grad):
    return (low(grad),)
low.defvjp(low_keep, low_pass)
low_back.defvjp(back_keep, back_low)
EPSILON = 1e-06
SOFT_CAP = 50.0
ROPE_BASE = 10000.0
MASKED = -1e+30
HIGHEST = lax.Precision.HIGHEST

def matmul(left, right):
    return jnp.dot(left, right, precision=HIGHEST, preferred_element_type=jnp.float32)

def rms_norm(vector, gain):
    scale = lax.rsqrt(lax.optimization_barrier(jnp.mean(vector * vector, axis=-1, keepdims=True)) + EPSILON)
    return vector * scale * gain

def rotary(vector, positions):
    half_dim = vector.shape[-1] // 2
    frequency = ROPE_BASE ** (-jnp.arange(half_dim, dtype=jnp.float32) * 2.0 / vector.shape[-1])
    angles = positions.astype(jnp.float32)[:, None, None] * frequency
    cosine = jnp.cos(angles)
    sine = jnp.sin(angles)
    first_half = vector[..., :half_dim]
    second_half = vector[..., half_dim:]
    return jnp.concatenate([first_half * cosine - second_half * sine, second_half * cosine + first_half * sine], axis=-1)

def layer_forward(inputs, weights):
    pre_gain, query_w, key_w, value_w, out_w, post_gain, ffw_gain, gate_w, up_w, down_w, final_gain = weights
    length = inputs.shape[0]
    positions = jnp.arange(length, dtype=jnp.int32)
    normed_one = low(rms_norm(inputs, pre_gain))
    query_lin = low_back(matmul(normed_one, query_w)).reshape(length, Q_HEADS, HEAD_DIM)
    queries = low(rotary(query_lin, positions) * HEAD_DIM ** (-0.5))
    key_lin = low_back(matmul(normed_one, key_w)).reshape(length, KV_HEADS, HEAD_DIM)
    keys = low(rotary(key_lin, positions))
    values = low(low_back(matmul(normed_one, value_w))).reshape(length, KV_HEADS, HEAD_DIM)
    group_size = Q_HEADS // KV_HEADS
    block_len = min(512, length)
    padded_keys = jnp.pad(keys, ((WINDOW, 0), (0, 0), (0, 0)))
    padded_values = jnp.pad(values, ((WINDOW, 0), (0, 0), (0, 0)))

    def attend(start):
        query_block = lax.dynamic_slice_in_dim(queries, start, block_len, 0).reshape(block_len, KV_HEADS, group_size, HEAD_DIM)
        key_block = lax.dynamic_slice_in_dim(padded_keys, start, WINDOW + block_len, 0)
        value_block = lax.dynamic_slice_in_dim(padded_values, start, WINDOW + block_len, 0)
        raw_scores = low_back(jnp.einsum('qgrd,kgd->grqk', query_block, key_block, precision=HIGHEST))
        capped = SOFT_CAP * jnp.tanh(raw_scores / SOFT_CAP)
        query_pos = start + jnp.arange(block_len, dtype=jnp.int32)
        key_pos = start - WINDOW + jnp.arange(WINDOW + block_len, dtype=jnp.int32)
        distance = query_pos[:, None] - key_pos[None, :]
        inside = (distance >= 0) & (distance < WINDOW) & (key_pos[None, :] >= 0)
        masked_scores = jnp.where(inside, capped, MASKED)
        top_score = lax.optimization_barrier(jnp.max(masked_scores, axis=-1, keepdims=True))
        weights_exp = jnp.exp(masked_scores - top_score)
        probs = low(weights_exp / lax.optimization_barrier(jnp.sum(weights_exp, axis=-1, keepdims=True)))
        block_out = jnp.einsum('grqk,kgd->qgrd', probs, value_block, precision=HIGHEST)
        return block_out.reshape(block_len, Q_HEADS * HEAD_DIM)
    starts = jnp.arange(length // block_len, dtype=jnp.int32) * block_len
    attn_o = lax.map(jax.checkpoint(attend), starts).reshape(length, Q_HEADS * HEAD_DIM)
    attn_o = low(low_back(attn_o))
    attn = low_back(matmul(attn_o, out_w))
    resid = inputs + rms_norm(attn, post_gain)
    normed_two = low(rms_norm(resid, ffw_gain))
    gate_lin = low_back(matmul(normed_two, gate_w))
    up_lin = low_back(matmul(normed_two, up_w))
    hidden = low(jax.nn.gelu(gate_lin, approximate=True) * up_lin)
    mixed = low_back(matmul(hidden, down_w))
    return resid + rms_norm(mixed, final_gain)

def reference(tokens, cotangent, pre_attn_gain, w_query, w_key, w_value, w_out, post_attn_gain, pre_ffw_gain, w_gate, w_up, w_down, post_ffw_gain):
    weights = tuple((item.astype(jnp.float32) for item in (pre_attn_gain, w_query, w_key, w_value, w_out, post_attn_gain, pre_ffw_gain, w_gate, w_up, w_down, post_ffw_gain)))
    outputs = []
    input_grads = []
    totals = None
    for sequence in range(SEQS):
        result, pullback = jax.vjp(layer_forward, tokens[sequence].astype(jnp.float32), weights)
        input_grad, weight_grads = pullback(cotangent[sequence].astype(jnp.float32))
        outputs.append(result.astype(jnp.bfloat16))
        input_grads.append(input_grad.astype(jnp.bfloat16))
        totals = weight_grads if totals is None else jax.tree.map(jnp.add, totals, weight_grads)
    output = jnp.stack(outputs)
    tokens_grad = jnp.stack(input_grads)
    return (output, tokens_grad, totals[0], totals[1], totals[2], totals[3], totals[4], totals[5], totals[6], totals[7], totals[8], totals[9], totals[10])
```

```python
import functools

import jax
import jax.numpy as jnp
from jax import lax
from jax.experimental import pallas as pl
from jax.experimental.pallas import tpu as pltpu
from jax.sharding import PartitionSpec as P

Q_HEADS = 8
KV_HEADS = 4
HEAD_DIM = 256
WINDOW = 4096

EPSILON = 1e-06
SOFT_CAP = 50.0
ROPE_BASE = 10000.0
MESH = pl.DeviceIdType.MESH
VMEM_LIMIT = 56 * 1024 * 1024
LANES = 128
BF16 = jnp.bfloat16
F32 = jnp.float32


def after(value, *earlier):
    return lax.optimization_barrier((value, *earlier))[0]


def dot_nn(left, right):
    return lax.dot_general(left, right, (((1,), (0,)), ((), ())), preferred_element_type=F32)


def dot_nt(left, right):
    return lax.dot_general(left, right, (((1,), (1,)), ((), ())), preferred_element_type=F32)


def dot_tn(left, right):
    return lax.dot_general(left, right, (((0,), (0,)), ((), ())), preferred_element_type=F32)


def rms_scale(vector):
    return lax.rsqrt(jnp.mean(vector * vector, axis=-1, keepdims=True) + EPSILON)


def norm_back(grad_in, unit, scale, gain):
    gain_grad = jnp.sum(grad_in * unit, axis=0)
    unit_grad = grad_in * gain
    vector_grad = scale * (unit_grad - unit * jnp.mean(unit_grad * unit, axis=-1, keepdims=True))
    return (vector_grad, gain_grad)


def rotary(vector, cosine, sine, direction):
    half_dim = vector.shape[-1] // 2
    first_half = vector[..., :half_dim]
    second_half = vector[..., half_dim:]
    return jnp.concatenate(
        [
            first_half * cosine - direction * (second_half * sine),
            second_half * cosine + direction * (first_half * sine),
        ],
        axis=-1,
    )


def gather_kernel(sizes, x_ref, o_ref, send_sem, recv_sem):
    dp_size, seq_size = sizes
    count = dp_size * seq_size
    dp, seq, mp = lax.axis_index("dp"), lax.axis_index("seq"), lax.axis_index("mp")
    rank = dp * seq_size + seq

    def peer(k):
        other = lax.rem(rank + k, count)
        return (other // seq_size, lax.rem(other, seq_size), mp)

    barrier = pltpu.get_barrier_semaphore()
    for k in range(1, count):
        pl.semaphore_signal(barrier, inc=1, device_id=peer(k), device_id_type=MESH)
    pl.semaphore_wait(barrier, count - 1)
    copies = []
    for k in range(1, count):
        copies.append(
            pltpu.make_async_remote_copy(
                src_ref=x_ref,
                dst_ref=o_ref.at[rank],
                send_sem=send_sem.at[k],
                recv_sem=recv_sem.at[k],
                device_id=peer(k),
                device_id_type=MESH,
            )
        )
        copies[-1].start()
    o_ref[pl.ds(rank, 1)] = x_ref[...][None]
    for copy in copies:
        copy.wait()


def gather_gains(gains, dp_size, seq_size):
    count = dp_size * seq_size
    local = gains[0].shape[0]
    width = -(-local // LANES) * LANES
    block = jnp.stack([gain.astype(F32) for gain in gains])
    block = jnp.pad(block, ((0, 8 - len(gains)), (0, width - local)))
    full = pl.pallas_call(
        functools.partial(gather_kernel, (dp_size, seq_size)),
        out_shape=jax.ShapeDtypeStruct((count, 8, width), F32),
        in_specs=[pl.BlockSpec(memory_space=pltpu.VMEM)],
        out_specs=pl.BlockSpec(memory_space=pltpu.VMEM),
        scratch_shapes=[
            pltpu.SemaphoreType.DMA((count,)),
            pltpu.SemaphoreType.DMA((count,)),
        ],
        compiler_params=pltpu.CompilerParams(collective_id=1, has_side_effects=True),
    )(block)
    full = jnp.transpose(full[:, : len(gains), :local], (1, 0, 2)).reshape(len(gains), -1)
    return [full[i] for i in range(len(gains))]


def reduce_kernel(sizes, x_ref, o_ref, mine, from_mp, from_ws, sems):
    dp_size, seq_size, mp_size = sizes
    count = dp_size * seq_size
    dp, seq, mp = lax.axis_index("dp"), lax.axis_index("seq"), lax.axis_index("mp")
    rank = dp * seq_size + seq

    def mp_peer(k):
        return (dp, seq, lax.rem(mp + k, mp_size))

    def ws_rank(k):
        return lax.rem(rank + k, count)

    def ws_peer(k):
        other = ws_rank(k)
        return (other // seq_size, lax.rem(other, seq_size), mp)

    barrier = pltpu.get_barrier_semaphore()
    for k in range(1, mp_size):
        pl.semaphore_signal(barrier, inc=1, device_id=mp_peer(k), device_id_type=MESH)
    for k in range(1, count):
        pl.semaphore_signal(barrier, inc=1, device_id=ws_peer(k), device_id_type=MESH)
    pl.semaphore_wait(barrier, mp_size - 1 + count - 1)
    copies = []
    for k in range(1, mp_size):
        copies.append(
            pltpu.make_async_remote_copy(
                src_ref=x_ref,
                dst_ref=from_mp.at[k],
                send_sem=sems.at[0, k],
                recv_sem=sems.at[1, k],
                device_id=mp_peer(k),
                device_id_type=MESH,
            )
        )
        copies[-1].start()
    for copy in copies:
        copy.wait()
    total = x_ref[...]
    for k in range(1, mp_size):
        total = total + from_mp[k]
    mine[...] = total
    copies = []
    for k in range(1, count):
        copies.append(
            pltpu.make_async_remote_copy(
                src_ref=mine.at[ws_rank(k)],
                dst_ref=from_ws.at[k],
                send_sem=sems.at[2, k],
                recv_sem=sems.at[3, k],
                device_id=ws_peer(k),
                device_id_type=MESH,
            )
        )
        copies[-1].start()
    for copy in copies:
        copy.wait()
    own = mine[pl.ds(rank, 1)][0]
    for k in range(1, count):
        own = own + from_ws[k]
    o_ref[...] = own


def reduce_gains(grads, dp_size, seq_size, mp_size):
    count = dp_size * seq_size
    local = grads[0].shape[0] // count
    width = -(-local // LANES) * LANES
    block = jnp.transpose(jnp.stack(grads).reshape(len(grads), count, local), (1, 0, 2))
    block = jnp.pad(block, ((0, 0), (0, 8 - len(grads)), (0, width - local)))
    most = max(count, mp_size)
    total = pl.pallas_call(
        functools.partial(reduce_kernel, (dp_size, seq_size, mp_size)),
        out_shape=jax.ShapeDtypeStruct((8, width), F32),
        in_specs=[pl.BlockSpec(memory_space=pltpu.VMEM)],
        out_specs=pl.BlockSpec(memory_space=pltpu.VMEM),
        scratch_shapes=[
            pltpu.VMEM((count, 8, width), F32),
            pltpu.VMEM((mp_size, count, 8, width), F32),
            pltpu.VMEM((count, 8, width), F32),
            pltpu.SemaphoreType.DMA((4, most)),
        ],
        compiler_params=pltpu.CompilerParams(collective_id=2, has_side_effects=True),
    )(block)
    return [total[i, :local] for i in range(len(grads))]


def key_mask(shape, first_key, first_query, tile, far):
    key = first_key + lax.broadcasted_iota(jnp.int32, shape, 0)
    query = first_query + lax.rem(lax.broadcasted_iota(jnp.int32, shape, 1), tile)
    return key > query if far else key <= query


def for_key_tiles(tile_fn, index, tile, span, step, blocks, windowed):
    seq = lax.axis_index("seq")
    per_block = span // step
    low = jnp.maximum(seq - blocks, 0)
    if windowed:
        @pl.when(seq >= blocks)
        def _():
            tile_fn(seq - blocks, 0, span, "far")

        low = jnp.maximum(seq - blocks + 1, 0)

    def past(t, carry):
        tile_fn(lax.div(t, per_block), pl.multiple_of(lax.rem(t, per_block) * step, step), step, "")
        return carry

    lax.fori_loop(low * per_block, seq * per_block, past, 0)
    tile_fn(seq, 0, (index + 1) * tile, "near")


def attend_kernel(plan, q_ref, kv_ref, o_ref, of_ref, lse_ref, acc, total):
    tile, span, step, blocks, windowed = plan
    for i in range(q_ref.shape[0]):
        query = q_ref[i]
        rows = query.shape[0]
        acc[...] = jnp.zeros_like(acc)
        total[...] = jnp.zeros_like(total)

        def tile_fn(block, first, count, mask, i=i, query=query, rows=rows):
            key = kv_ref[block, 0, pl.ds(first, count), :]
            value = kv_ref[block, 1, pl.ds(first, count), :]
            raw = dot_nt(key, query)
            weight = jnp.exp(SOFT_CAP * jnp.tanh(raw * (1.0 / SOFT_CAP)))
            if mask:
                inside = key_mask(weight.shape, first, i * tile, tile, mask == "far")
                weight = jnp.where(inside, weight, 0.0)
            total[...] += jnp.sum(weight.reshape(count // 8, 8, rows), axis=0)
            acc[...] += dot_tn(value, weight.astype(BF16))

        for_key_tiles(tile_fn, i, tile, span, step, blocks, windowed)
        row_total = jnp.sum(total[...], axis=0, keepdims=True)
        out = (acc[...] / row_total).T
        o_ref[i] = out.astype(BF16)
        of_ref[i] = out
        lse_ref[i] = jnp.log(row_total)


def attend_back_kernel(plan, q_ref, do_ref, lse_ref, delta_ref, kv_ref, dq_ref, dkv_ref, grads, acc):
    tile, span, step, blocks, windowed = plan
    grads[...] = jnp.zeros_like(grads)
    for i in range(q_ref.shape[0]):
        query = q_ref[i]
        dout = do_ref[i]
        lse = lse_ref[i]
        delta = delta_ref[i]
        acc[...] = jnp.zeros_like(acc)

        def tile_fn(block, first, count, mask, i=i, query=query, dout=dout, lse=lse, delta=delta):
            key = kv_ref[block, 0, pl.ds(first, count), :]
            value = kv_ref[block, 1, pl.ds(first, count), :]
            bounded = jnp.tanh(dot_nt(key, query) * (1.0 / SOFT_CAP))
            prob = jnp.exp(SOFT_CAP * bounded - lse)
            if mask:
                inside = key_mask(prob.shape, first, i * tile, tile, mask == "far")
                prob = jnp.where(inside, prob, 0.0)
            dprob = dot_nt(value, dout)
            draw = (prob * (dprob - delta) * (1.0 - bounded * bounded)).astype(BF16)
            grads[block, 1, pl.ds(first, count), :] += dot_nn(prob.astype(BF16), dout)
            grads[block, 0, pl.ds(first, count), :] += dot_nn(draw, query)
            acc[...] += dot_tn(key, draw)

        for_key_tiles(tile_fn, i, tile, span, step, blocks, windowed)
        dq_ref[i] = acc[...].T
    dkv_ref[...] = grads[...].astype(BF16)


def attention_plan(span, seq_size):
    blocks = WINDOW // span
    return (min(256, span), span, min(512, span), blocks, seq_size > blocks)


def attend(queries, pairs, plan):
    tiles, rows, width = queries.shape
    return pl.pallas_call(
        functools.partial(attend_kernel, plan),
        out_shape=(
            jax.ShapeDtypeStruct(queries.shape, BF16),
            jax.ShapeDtypeStruct(queries.shape, F32),
            jax.ShapeDtypeStruct((tiles, 1, rows), F32),
        ),
        in_specs=[pl.BlockSpec(memory_space=pltpu.VMEM)] * 2,
        out_specs=(pl.BlockSpec(memory_space=pltpu.VMEM),) * 3,
        scratch_shapes=[pltpu.VMEM((width, rows), F32), pltpu.VMEM((8, rows), F32)],
        compiler_params=pltpu.CompilerParams(vmem_limit_bytes=VMEM_LIMIT),
        cost_estimate=pl.CostEstimate(
            flops=4 * tiles * rows * width * plan[1] * 3,
            bytes_accessed=4 * queries.size * 2,
            transcendentals=0,
        ),
    )(queries, pairs)


def attend_back(queries, dout, lse, delta, pairs, plan):
    tiles, rows, width = queries.shape
    return pl.pallas_call(
        functools.partial(attend_back_kernel, plan),
        out_shape=(
            jax.ShapeDtypeStruct(queries.shape, F32),
            jax.ShapeDtypeStruct(pairs.shape, BF16),
        ),
        in_specs=[pl.BlockSpec(memory_space=pltpu.VMEM)] * 5,
        out_specs=(pl.BlockSpec(memory_space=pltpu.VMEM),) * 2,
        scratch_shapes=[pltpu.VMEM(pairs.shape, F32), pltpu.VMEM((width, rows), F32)],
        compiler_params=pltpu.CompilerParams(vmem_limit_bytes=VMEM_LIMIT),
        cost_estimate=pl.CostEstimate(
            flops=10 * tiles * rows * width * plan[1] * 3,
            bytes_accessed=4 * queries.size * 2,
            transcendentals=0,
        ),
    )(queries, dout, lse, delta, pairs)


def swapped(x, axis, k):
    return lax.ppermute(x, axis, [(i, i ^ k) for i in range(lax.axis_size(axis))])


def shards(
    tokens,
    cotangent,
    pre_attn_gain,
    w_query,
    w_key,
    w_value,
    w_out,
    post_attn_gain,
    pre_ffw_gain,
    w_gate,
    w_up,
    w_down,
    post_ffw_gain,
):
    dp_size, seq_size, mp_size = (lax.axis_size(axis) for axis in ("dp", "seq", "mp"))
    dp, seq, mp = lax.axis_index("dp"), lax.axis_index("seq"), lax.axis_index("mp")
    both = ("dp", "seq")
    heads = w_query.shape[1] // HEAD_DIM
    group = Q_HEADS // KV_HEADS
    kv_first = mp * heads // group
    q_width = heads * HEAD_DIM
    span = tokens.shape[1]
    width = tokens.shape[2]
    share = span // mp_size
    plan = attention_plan(span, seq_size)
    tile = plan[0]
    tiles = span // tile

    def gather_weight(x):
        return lax.all_gather(x, both, axis=0, tiled=True)

    w_qkv_own = jnp.concatenate(
        [
            w_query,
            lax.dynamic_slice_in_dim(w_key, kv_first * HEAD_DIM, HEAD_DIM, 1),
            lax.dynamic_slice_in_dim(w_value, kv_first * HEAD_DIM, HEAD_DIM, 1),
        ],
        axis=1,
    )
    w_qkv = gather_weight(w_qkv_own)
    w_out_t = gather_weight(after(w_out.T, w_qkv))
    gain_one, gain_two, gain_three, gain_four = gather_gains(
        [pre_attn_gain, post_attn_gain, pre_ffw_gain, post_ffw_gain], dp_size, seq_size
    )

    inputs = tokens[0].astype(F32)
    positions = seq * span + jnp.arange(span, dtype=jnp.int32)
    half_dim = HEAD_DIM // 2
    frequency = ROPE_BASE ** (-jnp.arange(half_dim, dtype=F32) * 2.0 / HEAD_DIM)
    angles = positions.astype(F32)[:, None, None] * frequency
    cosine = jnp.cos(angles)
    sine = jnp.sin(angles)
    scale_one = rms_scale(inputs)
    normed_one = (inputs * scale_one * gain_one).astype(BF16)
    key_lin = dot_nn(normed_one, w_qkv[:, q_width : q_width + HEAD_DIM])
    keys_own = rotary(key_lin, cosine[:, 0], sine[:, 0], 1.0).astype(BF16)
    values_own = dot_nn(normed_one, w_qkv[:, q_width + HEAD_DIM :]).astype(BF16)
    pairs = lax.all_gather(jnp.stack([keys_own, values_own]), "seq", axis=0)
    query_lin = dot_nn(normed_one, w_qkv[:, :q_width]).reshape(span, heads, HEAD_DIM)
    queries = (rotary(query_lin, cosine, sine, 1.0) * HEAD_DIM ** (-0.5)).astype(BF16)

    def to_tiles(x):
        x = x.reshape(tiles, tile, heads, -1)
        return jnp.transpose(x, (0, 2, 1, 3)).reshape(tiles, heads * tile, -1)

    def from_tiles(x):
        x = x.reshape(tiles, heads, tile, -1)
        return jnp.transpose(x, (0, 2, 1, 3)).reshape(span, -1)

    queries = to_tiles(queries)
    gate_w = gather_weight(after(w_gate, pairs))
    up_w = gather_weight(after(w_up, gate_w))
    down_wt = gather_weight(after(w_down.T, up_w))

    attn_tiles, attn_exact, lse = attend(queries, pairs, plan)
    attn_o = from_tiles(attn_tiles)

    def owner_rows(x, k):
        return lax.dynamic_slice_in_dim(x, (mp ^ k) * share, share, 0)

    def by_owner(x):
        return jnp.concatenate([owner_rows(x, k) for k in range(mp_size)], axis=0)

    def in_place(x):
        return jnp.concatenate(
            [lax.dynamic_slice_in_dim(x, (mp ^ k) * share, share, 0) for k in range(mp_size)], axis=0
        )

    def row_total(part_fn):
        arrived = [swapped(part_fn(k).astype(BF16), "mp", k) for k in reversed(range(1, mp_size))]
        total = part_fn(0)
        for part in arrived:
            total = total + part.astype(F32)
        return total

    def row_gather(rows):
        return jnp.concatenate(
            [rows] + [swapped(rows, "mp", k) for k in range(1, mp_size)], axis=0
        )

    def group_of(x, k):
        return x[k * share : (k + 1) * share]

    attn_o = by_owner(attn_o)
    inputs_own = owner_rows(tokens[0], 0).astype(F32)
    grad_out = owner_rows(cotangent[0], 0).astype(F32)

    attn = row_total(lambda k: dot_nt(group_of(attn_o, k), w_out_t))
    scale_two = rms_scale(attn)
    unit_two = attn * scale_two
    resid = inputs_own + unit_two * gain_two
    scale_three = rms_scale(resid)
    unit_three = resid * scale_three
    normed_two = row_gather((unit_three * gain_three).astype(BF16))

    gate_lin = dot_nn(normed_two, gate_w)
    up_lin = dot_nn(normed_two, up_w)
    gate_act, gelu_pull = jax.vjp(lambda gate_in: jax.nn.gelu(gate_in, approximate=True), gate_lin)
    hidden = (gate_act * up_lin).astype(BF16)
    mixed = row_total(lambda k: dot_nt(group_of(hidden, k), down_wt))
    scale_four = rms_scale(mixed)
    unit_four = mixed * scale_four
    output = resid + unit_four * gain_four
    dmixed, grad_gain_four = norm_back(grad_out, unit_four, scale_four, gain_four)
    dmixed_low = row_gather(dmixed.astype(BF16))

    half = width // dp_size

    def weight_grad(left, right):
        parts = []
        for k in reversed(range(dp_size)):
            columns = lax.dynamic_slice_in_dim(left, (dp ^ k) * half, half, 1)
            part = dot_tn(columns, right)
            if k:
                parts.append(swapped(part.astype(BF16), "dp", k).astype(F32))
            else:
                total = part
        for part in parts:
            total = total + part
        return total.astype(BF16)

    def spread(x):
        return lax.psum_scatter(x, "seq", scatter_dimension=0, tiled=True)

    dhidden = dot_nn(dmixed_low, down_wt)
    dgate_low = gelu_pull(dhidden * up_lin)[0].astype(BF16)
    dup_low = (dhidden * gate_act).astype(BF16)
    grad_down_t = spread(weight_grad(dmixed_low, hidden))
    dnormed_two = row_total(
        lambda k: dot_nt(group_of(dgate_low, k), gate_w) + dot_nt(group_of(dup_low, k), up_w)
    )
    dresid_norm, grad_gain_three = norm_back(dnormed_two, unit_three, scale_three, gain_three)
    dresid = grad_out + dresid_norm
    dattn, grad_gain_two = norm_back(dresid, unit_two, scale_two, gain_two)
    dattn_low = row_gather(dattn.astype(BF16))
    grad_gate = spread(weight_grad(normed_two, dgate_low))
    grad_up = spread(weight_grad(normed_two, dup_low))

    dattn_o = in_place(dot_nn(dattn_low, w_out_t)).astype(BF16)
    dattn_tiles = to_tiles(dattn_o)
    delta = jnp.sum(dattn_tiles.astype(F32) * attn_exact, axis=-1)[:, None, :]
    dquery_tiles, dpairs = attend_back(queries, dattn_tiles, lse, delta, pairs, plan)
    own_grads = lax.psum_scatter(dpairs, "seq", scatter_dimension=0, tiled=False).astype(F32)
    dquery = from_tiles(dquery_tiles).reshape(span, heads, HEAD_DIM)
    dquery_low = (
        rotary(dquery * HEAD_DIM ** (-0.5), cosine, sine, -1.0).reshape(span, q_width).astype(BF16)
    )
    dkey_low = rotary(own_grads[0], cosine[:, 0], sine[:, 0], -1.0).astype(BF16)
    dvalue_low = own_grads[1].astype(BF16)
    dqkv_low = jnp.concatenate([dquery_low, dkey_low, dvalue_low], axis=1)
    dnormed_one = row_total(lambda k: dot_nt(owner_rows(dqkv_low, k), w_qkv))
    grad_out_wt = spread(weight_grad(dattn_low, attn_o))
    grad_qkv = spread(weight_grad(normed_one, dqkv_low))

    scale_own = owner_rows(scale_one, 0)
    unit_one = inputs_own * scale_own
    dinput_norm, grad_gain_one = norm_back(dnormed_one, unit_one, scale_own, gain_one)
    tokens_grad = (dresid + dinput_norm).astype(BF16)

    kv_grad = grad_qkv[:, q_width:]
    empty = jnp.zeros((2, w_key.shape[0], w_key.shape[1]), F32)
    kv_total = empty
    for k in range(mp_size):
        piece = (swapped(kv_grad, "mp", k) if k else kv_grad).astype(F32)
        first = (mp ^ k) * heads // group * HEAD_DIM
        piece = jnp.stack([piece[:, :HEAD_DIM], piece[:, HEAD_DIM:]])
        before = lax.dynamic_slice_in_dim(kv_total, first, HEAD_DIM, 2)
        kv_total = lax.dynamic_update_slice_in_dim(kv_total, before + piece, first, 2)

    gain_grads = reduce_gains(
        [grad_gain_one, grad_gain_two, grad_gain_three, grad_gain_four], dp_size, seq_size, mp_size
    )
    return (
        output.astype(BF16)[None],
        tokens_grad[None],
        gain_grads[0],
        grad_qkv[:, :q_width].astype(F32),
        kv_total[0],
        kv_total[1],
        grad_out_wt.astype(F32).T,
        gain_grads[1],
        gain_grads[2],
        grad_gate.astype(F32),
        grad_up.astype(F32),
        grad_down_t.astype(F32).T,
        gain_grads[3],
    )


def solution(mesh):
    weight = P(("dp", "seq"), "mp")
    whole_rows = P(("dp", "seq"), None)
    columns = P("mp", ("dp", "seq"))
    gain = P(("dp", "seq"))
    tokens = P("dp", "seq", None)
    rows = P("dp", ("seq", "mp"), None)
    in_specs = (
        tokens,
        tokens,
        gain,
        weight,
        whole_rows,
        whole_rows,
        columns,
        gain,
        gain,
        weight,
        weight,
        columns,
        gain,
    )
    out_specs = (
        rows,
        rows,
        gain,
        weight,
        whole_rows,
        whole_rows,
        columns,
        gain,
        gain,
        weight,
        weight,
        columns,
        gain,
    )
    return jax.shard_map(shards, mesh=mesh, in_specs=in_specs, out_specs=out_specs, check_vma=False)
```

```python
import functools

import jax
import jax.numpy as jnp
from jax import lax
from jax.experimental import pallas as pl
from jax.experimental.pallas import tpu as pltpu
from jax.sharding import PartitionSpec as P

Q_HEADS = 8
KV_HEADS = 4
HEAD_DIM = 256
WINDOW = 4096

EPSILON = 1e-06
SOFT_CAP = 50.0
ROPE_BASE = 10000.0
MESH = pl.DeviceIdType.MESH
VMEM_LIMIT = 56 * 1024 * 1024
LANES = 128
BF16 = jnp.bfloat16
F32 = jnp.float32


def after(value, *earlier):
    return lax.optimization_barrier((value, *earlier))[0]


def dot_nn(left, right):
    return lax.dot_general(left, right, (((1,), (0,)), ((), ())), preferred_element_type=F32)


def dot_nt(left, right):
    return lax.dot_general(left, right, (((1,), (1,)), ((), ())), preferred_element_type=F32)


def dot_tn(left, right):
    return lax.dot_general(left, right, (((0,), (0,)), ((), ())), preferred_element_type=F32)


def rms_scale(vector):
    return lax.rsqrt(jnp.mean(vector * vector, axis=-1, keepdims=True) + EPSILON)


def rotary(vector, cosine, sine, direction):
    half_dim = vector.shape[-1] // 2
    first_half = vector[..., :half_dim]
    second_half = vector[..., half_dim:]
    return jnp.concatenate(
        [
            first_half * cosine - direction * (second_half * sine),
            second_half * cosine + direction * (first_half * sine),
        ],
        axis=-1,
    )


def gather_kernel(sizes, x_ref, o_ref, send_sem, recv_sem):
    dp_size, seq_size = sizes
    count = dp_size * seq_size
    dp, seq, mp = lax.axis_index("dp"), lax.axis_index("seq"), lax.axis_index("mp")
    rank = dp * seq_size + seq

    def peer(k):
        other = lax.rem(rank + k, count)
        return (other // seq_size, lax.rem(other, seq_size), mp)

    barrier = pltpu.get_barrier_semaphore()
    for k in range(1, count):
        pl.semaphore_signal(barrier, inc=1, device_id=peer(k), device_id_type=MESH)
    pl.semaphore_wait(barrier, count - 1)
    copies = []
    for k in range(1, count):
        copies.append(
            pltpu.make_async_remote_copy(
                src_ref=x_ref,
                dst_ref=o_ref.at[rank],
                send_sem=send_sem.at[k],
                recv_sem=recv_sem.at[k],
                device_id=peer(k),
                device_id_type=MESH,
            )
        )
        copies[-1].start()
    o_ref[pl.ds(rank, 1)] = x_ref[...][None]
    for copy in copies:
        copy.wait()


def gather_gains(gains, dp_size, seq_size):
    count = dp_size * seq_size
    local = gains[0].shape[0]
    width = -(-local // LANES) * LANES
    block = jnp.stack([gain.astype(F32) for gain in gains])
    block = jnp.pad(block, ((0, 8 - len(gains)), (0, width - local)))
    full = pl.pallas_call(
        functools.partial(gather_kernel, (dp_size, seq_size)),
        out_shape=jax.ShapeDtypeStruct((count, 8, width), F32),
        in_specs=[pl.BlockSpec(memory_space=pltpu.VMEM)],
        out_specs=pl.BlockSpec(memory_space=pltpu.VMEM),
        scratch_shapes=[
            pltpu.SemaphoreType.DMA((count,)),
            pltpu.SemaphoreType.DMA((count,)),
        ],
        compiler_params=pltpu.CompilerParams(collective_id=1, has_side_effects=True),
    )(block)
    full = jnp.transpose(full[:, : len(gains), :local], (1, 0, 2)).reshape(len(gains), -1)
    return [full[i : i + 1] for i in range(len(gains))]


def flipped(index, k):
    result, bit = index, 1
    while bit <= k:
        if k & bit:
            result = result + bit * (1 - 2 * lax.rem(index // bit, 2))
        bit *= 2
    return result


def last_kernel(sizes, heads, x_ref, kv_ref, o_ref, key_ref, value_ref, mine, from_mp, from_ws, kv_from, sems):
    dp_size, seq_size, mp_size = sizes
    count = dp_size * seq_size
    dp, seq, mp = lax.axis_index("dp"), lax.axis_index("seq"), lax.axis_index("mp")
    rank = dp * seq_size + seq

    def mp_peer(k):
        return (dp, seq, flipped(mp, k))

    def ws_rank(k):
        return lax.rem(rank + k, count)

    def ws_peer(k):
        other = ws_rank(k)
        return (other // seq_size, lax.rem(other, seq_size), mp)

    def remote(src, dst, kind, k, device):
        copy = pltpu.make_async_remote_copy(
            src_ref=src,
            dst_ref=dst,
            send_sem=sems.at[kind, 0, k],
            recv_sem=sems.at[kind, 1, k],
            device_id=device,
            device_id_type=MESH,
        )
        copy.start()
        return copy

    barrier = pltpu.get_barrier_semaphore()
    for k in range(1, mp_size):
        pl.semaphore_signal(barrier, inc=1, device_id=mp_peer(k), device_id_type=MESH)
    for k in range(1, count):
        pl.semaphore_signal(barrier, inc=1, device_id=ws_peer(k), device_id_type=MESH)
    pl.semaphore_wait(barrier, mp_size - 1 + count - 1)
    copies = [remote(x_ref, from_mp.at[k], 0, k, mp_peer(k)) for k in range(1, mp_size)]
    kv_copies = [remote(kv_ref, kv_from.at[k], 1, k, mp_peer(k)) for k in range(1, mp_size)]
    for copy in copies:
        copy.wait()
    total = x_ref[...]
    for k in range(1, mp_size):
        total = total + from_mp[k]
    mine[...] = total
    copies = [remote(mine.at[ws_rank(k)], from_ws.at[k], 2, k, ws_peer(k)) for k in range(1, count)]
    key_ref[...] = jnp.zeros_like(key_ref)
    value_ref[...] = jnp.zeros_like(value_ref)
    for k in range(mp_size):
        if k:
            kv_copies[k - 1].wait()
        piece = (kv_from[k] if k else kv_ref[...]).astype(F32)
        head = flipped(mp, k) * heads // (Q_HEADS // KV_HEADS)
        columns = pl.ds(pl.multiple_of(head * HEAD_DIM, HEAD_DIM), HEAD_DIM)
        key_ref[:, columns] += piece[:, :HEAD_DIM]
        value_ref[:, columns] += piece[:, HEAD_DIM:]
    for copy in copies:
        copy.wait()
    own = mine[pl.ds(rank, 1)][0]
    for k in range(1, count):
        own = own + from_ws[k]
    o_ref[...] = own


def last_sums(grads, kv, kv_width, heads, sizes):
    dp_size, seq_size, mp_size = sizes
    count = dp_size * seq_size
    local = grads[0].shape[0] // count
    width = -(-local // LANES) * LANES
    block = jnp.transpose(jnp.stack(grads).reshape(len(grads), count, local), (1, 0, 2))
    block = jnp.pad(block, ((0, 0), (0, 8 - len(grads)), (0, width - local)))
    kv_out = jax.ShapeDtypeStruct((kv.shape[0], kv_width), F32)
    total, key, value = pl.pallas_call(
        functools.partial(last_kernel, sizes, heads),
        out_shape=(jax.ShapeDtypeStruct((8, width), F32), kv_out, kv_out),
        in_specs=[pl.BlockSpec(memory_space=pltpu.VMEM)] * 2,
        out_specs=(pl.BlockSpec(memory_space=pltpu.VMEM),) * 3,
        scratch_shapes=[
            pltpu.VMEM((count, 8, width), F32),
            pltpu.VMEM((mp_size, count, 8, width), F32),
            pltpu.VMEM((count, 8, width), F32),
            pltpu.VMEM((mp_size, *kv.shape), BF16),
            pltpu.SemaphoreType.DMA((3, 2, max(count, mp_size))),
        ],
        compiler_params=pltpu.CompilerParams(
            collective_id=2, has_side_effects=True, vmem_limit_bytes=VMEM_LIMIT
        ),
    )(block, kv)
    return [total[i, :local] for i in range(len(grads))], key, value


def key_mask(shape, first_key, first_query, tile, far):
    key = first_key + lax.broadcasted_iota(jnp.int32, shape, 0)
    query = first_query + lax.rem(lax.broadcasted_iota(jnp.int32, shape, 1), tile)
    return key > query if far else key <= query


def for_key_tiles(tile_fn, index, tile, span, step, hops, windowed):
    seq = lax.axis_index("seq")
    per_block = span // step
    last = jnp.minimum(seq, hops)
    if windowed:
        @pl.when(seq >= hops)
        def _():
            tile_fn(pl.multiple_of((seq - hops) * span, span), span, "far")

        last = jnp.minimum(seq, hops - 1)

    def past(t, carry):
        tile_fn(pl.multiple_of(t * step, step), step, "")
        return carry

    lax.fori_loop((seq - last) * per_block, seq * per_block, past, 0)
    tile_fn(pl.multiple_of(seq * span, span), (index + 1) * tile, "near")


def head_rows(ref, index, tile):
    block = ref[pl.ds(index * tile, tile), :]
    return jnp.concatenate(
        [block[:, h * HEAD_DIM : (h + 1) * HEAD_DIM] for h in range(ref.shape[1] // HEAD_DIM)], axis=0
    )


def put_head_rows(ref, index, tile, rows):
    for h in range(ref.shape[1] // HEAD_DIM):
        ref[pl.ds(index * tile, tile), h * HEAD_DIM : (h + 1) * HEAD_DIM] = rows[
            h * tile : (h + 1) * tile
        ].astype(ref.dtype)


def attend_kernel(plan, q_ref, kv_ref, o_ref, of_ref, lse_ref, acc, total):
    tile, span, step, hops, windowed = plan
    for i in range(span // tile):
        query = head_rows(q_ref, i, tile)
        rows = query.shape[0]
        acc[...] = jnp.zeros_like(acc)
        total[...] = jnp.zeros_like(total)

        def tile_fn(first, count, mask, i=i, query=query, rows=rows):
            key = kv_ref[pl.ds(first, count), :HEAD_DIM]
            value = kv_ref[pl.ds(first, count), HEAD_DIM:]
            raw = dot_nt(key, query)
            weight = jnp.exp(SOFT_CAP * jnp.tanh(raw * (1.0 / SOFT_CAP)))
            if mask:
                inside = key_mask(weight.shape, 0, i * tile, tile, mask == "far")
                weight = jnp.where(inside, weight, 0.0)
            total[...] += jnp.sum(weight.reshape(count // 8, 8, rows), axis=0)
            acc[...] += dot_tn(value, weight.astype(BF16))

        for_key_tiles(tile_fn, i, tile, span, step, hops, windowed)
        row_total = jnp.sum(total[...], axis=0, keepdims=True)
        out = (acc[...] / row_total).T
        put_head_rows(o_ref, i, tile, out)
        put_head_rows(of_ref, i, tile, out)
        lse_ref[i] = jnp.log(row_total)


def attend_back_kernel(plan, q_ref, do_ref, of_ref, lse_ref, kv_ref, dq_ref, dkv_ref, grads, acc):
    tile, span, step, hops, windowed = plan
    grads[...] = jnp.zeros_like(grads)
    for i in range(span // tile):
        query = head_rows(q_ref, i, tile)
        dout = head_rows(do_ref, i, tile)
        lse = lse_ref[i]
        delta = jnp.sum(dout.astype(F32) * head_rows(of_ref, i, tile), axis=-1, keepdims=True)
        delta = jnp.broadcast_to(delta, (delta.shape[0], LANES)).T[:1]
        acc[...] = jnp.zeros_like(acc)

        def tile_fn(first, count, mask, i=i, query=query, dout=dout, lse=lse, delta=delta):
            key = kv_ref[pl.ds(first, count), :HEAD_DIM]
            value = kv_ref[pl.ds(first, count), HEAD_DIM:]
            bounded = jnp.tanh(dot_nt(key, query) * (1.0 / SOFT_CAP))
            prob = jnp.exp(SOFT_CAP * bounded - lse)
            if mask:
                inside = key_mask(prob.shape, 0, i * tile, tile, mask == "far")
                prob = jnp.where(inside, prob, 0.0)
            dprob = dot_nt(value, dout)
            draw = (prob * (dprob - delta) * (1.0 - bounded * bounded)).astype(BF16)
            grads[pl.ds(first, count), HEAD_DIM:] += dot_nn(prob.astype(BF16), dout)
            grads[pl.ds(first, count), :HEAD_DIM] += dot_nn(draw, query)
            acc[...] += dot_tn(key, draw)

        for_key_tiles(tile_fn, i, tile, span, step, hops, windowed)
        put_head_rows(dq_ref, i, tile, acc[...].T)
    dkv_ref[...] = grads[...].astype(BF16)


def attention_plan(span, seq_size):
    hops = min(WINDOW // span, seq_size - 1)
    return (min(256, span), span, min(512, span), hops, seq_size * span > WINDOW)


def attend(queries, pairs, plan):
    tile, span = plan[:2]
    heads = queries.shape[1] // HEAD_DIM
    rows = heads * tile
    return pl.pallas_call(
        functools.partial(attend_kernel, plan),
        out_shape=(
            jax.ShapeDtypeStruct(queries.shape, BF16),
            jax.ShapeDtypeStruct(queries.shape, F32),
            jax.ShapeDtypeStruct((span // tile, 1, rows), F32),
        ),
        in_specs=[pl.BlockSpec(memory_space=pltpu.VMEM)] * 2,
        out_specs=(pl.BlockSpec(memory_space=pltpu.VMEM),) * 3,
        scratch_shapes=[pltpu.VMEM((HEAD_DIM, rows), F32), pltpu.VMEM((8, rows), F32)],
        compiler_params=pltpu.CompilerParams(vmem_limit_bytes=VMEM_LIMIT),
        cost_estimate=pl.CostEstimate(
            flops=12 * queries.size * span, bytes_accessed=8 * queries.size, transcendentals=0
        ),
    )(queries, pairs)


def attend_back(queries, dout, exact, lse, pairs, plan):
    tile, span = plan[:2]
    rows = queries.shape[1] // HEAD_DIM * tile
    return pl.pallas_call(
        functools.partial(attend_back_kernel, plan),
        out_shape=(
            jax.ShapeDtypeStruct(queries.shape, F32),
            jax.ShapeDtypeStruct(pairs.shape, BF16),
        ),
        in_specs=[pl.BlockSpec(memory_space=pltpu.VMEM)] * 5,
        out_specs=(pl.BlockSpec(memory_space=pltpu.VMEM),) * 2,
        scratch_shapes=[pltpu.VMEM(pairs.shape, F32), pltpu.VMEM((HEAD_DIM, rows), F32)],
        compiler_params=pltpu.CompilerParams(vmem_limit_bytes=VMEM_LIMIT),
        cost_estimate=pl.CostEstimate(
            flops=30 * queries.size * span, bytes_accessed=8 * queries.size, transcendentals=0
        ),
    )(queries, dout, exact, lse, pairs)


def remote_copy(src, dst, sems, index, device):
    copy = pltpu.make_async_remote_copy(
        src_ref=src,
        dst_ref=dst,
        send_sem=sems.at[(0, *index)],
        recv_sem=sems.at[(1, *index)],
        device_id=device,
        device_id_type=MESH,
    )
    copy.start()
    return copy


def sum_direct(parts_at, steps, step, mp_size, peer, total, sent, arrived, sems):
    copies = []
    for t in range(steps):
        for k in range(mp_size - 1, -1, -1):
            part = parts_at(t, k)
            if k == 0:
                total[:, t * step : (t + 1) * step] = part
            else:
                sent[t, k - 1] = part.astype(BF16)
                copies.append(
                    remote_copy(sent.at[t, k - 1], arrived.at[t, k - 1], sems, (t, k - 1), peer(k))
                )
    for t in range(steps):
        for k in range(1, mp_size):
            copies[t * (mp_size - 1) + mp_size - 1 - k].wait_recv()
            total[:, t * step : (t + 1) * step] += arrived[t, k - 1].astype(F32)
    return copies


def sum_square(parts_at, steps, step, peer, total, kept, sent, arrived, sems):
    half = step // 2
    copies, second = [], []
    for t in range(steps):
        first = t * step
        far = parts_at(t, 3)
        sent[t, 0, 1] = far[:, :half].astype(BF16)
        sent[t, 1, 1] = far[:, half:].astype(BF16)
        part = parts_at(t, 1)
        sent[t, 0, 0] = part[:, :half].astype(BF16)
        kept[t, 0] = part[:, half:]
        copies.append(
            remote_copy(sent.at[t, 0, pl.ds(0, 2)], arrived.at[t, 0, pl.ds(0, 2)], sems, (t, 0), peer(1))
        )
        part = parts_at(t, 2)
        sent[t, 1, 0] = part[:, half:].astype(BF16)
        kept[t, 1] = part[:, :half]
        copies.append(
            remote_copy(sent.at[t, 1, pl.ds(0, 2)], arrived.at[t, 1, pl.ds(0, 2)], sems, (t, 1), peer(2))
        )
        total[:, first : first + step] = parts_at(t, 0)
    for t in range(steps):
        copies[2 * t].wait_recv()
        sent[t, 1, 2] = (kept[t, 1] + arrived[t, 0, 1].astype(F32)).astype(BF16)
        second.append(remote_copy(sent.at[t, 1, 2], arrived.at[t, 1, 2], sems, (t, 2), peer(2)))
        copies[2 * t + 1].wait_recv()
        sent[t, 0, 2] = (kept[t, 0] + arrived[t, 1, 1].astype(F32)).astype(BF16)
        second.append(remote_copy(sent.at[t, 0, 2], arrived.at[t, 0, 2], sems, (t, 3), peer(1)))
    for t in range(steps):
        first = t * step
        second[2 * t].wait_recv()
        total[:, first : first + half] += arrived[t, 0, 0].astype(F32) + arrived[t, 1, 2].astype(F32)
        second[2 * t + 1].wait_recv()
        total[:, first + half : first + step] += arrived[t, 1, 0].astype(F32) + arrived[t, 0, 2].astype(
            F32
        )
    return copies + second


def gather_direct(own, gathered, share, mp_size, peer, sems):
    copies = [
        remote_copy(own, gathered.at[pl.ds(k * share, share)], sems, (k,), peer(k))
        for k in range(mp_size - 1, 0, -1)
    ]
    for copy in copies:
        copy.wait()


def gather_square(own, gathered, share, peer, sems):
    half = share // 2

    def place(k, lower):
        return gathered.at[pl.ds(k * share + lower * half, half)]

    upper, lower = own.at[pl.ds(0, half)], own.at[pl.ds(half, half)]
    to_one = remote_copy(upper, place(1, 0), sems, (0,), peer(1))
    to_two = remote_copy(lower, place(2, 1), sems, (1,), peer(2))
    copies = [
        remote_copy(upper, place(2, 0), sems, (2,), peer(2)),
        remote_copy(lower, place(1, 1), sems, (3,), peer(1)),
    ]
    to_one.wait_recv()
    copies.append(remote_copy(place(1, 0), place(3, 0), sems, (4,), peer(2)))
    to_two.wait_recv()
    copies.append(remote_copy(place(2, 1), place(3, 1), sems, (5,), peer(1)))
    to_one.wait_send()
    to_two.wait_send()
    for copy in copies:
        copy.wait()


def rows_kernel(plan, rows_fn, *refs):
    mp_size, share, step, row_step, natural, n_left, n_aux, n_out, gather = plan
    lefts, weight_ref, refs = refs[:n_left], refs[n_left], refs[n_left + 1 :]
    aux, refs = refs[:n_aux], refs[n_aux:]
    outs, refs = refs[:n_out], refs[n_out:]
    if gather:
        gathered, refs = refs[0], refs[1:]
    left, weight, kept, sent, arrived, total, own, in_sem, sum_sem, row_sem = refs
    steps = total.shape[1] // step
    dp, seq, mp = lax.axis_index("dp"), lax.axis_index("seq"), lax.axis_index("mp")

    def peer(k):
        return (dp, seq, flipped(mp, k))

    left_copies, weight_copies = {}, []
    for k in range(mp_size):
        first = (flipped(mp, k) if natural else k) * share
        left_copies[k] = []
        column = 0
        for i, ref in enumerate(lefts):
            depth = ref.shape[1]
            left_copies[k].append(
                pltpu.make_async_copy(
                    ref.at[pl.ds(first, share)],
                    left.at[k, :, pl.ds(column, depth)],
                    in_sem.at[2 + k * n_left + i],
                )
            )
            column += depth
    for t in range(steps):
        weight_copies.append(
            pltpu.make_async_copy(
                weight_ref.at[pl.ds(t * step, step)], weight.at[t % 2], in_sem.at[t % 2]
            )
        )
    weight_copies[0].start()
    for k in range(mp_size - 1, -1, -1):
        for copy in left_copies[k]:
            copy.start()

    barrier = pltpu.get_barrier_semaphore()
    for k in range(1, mp_size):
        pl.semaphore_signal(barrier, inc=1, device_id=peer(k), device_id_type=MESH)
    pl.semaphore_wait(barrier, mp_size - 1)

    def parts_at(t, k):
        if k == mp_size - 1:
            weight_copies[t].wait()
            if t + 1 < steps:
                weight_copies[t + 1].start()
        if t == 0:
            for copy in left_copies[k]:
                copy.wait()
        return dot_nt(left[k], weight[t % 2])

    if mp_size == 4:
        sums = sum_square(parts_at, steps, step, peer, total, kept, sent, arrived, sum_sem)
    else:
        sums = sum_direct(parts_at, steps, step, mp_size, peer, total, sent, arrived, sum_sem)

    def rows_at(r, carry):
        rows = pl.ds(pl.multiple_of(r * row_step, row_step), row_step)
        result = rows_fn(total[rows, :], rows, aux, outs)
        if gather:
            own[rows, :] = result.astype(BF16)
        return carry

    for ref in outs:
        if ref.shape[0] == 8:
            ref[...] = jnp.zeros_like(ref)
    lax.fori_loop(0, share // row_step, rows_at, 0)
    if gather:
        keep = pltpu.make_async_copy(own, gathered.at[pl.ds(0, share)], in_sem.at[0])
        keep.start()
        if mp_size == 4:
            gather_square(own, gathered, share, peer, row_sem)
        else:
            gather_direct(own, gathered, share, mp_size, peer, row_sem)
        keep.wait()
    for copy in sums:
        copy.wait_send()


def sum_rows(lefts, weight, rows_fn, aux, outs, gather, natural, mp_size, collective_id):
    span = lefts[0].shape[0]
    width, depth = weight.shape
    share = span // mp_size
    step = 768 if width % 768 == 0 else width
    row_step = min(32, share)
    steps = width // step
    plan = (mp_size, share, step, row_step, natural, len(lefts), len(aux), len(outs), gather)
    out_shape = [jax.ShapeDtypeStruct((rows, width), dtype) for rows, dtype in outs]
    out_specs = [pl.BlockSpec(memory_space=pltpu.VMEM)] * len(outs)
    if gather:
        out_shape.append(jax.ShapeDtypeStruct((span, width), BF16))
        out_specs.append(pl.BlockSpec(memory_space=pl.ANY))
    if mp_size == 4:
        pieces, kept = (steps, 2, 3, share, step // 2), (steps, 2, share, step // 2)
    else:
        pieces, kept = (steps, mp_size - 1, share, step), (8, LANES)
    return pl.pallas_call(
        functools.partial(rows_kernel, plan, rows_fn),
        out_shape=out_shape,
        in_specs=[pl.BlockSpec(memory_space=pl.ANY)] * (len(lefts) + 1)
        + [pl.BlockSpec(memory_space=pltpu.VMEM)] * len(aux),
        out_specs=out_specs,
        scratch_shapes=[
            pltpu.VMEM((mp_size, share, depth), BF16),
            pltpu.VMEM((2, step, depth), BF16),
            pltpu.VMEM(kept, F32),
            pltpu.VMEM(pieces, BF16),
            pltpu.VMEM(pieces, BF16),
            pltpu.VMEM((share, width), F32),
            pltpu.VMEM((share, width), BF16),
            pltpu.SemaphoreType.DMA((2 + mp_size * len(lefts),)),
            pltpu.SemaphoreType.DMA((2, steps, max(4, mp_size - 1))),
            pltpu.SemaphoreType.DMA((2, max(6, mp_size))),
        ],
        compiler_params=pltpu.CompilerParams(
            collective_id=collective_id, has_side_effects=True, vmem_limit_bytes=VMEM_LIMIT
        ),
    )(*lefts, weight, *aux)


def weight_grad_kernel(plan, *refs):
    n_right, tile, half = plan
    left_ref, rights, out_ref = refs[0], refs[1 : 1 + n_right], refs[1 + n_right]
    left, right, sent, arrived, own, result, in_sem, swap_sem, out_sem = refs[2 + n_right :]
    dp, seq, mp = lax.axis_index("dp"), lax.axis_index("seq"), lax.axis_index("mp")
    other = (1 - dp, seq, mp)
    lefts = []
    for i, side in enumerate((1 - dp, dp)):
        columns = pl.ds(pl.multiple_of(side * half, LANES), half)
        lefts.append(pltpu.make_async_copy(left_ref.at[:, columns], left.at[i], in_sem.at[2 + i]))
        lefts[i].start()
    sources = []
    for ref in rights:
        for first in range(0, ref.shape[1], tile):
            sources.append(ref.at[:, pl.ds(first, tile)])
    tiles = len(sources)
    loads = [
        pltpu.make_async_copy(source, right.at[t % 2], in_sem.at[t % 2])
        for t, source in enumerate(sources)
    ]
    loads[0].start()
    barrier = pltpu.get_barrier_semaphore()
    pl.semaphore_signal(barrier, inc=1, device_id=other, device_id_type=MESH)
    pl.semaphore_wait(barrier, 1)
    swaps, stores = [], []

    def finish(t):
        swaps[t].wait_recv()
        if t >= 2:
            stores[t - 2].wait()
        result[t % 2] = (own[t % 2] + arrived[t].astype(F32)).astype(BF16)
        stores.append(
            pltpu.make_async_copy(
                result.at[t % 2], out_ref.at[:, pl.ds(t * tile, tile)], out_sem.at[t % 2]
            )
        )
        stores[t].start()

    for t in range(tiles):
        loads[t].wait()
        if t + 1 < tiles:
            loads[t + 1].start()
        if t == 0:
            lefts[0].wait()
        sent[t] = dot_tn(left[0], right[t % 2]).astype(BF16)
        swaps.append(remote_copy(sent.at[t], arrived.at[t], swap_sem, (t,), other))
        if t == 0:
            lefts[1].wait()
        own[t % 2] = dot_tn(left[1], right[t % 2])
        if t >= 1:
            finish(t - 1)
    finish(tiles - 1)
    for store in stores[-2:]:
        store.wait()
    for swap in swaps:
        swap.wait_send()


def weight_grad(left, rights, collective_id):
    rows, width = left.shape
    half = width // 2
    total = sum(right.shape[1] for right in rights)
    tile = min(768 if rights[0].shape[1] % 768 == 0 else 384, rights[0].shape[1])
    tile = next(t for t in (tile, 256, LANES) if all(right.shape[1] % t == 0 for right in rights))
    tiles = total // tile
    return pl.pallas_call(
        functools.partial(weight_grad_kernel, (len(rights), tile, half)),
        out_shape=jax.ShapeDtypeStruct((half, total), BF16),
        in_specs=[pl.BlockSpec(memory_space=pl.ANY)] * (1 + len(rights)),
        out_specs=pl.BlockSpec(memory_space=pl.ANY),
        scratch_shapes=[
            pltpu.VMEM((2, rows, half), BF16),
            pltpu.VMEM((2, rows, tile), BF16),
            pltpu.VMEM((tiles, half, tile), BF16),
            pltpu.VMEM((tiles, half, tile), BF16),
            pltpu.VMEM((2, half, tile), F32),
            pltpu.VMEM((2, half, tile), BF16),
            pltpu.SemaphoreType.DMA((4,)),
            pltpu.SemaphoreType.DMA((2, tiles)),
            pltpu.SemaphoreType.DMA((2,)),
        ],
        compiler_params=pltpu.CompilerParams(
            collective_id=collective_id, has_side_effects=True, vmem_limit_bytes=VMEM_LIMIT
        ),
    )(left, *rights)


def hidden_back_kernel(dmixed_ref, down_ref, act_ref, slope_ref, dgate_ref, dup_ref):
    dhidden = dot_nn(dmixed_ref[...], down_ref[...])
    dgate_ref[...] = (dhidden * slope_ref[...].astype(F32)).astype(BF16)
    dup_ref[...] = (dhidden * act_ref[...].astype(F32)).astype(BF16)


def hidden_back(dmixed, down_wt, act, slope):
    rows, width = dmixed.shape
    units = down_wt.shape[1]
    tile = 256 if units % 256 == 0 else units
    columns = pl.BlockSpec((rows, tile), lambda i: (0, i))
    return pl.pallas_call(
        hidden_back_kernel,
        grid=(units // tile,),
        out_shape=(jax.ShapeDtypeStruct((rows, units), BF16),) * 2,
        in_specs=[
            pl.BlockSpec((rows, width), lambda i: (0, 0)),
            pl.BlockSpec((width, tile), lambda i: (0, i)),
            columns,
            columns,
        ],
        out_specs=(columns, columns),
        compiler_params=pltpu.CompilerParams(vmem_limit_bytes=VMEM_LIMIT),
    )(dmixed, down_wt, act, slope)


def fold_rows(x):
    return jnp.sum(x.reshape(x.shape[0] // 8, 8, x.shape[1]), axis=0)


def after_attention(attn, rows, aux, outs):
    tokens, gain_two, gain_three = aux
    attn_out, resid_out = outs
    resid = tokens[rows, :].astype(F32) + attn * rms_scale(attn) * gain_two[...]
    attn_out[rows, :] = attn
    resid_out[rows, :] = resid
    return resid * rms_scale(resid) * gain_three[...]


def after_ffw(mixed, rows, aux, outs):
    resid, cotangent, gain_four = aux
    output, gain_grad = outs
    scale = rms_scale(mixed)
    unit = mixed * scale
    grad_out = cotangent[rows, :].astype(F32)
    output[rows, :] = (resid[rows, :] + unit * gain_four[...]).astype(BF16)
    gain_grad[...] += fold_rows(grad_out * unit)
    return vector_back(grad_out, unit, scale, gain_four[...])


def vector_back(grad_in, unit, scale, gain):
    unit_grad = grad_in * gain
    return scale * (unit_grad - unit * jnp.mean(unit_grad * unit, axis=-1, keepdims=True))


def before_ffw(dnormed_two, rows, aux, outs):
    resid, attn, cotangent, gain_two, gain_three = aux
    dresid_out, gain_two_grad, gain_three_grad = outs
    scale = rms_scale(resid[rows, :])
    unit = resid[rows, :] * scale
    gain_three_grad[...] += fold_rows(dnormed_two * unit)
    dresid = cotangent[rows, :].astype(F32) + vector_back(dnormed_two, unit, scale, gain_three[...])
    dresid_out[rows, :] = dresid
    scale = rms_scale(attn[rows, :])
    unit = attn[rows, :] * scale
    gain_two_grad[...] += fold_rows(dresid * unit)
    return vector_back(dresid, unit, scale, gain_two[...])


def before_attention(dnormed_one, rows, aux, outs):
    tokens, dresid, gain_one = aux
    tokens_grad, gain_grad = outs
    vector = tokens[rows, :].astype(F32)
    scale = rms_scale(vector)
    unit = vector * scale
    gain_grad[...] += fold_rows(dnormed_one * unit)
    back = vector_back(dnormed_one, unit, scale, gain_one[...])
    tokens_grad[rows, :] = (dresid[rows, :] + back).astype(BF16)


def swapped(x, axis, k):
    return lax.ppermute(x, axis, [(i, i ^ k) for i in range(lax.axis_size(axis))])


def shards(
    tokens,
    cotangent,
    pre_attn_gain,
    w_query,
    w_key,
    w_value,
    w_out,
    post_attn_gain,
    pre_ffw_gain,
    w_gate,
    w_up,
    w_down,
    post_ffw_gain,
):
    dp_size, seq_size, mp_size = (lax.axis_size(axis) for axis in ("dp", "seq", "mp"))
    dp, seq, mp = lax.axis_index("dp"), lax.axis_index("seq"), lax.axis_index("mp")
    both = ("dp", "seq")
    heads = w_query.shape[1] // HEAD_DIM
    group = Q_HEADS // KV_HEADS
    kv_first = mp * heads // group
    q_width = heads * HEAD_DIM
    span = tokens.shape[1]
    width = tokens.shape[2]
    share = span // mp_size
    plan = attention_plan(span, seq_size)

    def gather_weight(x):
        return lax.all_gather(x, both, axis=0, tiled=True)

    w_qkv_own = jnp.concatenate(
        [
            w_query,
            lax.dynamic_slice_in_dim(w_key, kv_first * HEAD_DIM, HEAD_DIM, 1),
            lax.dynamic_slice_in_dim(w_value, kv_first * HEAD_DIM, HEAD_DIM, 1),
        ],
        axis=1,
    )
    w_qkv = gather_weight(w_qkv_own)
    gain_one, gain_two, gain_three, gain_four = gather_gains(
        [pre_attn_gain, post_attn_gain, pre_ffw_gain, post_ffw_gain], dp_size, seq_size
    )

    inputs = tokens[0].astype(F32)
    positions = seq * span + jnp.arange(span, dtype=jnp.int32)
    half_dim = HEAD_DIM // 2
    frequency = ROPE_BASE ** (-jnp.arange(half_dim, dtype=F32) * 2.0 / HEAD_DIM)
    angles = positions.astype(F32)[:, None, None] * frequency
    cosine = jnp.cos(angles)
    sine = jnp.sin(angles)
    scale_one = rms_scale(inputs)
    normed_one = (inputs * scale_one * gain_one).astype(BF16)
    w_out_t = gather_weight(after(w_out.T, w_qkv, normed_one))
    key_lin = dot_nn(normed_one, w_qkv[:, q_width : q_width + HEAD_DIM])
    keys_own = rotary(key_lin, cosine[:, 0], sine[:, 0], 1.0).astype(BF16)
    values_own = dot_nn(normed_one, w_qkv[:, q_width + HEAD_DIM :]).astype(BF16)
    own_pair = jnp.concatenate([keys_own, values_own], axis=1)
    pairs = lax.all_gather(after(own_pair, w_out_t), "seq", axis=0, tiled=True)
    query_lin = dot_nn(normed_one, w_qkv[:, :q_width]).reshape(span, heads, HEAD_DIM)
    queries = (rotary(query_lin, cosine, sine, 1.0) * HEAD_DIM ** (-0.5)).astype(BF16)
    queries = queries.reshape(span, q_width)

    ffw = w_gate.shape[1]
    gate_up_w = gather_weight(after(jnp.concatenate([w_gate, w_up], axis=1), pairs))
    gate_w, up_w = gate_up_w[:, :ffw], gate_up_w[:, ffw:]

    attn_o, attn_exact, lse = attend(queries, pairs, plan)
    own_first = mp * share
    tokens_own = lax.dynamic_slice_in_dim(tokens[0], own_first, share, 0)
    cotangent_own = lax.dynamic_slice_in_dim(cotangent[0], own_first, share, 0)

    def by_owner(x):
        return jnp.concatenate(
            [lax.dynamic_slice_in_dim(x, (mp ^ k) * share, share, 0) for k in range(mp_size)], axis=0
        )

    attn, resid, normed_two = sum_rows(
        (attn_o,),
        w_out_t,
        after_attention,
        (tokens_own, gain_two, gain_three),
        ((share, F32), (share, F32)),
        True,
        True,
        mp_size,
        3,
    )
    down_wt = gather_weight(after(w_down.T, gate_up_w, normed_two))

    gate_lin = dot_nn(normed_two, gate_w)
    up_lin = dot_nn(normed_two, up_w)
    gate_act, gelu_pull = jax.vjp(lambda gate_in: jax.nn.gelu(gate_in, approximate=True), gate_lin)
    hidden = (gate_act * up_lin).astype(BF16)
    slope = gelu_pull(up_lin)[0].astype(BF16)
    gate_act = gate_act.astype(BF16)
    output, grad_gain_four, dmixed_low = sum_rows(
        (hidden,),
        down_wt,
        after_ffw,
        (resid, cotangent_own, gain_four),
        ((share, BF16), (8, F32)),
        True,
        False,
        mp_size,
        4,
    )

    def spread(x):
        return lax.psum_scatter(x, "seq", scatter_dimension=0, tiled=True)

    grad_down_sum = weight_grad(dmixed_low, (hidden,), 7)
    grad_down_t = spread(grad_down_sum)
    dgate_low, dup_low = hidden_back(after(dmixed_low, grad_down_sum), down_wt, gate_act, slope)
    grad_gate_up_sum = weight_grad(normed_two, (dgate_low, dup_low), 8)
    dresid, grad_gain_two, grad_gain_three, dattn_low = sum_rows(
        (after(dgate_low, grad_down_t, grad_gate_up_sum), dup_low),
        gate_up_w,
        before_ffw,
        (resid, attn, cotangent_own, gain_two, gain_three),
        ((share, F32), (8, F32), (8, F32)),
        True,
        False,
        mp_size,
        5,
    )
    grad_gate_up = spread(after(grad_gate_up_sum, grad_down_t))

    dattn_o = by_owner(dot_nn(dattn_low, w_out_t)).astype(BF16)
    dquery, dpairs = attend_back(queries, dattn_o, attn_exact, lse, pairs, plan)
    own_grads = spread(after(dpairs, grad_gate_up)).astype(F32)
    dkey_rot = own_grads[:, :HEAD_DIM]
    dkey_low = rotary(dkey_rot, cosine[:, 0], sine[:, 0], -1.0).astype(BF16)
    dvalue_low = own_grads[:, HEAD_DIM:].astype(BF16)
    dquery = dquery.reshape(span, heads, HEAD_DIM)
    dquery_low = (
        rotary(dquery * HEAD_DIM ** (-0.5), cosine, sine, -1.0).reshape(span, q_width).astype(BF16)
    )
    dkv_low = jnp.concatenate([dkey_low, dvalue_low], axis=1)
    grad_out_t = spread(after(weight_grad(dattn_low, (by_owner(attn_o),), 9), own_grads))
    grad_qkv = spread(after(weight_grad(normed_one, (dquery_low, dkv_low), 10), grad_out_t))
    tokens_grad, grad_gain_one = sum_rows(
        (dquery_low, after(dkv_low, grad_out_t)),
        w_qkv,
        before_attention,
        (tokens_own, dresid, gain_one),
        ((share, BF16), (8, F32)),
        False,
        True,
        mp_size,
        6,
    )

    gain_grads, grad_key, grad_value = last_sums(
        [
            jnp.sum(grad, axis=0)
            for grad in (grad_gain_one, grad_gain_two, grad_gain_three, grad_gain_four)
        ],
        grad_qkv[:, q_width:],
        w_key.shape[1],
        heads,
        (dp_size, seq_size, mp_size),
    )
    return (
        output[None],
        tokens_grad[None],
        gain_grads[0],
        grad_qkv[:, :q_width].astype(F32),
        grad_key,
        grad_value,
        grad_out_t.astype(F32).T,
        gain_grads[1],
        gain_grads[2],
        grad_gate_up[:, :ffw].astype(F32),
        grad_gate_up[:, ffw:].astype(F32),
        grad_down_t.astype(F32).T,
        gain_grads[3],
    )


def solution(mesh):
    weight = P(("dp", "seq"), "mp")
    whole_rows = P(("dp", "seq"), None)
    columns = P("mp", ("dp", "seq"))
    gain = P(("dp", "seq"))
    tokens = P("dp", "seq", None)
    rows = P("dp", ("seq", "mp"), None)
    in_specs = (
        tokens,
        tokens,
        gain,
        weight,
        whole_rows,
        whole_rows,
        columns,
        gain,
        gain,
        weight,
        weight,
        columns,
        gain,
    )
    out_specs = (
        rows,
        rows,
        gain,
        weight,
        whole_rows,
        whole_rows,
        columns,
        gain,
        gain,
        weight,
        weight,
        columns,
        gain,
    )
    return jax.shard_map(shards, mesh=mesh, in_specs=in_specs, out_specs=out_specs, check_vma=False)
```

```python
import functools

import jax
import jax.numpy as jnp
from jax import lax
from jax.experimental import pallas as pl
from jax.experimental.pallas import tpu as pltpu
from jax.sharding import PartitionSpec as P

Q_HEADS = 8
KV_HEADS = 4
HEAD_DIM = 256
WINDOW = 4096

EPSILON = 1e-06
SOFT_CAP = 50.0
ROPE_BASE = 10000.0
GELU_SCALE = (2.0 / 3.141592653589793) ** 0.5
GELU_CUBE = 0.044715
MESH = pl.DeviceIdType.MESH
VMEM_LIMIT = 56 * 1024 * 1024
LANES = 128
BF16 = jnp.bfloat16
F32 = jnp.float32


def after(value, *earlier):
    return lax.optimization_barrier((value, *earlier))[0]


def dot_nn(left, right):
    return lax.dot_general(left, right, (((1,), (0,)), ((), ())), preferred_element_type=F32)


def dot_nt(left, right):
    return lax.dot_general(left, right, (((1,), (1,)), ((), ())), preferred_element_type=F32)


def dot_tn(left, right):
    return lax.dot_general(left, right, (((0,), (0,)), ((), ())), preferred_element_type=F32)


def rms_scale(vector):
    return lax.rsqrt(jnp.mean(vector * vector, axis=-1, keepdims=True) + EPSILON)


def rotary(vector, cosine, sine, direction):
    half_dim = vector.shape[-1] // 2
    first_half = vector[..., :half_dim]
    second_half = vector[..., half_dim:]
    return jnp.concatenate(
        [
            first_half * cosine - direction * (second_half * sine),
            second_half * cosine + direction * (first_half * sine),
        ],
        axis=-1,
    )


def gather_kernel(sizes, x_ref, o_ref, send_sem, recv_sem):
    dp_size, seq_size = sizes
    count = dp_size * seq_size
    dp, seq, mp = lax.axis_index("dp"), lax.axis_index("seq"), lax.axis_index("mp")
    rank = dp * seq_size + seq

    def peer(k):
        other = lax.rem(rank + k, count)
        return (other // seq_size, lax.rem(other, seq_size), mp)

    barrier = pltpu.get_barrier_semaphore()
    for k in range(1, count):
        pl.semaphore_signal(barrier, inc=1, device_id=peer(k), device_id_type=MESH)
    pl.semaphore_wait(barrier, count - 1)
    copies = []
    for k in range(1, count):
        copies.append(
            pltpu.make_async_remote_copy(
                src_ref=x_ref,
                dst_ref=o_ref.at[rank],
                send_sem=send_sem.at[k],
                recv_sem=recv_sem.at[k],
                device_id=peer(k),
                device_id_type=MESH,
            )
        )
        copies[-1].start()
    o_ref[pl.ds(rank, 1)] = x_ref[...][None]
    for copy in copies:
        copy.wait()


def gather_gains(gains, dp_size, seq_size):
    count = dp_size * seq_size
    local = gains[0].shape[0]
    width = -(-local // LANES) * LANES
    block = jnp.stack([gain.astype(F32) for gain in gains])
    block = jnp.pad(block, ((0, 8 - len(gains)), (0, width - local)))
    full = pl.pallas_call(
        functools.partial(gather_kernel, (dp_size, seq_size)),
        out_shape=jax.ShapeDtypeStruct((count, 8, width), F32),
        in_specs=[pl.BlockSpec(memory_space=pltpu.VMEM)],
        out_specs=pl.BlockSpec(memory_space=pltpu.VMEM),
        scratch_shapes=[
            pltpu.SemaphoreType.DMA((count,)),
            pltpu.SemaphoreType.DMA((count,)),
        ],
        compiler_params=pltpu.CompilerParams(collective_id=1, has_side_effects=True),
    )(block)
    full = jnp.transpose(full[:, : len(gains), :local], (1, 0, 2)).reshape(len(gains), -1)
    return [full[i : i + 1] for i in range(len(gains))]


def flipped(index, k):
    result, bit = index, 1
    while bit <= k:
        if k & bit:
            result = result + bit * (1 - 2 * lax.rem(index // bit, 2))
        bit *= 2
    return result


def last_kernel(sizes, heads, x_ref, kv_ref, o_ref, key_ref, value_ref, mine, from_mp, from_ws, kv_from, sems):
    dp_size, seq_size, mp_size = sizes
    count = dp_size * seq_size
    dp, seq, mp = lax.axis_index("dp"), lax.axis_index("seq"), lax.axis_index("mp")
    rank = dp * seq_size + seq

    def mp_peer(k):
        return (dp, seq, flipped(mp, k))

    def ws_rank(k):
        return lax.rem(rank + k, count)

    def ws_peer(k):
        other = ws_rank(k)
        return (other // seq_size, lax.rem(other, seq_size), mp)

    def remote(src, dst, kind, k, device):
        copy = pltpu.make_async_remote_copy(
            src_ref=src,
            dst_ref=dst,
            send_sem=sems.at[kind, 0, k],
            recv_sem=sems.at[kind, 1, k],
            device_id=device,
            device_id_type=MESH,
        )
        copy.start()
        return copy

    barrier = pltpu.get_barrier_semaphore()
    for k in range(1, mp_size):
        pl.semaphore_signal(barrier, inc=1, device_id=mp_peer(k), device_id_type=MESH)
    for k in range(1, count):
        pl.semaphore_signal(barrier, inc=1, device_id=ws_peer(k), device_id_type=MESH)
    pl.semaphore_wait(barrier, mp_size - 1 + count - 1)
    copies = [remote(x_ref, from_mp.at[k], 0, k, mp_peer(k)) for k in range(1, mp_size)]
    kv_copies = [remote(kv_ref, kv_from.at[k], 1, k, mp_peer(k)) for k in range(1, mp_size)]
    for copy in copies:
        copy.wait()
    total = x_ref[...]
    for k in range(1, mp_size):
        total = total + from_mp[k]
    mine[...] = total
    copies = [remote(mine.at[ws_rank(k)], from_ws.at[k], 2, k, ws_peer(k)) for k in range(1, count)]
    key_ref[...] = jnp.zeros_like(key_ref)
    value_ref[...] = jnp.zeros_like(value_ref)
    for k in range(mp_size):
        if k:
            kv_copies[k - 1].wait()
        piece = (kv_from[k] if k else kv_ref[...]).astype(F32)
        head = flipped(mp, k) * heads // (Q_HEADS // KV_HEADS)
        columns = pl.ds(pl.multiple_of(head * HEAD_DIM, HEAD_DIM), HEAD_DIM)
        key_ref[:, columns] += piece[:, :HEAD_DIM]
        value_ref[:, columns] += piece[:, HEAD_DIM:]
    for copy in copies:
        copy.wait()
    own = mine[pl.ds(rank, 1)][0]
    for k in range(1, count):
        own = own + from_ws[k]
    o_ref[...] = own


def last_sums(grads, kv, kv_width, heads, sizes):
    dp_size, seq_size, mp_size = sizes
    count = dp_size * seq_size
    local = grads[0].shape[0] // count
    width = -(-local // LANES) * LANES
    block = jnp.transpose(jnp.stack(grads).reshape(len(grads), count, local), (1, 0, 2))
    block = jnp.pad(block, ((0, 0), (0, 8 - len(grads)), (0, width - local)))
    kv_out = jax.ShapeDtypeStruct((kv.shape[0], kv_width), F32)
    total, key, value = pl.pallas_call(
        functools.partial(last_kernel, sizes, heads),
        out_shape=(jax.ShapeDtypeStruct((8, width), F32), kv_out, kv_out),
        in_specs=[pl.BlockSpec(memory_space=pltpu.VMEM)] * 2,
        out_specs=(pl.BlockSpec(memory_space=pltpu.VMEM),) * 3,
        scratch_shapes=[
            pltpu.VMEM((count, 8, width), F32),
            pltpu.VMEM((mp_size, count, 8, width), F32),
            pltpu.VMEM((count, 8, width), F32),
            pltpu.VMEM((mp_size, *kv.shape), BF16),
            pltpu.SemaphoreType.DMA((3, 2, max(count, mp_size))),
        ],
        compiler_params=pltpu.CompilerParams(
            collective_id=2, has_side_effects=True, vmem_limit_bytes=VMEM_LIMIT
        ),
    )(block, kv)
    return [total[i, :local] for i in range(len(grads))], key, value


def key_mask(shape, first_key, first_query, tile, far):
    key = first_key + lax.broadcasted_iota(jnp.int32, shape, 0)
    query = first_query + lax.rem(lax.broadcasted_iota(jnp.int32, shape, 1), tile)
    return key > query if far else key <= query


def for_key_tiles(tile_fn, index, tile, span, step, hops, windowed):
    seq = lax.axis_index("seq")
    per_block = span // step
    last = jnp.minimum(seq, hops)
    if windowed:
        @pl.when(seq >= hops)
        def _():
            tile_fn(pl.multiple_of((seq - hops) * span, span), span, "far")

        last = jnp.minimum(seq, hops - 1)

    def past(t, carry):
        tile_fn(pl.multiple_of(t * step, step), step, "")
        return carry

    lax.fori_loop((seq - last) * per_block, seq * per_block, past, 0)
    tile_fn(pl.multiple_of(seq * span, span), (index + 1) * tile, "near")


def head_rows(ref, index, tile):
    block = ref[pl.ds(index * tile, tile), :]
    return jnp.concatenate(
        [block[:, h * HEAD_DIM : (h + 1) * HEAD_DIM] for h in range(ref.shape[1] // HEAD_DIM)], axis=0
    )


def put_head_rows(ref, index, tile, rows):
    for h in range(ref.shape[1] // HEAD_DIM):
        ref[pl.ds(index * tile, tile), h * HEAD_DIM : (h + 1) * HEAD_DIM] = rows[
            h * tile : (h + 1) * tile
        ].astype(ref.dtype)


def attend_kernel(plan, q_ref, kv_ref, o_ref, of_ref, lse_ref, acc, total):
    tile, span, step, hops, windowed = plan
    for i in range(span // tile):
        query = head_rows(q_ref, i, tile)
        rows = query.shape[0]
        acc[...] = jnp.zeros_like(acc)
        total[...] = jnp.zeros_like(total)

        def tile_fn(first, count, mask, i=i, query=query, rows=rows):
            key = kv_ref[pl.ds(first, count), :HEAD_DIM]
            value = kv_ref[pl.ds(first, count), HEAD_DIM:]
            raw = dot_nt(key, query)
            weight = jnp.exp(SOFT_CAP * jnp.tanh(raw * (1.0 / SOFT_CAP)))
            if mask:
                inside = key_mask(weight.shape, 0, i * tile, tile, mask == "far")
                weight = jnp.where(inside, weight, 0.0)
            total[...] += jnp.sum(weight.reshape(count // 8, 8, rows), axis=0)
            acc[...] += dot_tn(value, weight.astype(BF16))

        for_key_tiles(tile_fn, i, tile, span, step, hops, windowed)
        row_total = jnp.sum(total[...], axis=0, keepdims=True)
        out = (acc[...] / row_total).T
        put_head_rows(o_ref, i, tile, out)
        put_head_rows(of_ref, i, tile, out)
        lse_ref[i] = jnp.log(row_total)


def attend_back_kernel(plan, q_ref, do_ref, of_ref, lse_ref, kv_ref, dq_ref, dkv_ref, grads, acc):
    tile, span, step, hops, windowed = plan
    grads[...] = jnp.zeros_like(grads)
    for i in range(span // tile):
        query = head_rows(q_ref, i, tile)
        dout = head_rows(do_ref, i, tile)
        lse = lse_ref[i]
        delta = jnp.sum(dout.astype(F32) * head_rows(of_ref, i, tile), axis=-1, keepdims=True)
        delta = jnp.broadcast_to(delta, (delta.shape[0], LANES)).T[:1]
        acc[...] = jnp.zeros_like(acc)

        def tile_fn(first, count, mask, i=i, query=query, dout=dout, lse=lse, delta=delta):
            key = kv_ref[pl.ds(first, count), :HEAD_DIM]
            value = kv_ref[pl.ds(first, count), HEAD_DIM:]
            bounded = jnp.tanh(dot_nt(key, query) * (1.0 / SOFT_CAP))
            prob = jnp.exp(SOFT_CAP * bounded - lse)
            if mask:
                inside = key_mask(prob.shape, 0, i * tile, tile, mask == "far")
                prob = jnp.where(inside, prob, 0.0)
            dprob = dot_nt(value, dout)
            draw = (prob * (dprob - delta) * (1.0 - bounded * bounded)).astype(BF16)
            grads[pl.ds(first, count), HEAD_DIM:] += dot_nn(prob.astype(BF16), dout)
            grads[pl.ds(first, count), :HEAD_DIM] += dot_nn(draw, query)
            acc[...] += dot_tn(key, draw)

        for_key_tiles(tile_fn, i, tile, span, step, hops, windowed)
        put_head_rows(dq_ref, i, tile, acc[...].T)
    dkv_ref[...] = grads[...].astype(BF16)


def attention_plan(span, seq_size):
    hops = min(WINDOW // span, seq_size - 1)
    return (min(256, span), span, min(512, span), hops, seq_size * span > WINDOW)


def attend(queries, pairs, plan):
    tile, span = plan[:2]
    heads = queries.shape[1] // HEAD_DIM
    rows = heads * tile
    return pl.pallas_call(
        functools.partial(attend_kernel, plan),
        out_shape=(
            jax.ShapeDtypeStruct(queries.shape, BF16),
            jax.ShapeDtypeStruct(queries.shape, F32),
            jax.ShapeDtypeStruct((span // tile, 1, rows), F32),
        ),
        in_specs=[pl.BlockSpec(memory_space=pltpu.VMEM)] * 2,
        out_specs=(pl.BlockSpec(memory_space=pltpu.VMEM),) * 3,
        scratch_shapes=[pltpu.VMEM((HEAD_DIM, rows), F32), pltpu.VMEM((8, rows), F32)],
        compiler_params=pltpu.CompilerParams(vmem_limit_bytes=VMEM_LIMIT),
        cost_estimate=pl.CostEstimate(
            flops=12 * queries.size * span, bytes_accessed=8 * queries.size, transcendentals=0
        ),
    )(queries, pairs)


def attend_back(queries, dout, exact, lse, pairs, plan):
    tile, span = plan[:2]
    rows = queries.shape[1] // HEAD_DIM * tile
    return pl.pallas_call(
        functools.partial(attend_back_kernel, plan),
        out_shape=(
            jax.ShapeDtypeStruct(queries.shape, F32),
            jax.ShapeDtypeStruct(pairs.shape, BF16),
        ),
        in_specs=[pl.BlockSpec(memory_space=pltpu.VMEM)] * 5,
        out_specs=(pl.BlockSpec(memory_space=pltpu.VMEM),) * 2,
        scratch_shapes=[pltpu.VMEM(pairs.shape, F32), pltpu.VMEM((HEAD_DIM, rows), F32)],
        compiler_params=pltpu.CompilerParams(vmem_limit_bytes=VMEM_LIMIT),
        cost_estimate=pl.CostEstimate(
            flops=30 * queries.size * span, bytes_accessed=8 * queries.size, transcendentals=0
        ),
    )(queries, dout, exact, lse, pairs)


def remote_copy(src, dst, sems, index, device):
    copy = pltpu.make_async_remote_copy(
        src_ref=src,
        dst_ref=dst,
        send_sem=sems.at[(0, *index)],
        recv_sem=sems.at[(1, *index)],
        device_id=device,
        device_id_type=MESH,
    )
    copy.start()
    return copy


def sum_direct(parts_at, steps, step, mp_size, peer, total, sent, arrived, sems):
    copies = []
    for t in range(steps):
        for k in range(mp_size - 1, -1, -1):
            part = parts_at(t, k)
            if k == 0:
                total[:, t * step : (t + 1) * step] = part
            else:
                sent[t, k - 1] = part.astype(BF16)
                copies.append(
                    remote_copy(sent.at[t, k - 1], arrived.at[t, k - 1], sems, (t, k - 1), peer(k))
                )
    for t in range(steps):
        for k in range(1, mp_size):
            copies[t * (mp_size - 1) + mp_size - 1 - k].wait_recv()
            total[:, t * step : (t + 1) * step] += arrived[t, k - 1].astype(F32)
    return copies


def sum_square(parts_at, steps, step, peer, total, kept, sent, arrived, sems):
    half = step // 2
    copies, second = [], []
    for t in range(steps):
        first = t * step
        far = parts_at(t, 3)
        sent[t, 0, 1] = far[:, :half].astype(BF16)
        sent[t, 1, 1] = far[:, half:].astype(BF16)
        part = parts_at(t, 1)
        sent[t, 0, 0] = part[:, :half].astype(BF16)
        kept[t, 0] = part[:, half:]
        copies.append(
            remote_copy(sent.at[t, 0, pl.ds(0, 2)], arrived.at[t, 0, pl.ds(0, 2)], sems, (t, 0), peer(1))
        )
        part = parts_at(t, 2)
        sent[t, 1, 0] = part[:, half:].astype(BF16)
        kept[t, 1] = part[:, :half]
        copies.append(
            remote_copy(sent.at[t, 1, pl.ds(0, 2)], arrived.at[t, 1, pl.ds(0, 2)], sems, (t, 1), peer(2))
        )
        total[:, first : first + step] = parts_at(t, 0)
    for t in range(steps):
        copies[2 * t].wait_recv()
        sent[t, 1, 2] = (kept[t, 1] + arrived[t, 0, 1].astype(F32)).astype(BF16)
        second.append(remote_copy(sent.at[t, 1, 2], arrived.at[t, 1, 2], sems, (t, 2), peer(2)))
        copies[2 * t + 1].wait_recv()
        sent[t, 0, 2] = (kept[t, 0] + arrived[t, 1, 1].astype(F32)).astype(BF16)
        second.append(remote_copy(sent.at[t, 0, 2], arrived.at[t, 0, 2], sems, (t, 3), peer(1)))
    for t in range(steps):
        first = t * step
        second[2 * t].wait_recv()
        total[:, first : first + half] += arrived[t, 0, 0].astype(F32) + arrived[t, 1, 2].astype(F32)
        second[2 * t + 1].wait_recv()
        total[:, first + half : first + step] += arrived[t, 1, 0].astype(F32) + arrived[t, 0, 2].astype(
            F32
        )
    return copies + second


def gather_direct(own, gathered, share, mp_size, peer, sems):
    copies = [
        remote_copy(own, gathered.at[pl.ds(k * share, share)], sems, (k,), peer(k))
        for k in range(mp_size - 1, 0, -1)
    ]
    for copy in copies:
        copy.wait()


def gather_square(own, gathered, share, peer, sems):
    half = share // 2

    def place(k, lower):
        return gathered.at[pl.ds(k * share + lower * half, half)]

    upper, lower = own.at[pl.ds(0, half)], own.at[pl.ds(half, half)]
    to_one = remote_copy(upper, place(1, 0), sems, (0,), peer(1))
    to_two = remote_copy(lower, place(2, 1), sems, (1,), peer(2))
    copies = [
        remote_copy(upper, place(2, 0), sems, (2,), peer(2)),
        remote_copy(lower, place(1, 1), sems, (3,), peer(1)),
    ]
    to_one.wait_recv()
    copies.append(remote_copy(place(1, 0), place(3, 0), sems, (4,), peer(2)))
    to_two.wait_recv()
    copies.append(remote_copy(place(2, 1), place(3, 1), sems, (5,), peer(1)))
    to_one.wait_send()
    to_two.wait_send()
    for copy in copies:
        copy.wait()


def rows_kernel(plan, rows_fn, *refs):
    mp_size, share, step, row_step, natural, n_left, n_aux, n_out, gather = plan
    lefts, weight_ref, refs = refs[:n_left], refs[n_left], refs[n_left + 1 :]
    aux, refs = refs[:n_aux], refs[n_aux:]
    outs, refs = refs[:n_out], refs[n_out:]
    if gather:
        gathered, refs = refs[0], refs[1:]
    left, weight, total, own, kept, sent, arrived, in_sem, sum_sem, row_sem = refs
    steps = total.shape[1] // step
    dp, seq, mp = lax.axis_index("dp"), lax.axis_index("seq"), lax.axis_index("mp")

    def peer(k):
        return (dp, seq, flipped(mp, k))

    left_copies, weight_copies = {}, []
    for k in range(mp_size):
        first = (flipped(mp, k) if natural else k) * share
        left_copies[k] = []
        column = 0
        for i, ref in enumerate(lefts):
            depth = ref.shape[1]
            left_copies[k].append(
                pltpu.make_async_copy(
                    ref.at[pl.ds(first, share)],
                    left.at[k, :, pl.ds(column, depth)],
                    in_sem.at[2 + k * n_left + i],
                )
            )
            column += depth
    for t in range(steps):
        weight_copies.append(
            pltpu.make_async_copy(
                weight_ref.at[pl.ds(t * step, step)], weight.at[t % 2], in_sem.at[t % 2]
            )
        )
    weight_copies[0].start()
    for k in range(mp_size - 1, -1, -1):
        for copy in left_copies[k]:
            copy.start()

    barrier = pltpu.get_barrier_semaphore()
    for k in range(1, mp_size):
        pl.semaphore_signal(barrier, inc=1, device_id=peer(k), device_id_type=MESH)
    pl.semaphore_wait(barrier, mp_size - 1)

    def parts_at(t, k):
        if k == mp_size - 1:
            weight_copies[t].wait()
            if t + 1 < steps:
                weight_copies[t + 1].start()
        if t == 0:
            for copy in left_copies[k]:
                copy.wait()
        return dot_nt(left[k], weight[t % 2])

    finish_rows(
        parts_at,
        (mp_size, share, step, row_step),
        (rows_fn, aux, outs, gathered if gather else None),
        peer,
        (total, own, kept, sent, arrived),
        (sum_sem, row_sem, in_sem.at[0]),
    )


def finish_rows(parts_at, sizes, rows, peer, buffers, sems):
    mp_size, share, step, row_step = sizes
    rows_fn, aux, outs, gathered = rows
    total, own, kept, sent, arrived = buffers
    sum_sem, row_sem, keep_sem = sems
    steps = total.shape[1] // step
    if mp_size == 4:
        sums = sum_square(parts_at, steps, step, peer, total, kept, sent, arrived, sum_sem)
    else:
        sums = sum_direct(parts_at, steps, step, mp_size, peer, total, sent, arrived, sum_sem)

    def rows_at(r, carry):
        rows = pl.ds(pl.multiple_of(r * row_step, row_step), row_step)
        result = rows_fn(total[rows, :], rows, aux, outs)
        if gathered is not None:
            own[rows, :] = result.astype(BF16)
        return carry

    for ref in outs:
        if ref.shape[0] == 8:
            ref[...] = jnp.zeros_like(ref)
    lax.fori_loop(0, share // row_step, rows_at, 0)
    if gathered is not None:
        keep = pltpu.make_async_copy(own, gathered.at[pl.ds(0, share)], keep_sem)
        keep.start()
        if mp_size == 4:
            gather_square(own, gathered, share, peer, row_sem)
        else:
            gather_direct(own, gathered, share, mp_size, peer, row_sem)
        keep.wait()
    for copy in sums:
        copy.wait_send()


def row_plan(width, share, mp_size):
    step = 768 if width % 768 == 0 else width
    steps = width // step
    if mp_size == 4:
        pieces, kept = (steps, 2, 3, share, step // 2), (steps, 2, share, step // 2)
    else:
        pieces, kept = (steps, mp_size - 1, share, step), (8, LANES)
    buffers = [
        pltpu.VMEM((share, width), F32),
        pltpu.VMEM((share, width), BF16),
        pltpu.VMEM(kept, F32),
        pltpu.VMEM(pieces, BF16),
        pltpu.VMEM(pieces, BF16),
    ]
    sems = [
        pltpu.SemaphoreType.DMA((2, steps, max(4, mp_size - 1))),
        pltpu.SemaphoreType.DMA((2, max(6, mp_size))),
    ]
    return step, min(32, share), buffers, sems


def sum_rows(lefts, weight, rows_fn, aux, outs, gather, natural, mp_size, collective_id):
    span = lefts[0].shape[0]
    width, depth = weight.shape
    share = span // mp_size
    step, row_step, buffers, sems = row_plan(width, share, mp_size)
    plan = (mp_size, share, step, row_step, natural, len(lefts), len(aux), len(outs), gather)
    out_shape = [jax.ShapeDtypeStruct((rows, width), dtype) for rows, dtype in outs]
    out_specs = [pl.BlockSpec(memory_space=pltpu.VMEM)] * len(outs)
    if gather:
        out_shape.append(jax.ShapeDtypeStruct((span, width), BF16))
        out_specs.append(pl.BlockSpec(memory_space=pl.ANY))
    return pl.pallas_call(
        functools.partial(rows_kernel, plan, rows_fn),
        out_shape=out_shape,
        in_specs=[pl.BlockSpec(memory_space=pl.ANY)] * (len(lefts) + 1)
        + [pl.BlockSpec(memory_space=pltpu.VMEM)] * len(aux),
        out_specs=out_specs,
        scratch_shapes=[
            pltpu.VMEM((mp_size, share, depth), BF16),
            pltpu.VMEM((2, step, depth), BF16),
            *buffers,
            pltpu.SemaphoreType.DMA((2 + mp_size * len(lefts),)),
            *sems,
        ],
        compiler_params=pltpu.CompilerParams(
            collective_id=collective_id, has_side_effects=True, vmem_limit_bytes=VMEM_LIMIT
        ),
    )(*lefts, weight, *aux)


def weight_grad_kernel(plan, *refs):
    n_right, tile, half, steps, seq_size = plan
    left_ref, rights, out_ref = refs[0], refs[1 : 1 + n_right], refs[1 + n_right]
    left, right, sent, arrived, own, result, in_sem, swap_sem, out_sem = refs[2 + n_right :]
    dp, seq, mp = lax.axis_index("dp"), lax.axis_index("seq"), lax.axis_index("mp")
    other = (1 - dp, seq, mp)
    lefts = []
    part = half // steps
    for i, side in enumerate((1 - dp, dp)):
        for n in range(steps):
            columns = pl.ds(pl.multiple_of((2 * n + side) * part, LANES), part)
            lefts.append(
                pltpu.make_async_copy(
                    left_ref.at[:, columns],
                    left.at[i, :, pl.ds(n * part, part)],
                    in_sem.at[2 + i * steps + n],
                )
            )
    for load in lefts:
        load.start()
    sources = []
    for ref in rights:
        for first in range(0, ref.shape[1], tile):
            sources.append(ref.at[:, pl.ds(first, tile)])
    tiles = len(sources)
    loads = [
        pltpu.make_async_copy(source, right.at[t % 2], in_sem.at[t % 2])
        for t, source in enumerate(sources)
    ]
    loads[0].start()
    barrier = pltpu.get_barrier_semaphore()
    pl.semaphore_signal(barrier, inc=1, device_id=other, device_id_type=MESH)
    pl.semaphore_wait(barrier, 1)
    swaps, stores = [], []

    def store(t):
        piece = part // seq_size
        copies = []
        for n in range(steps):
            for z in range(seq_size):
                copies.append(
                    pltpu.make_async_copy(
                        result.at[t % 2, pl.ds(n * part + z * piece, piece)],
                        out_ref.at[pl.ds((z * steps + n) * piece, piece), pl.ds(t * tile, tile)],
                        out_sem.at[t % 2, n * seq_size + z],
                    )
                )
        return copies

    def finish(t):
        swaps[t].wait_recv()
        if t >= 2:
            for copy in stores[t - 2]:
                copy.wait()
        result[t % 2] = (own[t % 2] + arrived[t].astype(F32)).astype(BF16)
        stores.append(store(t))
        for copy in stores[t]:
            copy.start()

    for t in range(tiles):
        loads[t].wait()
        if t + 1 < tiles:
            loads[t + 1].start()
        if t == 0:
            for load in lefts[:steps]:
                load.wait()
        sent[t] = dot_tn(left[0], right[t % 2]).astype(BF16)
        swaps.append(remote_copy(sent.at[t], arrived.at[t], swap_sem, (t,), other))
        if t == 0:
            for load in lefts[steps:]:
                load.wait()
        own[t % 2] = dot_tn(left[1], right[t % 2])
        if t >= 1:
            finish(t - 1)
    finish(tiles - 1)
    for copies in stores[-2:]:
        for copy in copies:
            copy.wait()
    for swap in swaps:
        swap.wait_send()


def weight_grad(left, rights, collective_id, steps=1, seq_size=1):
    rows, width = left.shape
    half = width // 2
    total = sum(right.shape[1] for right in rights)
    tile = min(768 if rights[0].shape[1] % 768 == 0 else 384, rights[0].shape[1])
    tile = next(t for t in (tile, 256, LANES) if all(right.shape[1] % t == 0 for right in rights))
    tiles = total // tile
    return pl.pallas_call(
        functools.partial(weight_grad_kernel, (len(rights), tile, half, steps, seq_size)),
        out_shape=jax.ShapeDtypeStruct((half, total), BF16),
        in_specs=[pl.BlockSpec(memory_space=pl.ANY)] * (1 + len(rights)),
        out_specs=pl.BlockSpec(memory_space=pl.ANY),
        scratch_shapes=[
            pltpu.VMEM((2, rows, half), BF16),
            pltpu.VMEM((2, rows, tile), BF16),
            pltpu.VMEM((tiles, half, tile), BF16),
            pltpu.VMEM((tiles, half, tile), BF16),
            pltpu.VMEM((2, half, tile), F32),
            pltpu.VMEM((2, half, tile), BF16),
            pltpu.SemaphoreType.DMA((2 + 2 * steps,)),
            pltpu.SemaphoreType.DMA((2, tiles)),
            pltpu.SemaphoreType.DMA((2, steps * seq_size)),
        ],
        compiler_params=pltpu.CompilerParams(
            collective_id=collective_id, has_side_effects=True, vmem_limit_bytes=VMEM_LIMIT
        ),
    )(left, *rights)


def ffw_kernel(plan, normed_ref, gate_up_ref, shard_ref, resid_ref, cotangent_ref, gain_ref, *refs):
    mp_size, seq_size, share, step, row_step, tile = plan
    output_ref, gain_grad_ref, dmixed_ref, hidden_ref, act_ref, slope_ref, down_ref = refs[:7]
    normed, gate_up, hidden, down, staged, *refs = refs[7:]
    buffers, refs = refs[:5], refs[5:]
    load_sem, store_sem, local_sem, line_sem, pair_sem, sum_sem, row_sem = refs
    steps, _, units = down.shape
    piece = step // (2 * seq_size)
    far = seq_size - 1
    dp, seq, mp = lax.axis_index("dp"), lax.axis_index("seq"), lax.axis_index("mp")
    sibling = (1 - dp, seq, mp)

    def peer(k):
        return (dp, seq, flipped(mp, k))

    def along(way):
        return (dp, seq + 1 - 2 * way, mp)

    def goes_on(way):
        return seq < far if way == 0 else seq > 0

    def comes(way, distance):
        return seq >= distance if way == 0 else seq + distance <= far

    def block(t, at):
        first = pl.multiple_of((dp * seq_size + at) * piece, piece)
        return down.at[t, pl.ds(first, piece)]

    def line(t, way, distance):
        at = seq - distance if way == 0 else seq + distance
        return pltpu.make_async_remote_copy(
            src_ref=block(t, at),
            dst_ref=block(t, at),
            send_sem=line_sem.at[0, t, way, distance],
            recv_sem=line_sem.at[1, t, way, distance],
            device_id=along(way),
            device_id_type=MESH,
        )

    def pair(t, way, distance):
        at = seq - distance if way == 0 else seq + distance
        return pltpu.make_async_remote_copy(
            src_ref=block(t, at),
            dst_ref=block(t, at),
            send_sem=pair_sem.at[0, t, way, distance],
            recv_sem=pair_sem.at[1, t, way, distance],
            device_id=sibling,
            device_id_type=MESH,
        )

    normed_load = pltpu.make_async_copy(normed_ref, normed, local_sem.at[0])
    normed_load.start()
    shard_loads = [
        pltpu.make_async_copy(
            shard_ref.at[pl.ds(t * piece, piece)], block(t, seq), local_sem.at[1 + t]
        )
        for t in range(steps)
    ]
    for load in shard_loads:
        load.start()

    def loads(i, slot):
        return [
            pltpu.make_async_copy(
                gate_up_ref.at[:, pl.ds(pl.multiple_of(side * units + i * tile, LANES), tile)],
                gate_up.at[slot, side],
                load_sem.at[slot, side],
            )
            for side in range(2)
        ]

    def stores(i, slot):
        columns = pl.ds(pl.multiple_of(i * tile, LANES), tile)
        return [
            pltpu.make_async_copy(staged.at[slot, 0], act_ref.at[:, columns], store_sem.at[slot, 0]),
            pltpu.make_async_copy(staged.at[slot, 1], slope_ref.at[:, columns], store_sem.at[slot, 1]),
        ]

    for load in loads(0, 0):
        load.start()
    barrier = pltpu.get_barrier_semaphore()
    for k in range(1, mp_size):
        pl.semaphore_signal(barrier, inc=1, device_id=peer(k), device_id_type=MESH)
    pl.semaphore_signal(barrier, inc=1, device_id=sibling, device_id_type=MESH)
    for way in range(2):
        @pl.when(goes_on(way))
        def _(way=way):
            pl.semaphore_signal(barrier, inc=1, device_id=along(way), device_id_type=MESH)

    line_peers = (seq + far) // seq_size + (2 * far - seq) // seq_size
    pl.semaphore_wait(barrier, mp_size + line_peers)

    for t in range(steps):
        shard_loads[t].wait()
        for way in range(2):
            @pl.when(goes_on(way))
            def _(t=t, way=way):
                line(t, way, 0).start()
    for t in range(steps):
        pair(t, 0, 0).start()
    normed_load.wait()

    def arrival(t, distance):
        for way in range(2):
            @pl.when(comes(way, distance))
            def _(way=way):
                line(t, way, distance - 1).wait_recv()
                if distance < far:
                    @pl.when(goes_on(way))
                    def _():
                        line(t, way, distance).start()

                pair(t, way, distance).start()

    arrivals = [(t, distance) for distance in range(1, seq_size) for t in range(steps)]
    tiles = units // tile
    early = [(2 * n + 2, event) for n, event in enumerate(arrivals) if 2 * n + 2 < tiles]
    late = arrivals[len(early) :]

    def units_at(i, carry):
        slot = lax.rem(i, 2)
        for load in loads(i, slot):
            load.wait()

        @pl.when(i + 1 < tiles)
        def _():
            for load in loads(i + 1, 1 - slot):
                load.start()

        @pl.when(i >= 2)
        def _():
            for store in stores(i - 2, slot):
                store.wait()

        gate = dot_nn(normed[...], gate_up[slot, 0])
        up = dot_nn(normed[...], gate_up[slot, 1])
        squared = gate * gate
        bend = jnp.tanh(GELU_SCALE * gate * (1.0 + GELU_CUBE * squared))
        side = 0.5 * (1.0 + bend)
        act = gate * side
        slope = side + (0.5 * GELU_SCALE) * gate * (1.0 - bend * bend) * (1.0 + 3.0 * GELU_CUBE * squared)
        staged[slot, 0] = act.astype(BF16)
        staged[slot, 1] = (slope * up).astype(BF16)
        for store in stores(i, slot):
            store.start()
        product = (act * up).astype(BF16)
        for k in range(mp_size):
            hidden[k, :, pl.ds(pl.multiple_of(i * tile, LANES), tile)] = product[
                k * share : (k + 1) * share
            ]
        for at, event in early:
            @pl.when(i == at)
            def _(event=event):
                arrival(*event)

        return carry

    lax.fori_loop(0, tiles, units_at, 0)
    for i in range(max(0, tiles - 2), tiles):
        for store in stores(i, i % 2):
            store.wait()
    hidden_stores = [
        pltpu.make_async_copy(hidden.at[k], hidden_ref.at[pl.ds(k * share, share)], local_sem.at[1 + k])
        for k in range(mp_size)
    ]
    for store in hidden_stores:
        store.start()
    down_stores = [
        pltpu.make_async_copy(
            down.at[t], down_ref.at[pl.ds(t * step, step)], local_sem.at[1 + mp_size + t]
        )
        for t in range(steps)
    ]
    waiting = list(late)

    def parts_at(t, k):
        if k == mp_size - 1:
            while (t, far) in waiting:
                arrival(*waiting.pop(0))
            pair(t, 0, 0).wait_recv()
            for way in range(2):
                for distance in range(1, seq_size):
                    @pl.when(comes(way, distance))
                    def _(way=way, distance=distance):
                        pair(t, way, distance).wait_recv()

            down_stores[t].start()
        return dot_nt(hidden[k], down[t])

    finish_rows(
        parts_at,
        (mp_size, share, step, row_step),
        (after_ffw, (resid_ref, cotangent_ref, gain_ref), (output_ref, gain_grad_ref), dmixed_ref),
        peer,
        buffers,
        (sum_sem, row_sem, local_sem.at[0]),
    )
    for store in hidden_stores + down_stores:
        store.wait()
    for t in range(steps):
        pair(t, 0, 0).wait_send()
        for way in range(2):
            for distance in range(seq_size - 1):
                @pl.when(goes_on(way) & comes(way, distance))
                def _(t=t, way=way, distance=distance):
                    line(t, way, distance).wait_send()

            for distance in range(1, seq_size):
                @pl.when(comes(way, distance))
                def _(t=t, way=way, distance=distance):
                    pair(t, way, distance).wait_send()


def ffw(normed, gate_up_w, down_shard, resid, cotangent, gain, sizes, collective_id):
    dp_size, seq_size, mp_size = sizes
    span, width = normed.shape
    units = gate_up_w.shape[1] // 2
    share = span // mp_size
    step, row_step, buffers, sems = row_plan(width, share, mp_size)
    steps = width // step
    tile = 256 if units % 256 == 0 else LANES
    plan = (mp_size, seq_size, share, step, row_step, tile)
    per_unit = jax.ShapeDtypeStruct((span, units), BF16)
    return pl.pallas_call(
        functools.partial(ffw_kernel, plan),
        out_shape=(
            jax.ShapeDtypeStruct((share, width), BF16),
            jax.ShapeDtypeStruct((8, width), F32),
            jax.ShapeDtypeStruct((span, width), BF16),
            per_unit,
            per_unit,
            per_unit,
            jax.ShapeDtypeStruct((width, units), BF16),
        ),
        in_specs=[pl.BlockSpec(memory_space=pl.ANY)] * 3 + [pl.BlockSpec(memory_space=pltpu.VMEM)] * 3,
        out_specs=(pl.BlockSpec(memory_space=pltpu.VMEM),) * 2 + (pl.BlockSpec(memory_space=pl.ANY),) * 5,
        scratch_shapes=[
            pltpu.VMEM((span, width), BF16),
            pltpu.VMEM((2, 2, width, tile), BF16),
            pltpu.VMEM((mp_size, share, units), BF16),
            pltpu.VMEM((steps, step, units), BF16),
            pltpu.VMEM((2, 2, span, tile), BF16),
            *buffers,
            pltpu.SemaphoreType.DMA((2, 2)),
            pltpu.SemaphoreType.DMA((2, 2)),
            pltpu.SemaphoreType.DMA((1 + mp_size + steps,)),
            pltpu.SemaphoreType.DMA((2, steps, 2, seq_size)),
            pltpu.SemaphoreType.DMA((2, steps, 2, seq_size)),
            *sems,
        ],
        compiler_params=pltpu.CompilerParams(
            collective_id=collective_id, has_side_effects=True, vmem_limit_bytes=VMEM_LIMIT
        ),
    )(normed, gate_up_w, down_shard, resid, cotangent, gain)


def hidden_back_kernel(dmixed_ref, down_ref, act_ref, slope_ref, dgate_ref, dup_ref):
    dhidden = dot_nn(dmixed_ref[...], down_ref[...])
    dgate_ref[...] = (dhidden * slope_ref[...].astype(F32)).astype(BF16)
    dup_ref[...] = (dhidden * act_ref[...].astype(F32)).astype(BF16)


def hidden_back(dmixed, down_wt, act, slope):
    rows, width = dmixed.shape
    units = down_wt.shape[1]
    tile = 256 if units % 256 == 0 else units
    columns = pl.BlockSpec((rows, tile), lambda i: (0, i))
    return pl.pallas_call(
        hidden_back_kernel,
        grid=(units // tile,),
        out_shape=(jax.ShapeDtypeStruct((rows, units), BF16),) * 2,
        in_specs=[
            pl.BlockSpec((rows, width), lambda i: (0, 0)),
            pl.BlockSpec((width, tile), lambda i: (0, i)),
            columns,
            columns,
        ],
        out_specs=(columns, columns),
        compiler_params=pltpu.CompilerParams(vmem_limit_bytes=VMEM_LIMIT),
    )(dmixed, down_wt, act, slope)


def fold_rows(x):
    return jnp.sum(x.reshape(x.shape[0] // 8, 8, x.shape[1]), axis=0)


def after_attention(attn, rows, aux, outs):
    tokens, gain_two, gain_three = aux
    attn_out, resid_out = outs
    resid = tokens[rows, :].astype(F32) + attn * rms_scale(attn) * gain_two[...]
    attn_out[rows, :] = attn
    resid_out[rows, :] = resid
    return resid * rms_scale(resid) * gain_three[...]


def after_ffw(mixed, rows, aux, outs):
    resid, cotangent, gain_four = aux
    output, gain_grad = outs
    scale = rms_scale(mixed)
    unit = mixed * scale
    grad_out = cotangent[rows, :].astype(F32)
    output[rows, :] = (resid[rows, :] + unit * gain_four[...]).astype(BF16)
    gain_grad[...] += fold_rows(grad_out * unit)
    return vector_back(grad_out, unit, scale, gain_four[...])


def vector_back(grad_in, unit, scale, gain):
    unit_grad = grad_in * gain
    return scale * (unit_grad - unit * jnp.mean(unit_grad * unit, axis=-1, keepdims=True))


def before_ffw(dnormed_two, rows, aux, outs):
    resid, attn, cotangent, gain_two, gain_three = aux
    dresid_out, gain_two_grad, gain_three_grad = outs
    scale = rms_scale(resid[rows, :])
    unit = resid[rows, :] * scale
    gain_three_grad[...] += fold_rows(dnormed_two * unit)
    dresid = cotangent[rows, :].astype(F32) + vector_back(dnormed_two, unit, scale, gain_three[...])
    dresid_out[rows, :] = dresid
    scale = rms_scale(attn[rows, :])
    unit = attn[rows, :] * scale
    gain_two_grad[...] += fold_rows(dresid * unit)
    return vector_back(dresid, unit, scale, gain_two[...])


def before_attention(dnormed_one, rows, aux, outs):
    tokens, dresid, gain_one = aux
    tokens_grad, gain_grad = outs
    vector = tokens[rows, :].astype(F32)
    scale = rms_scale(vector)
    unit = vector * scale
    gain_grad[...] += fold_rows(dnormed_one * unit)
    back = vector_back(dnormed_one, unit, scale, gain_one[...])
    tokens_grad[rows, :] = (dresid[rows, :] + back).astype(BF16)


def swapped(x, axis, k):
    return lax.ppermute(x, axis, [(i, i ^ k) for i in range(lax.axis_size(axis))])


def shards(
    tokens,
    cotangent,
    pre_attn_gain,
    w_query,
    w_key,
    w_value,
    w_out,
    post_attn_gain,
    pre_ffw_gain,
    w_gate,
    w_up,
    w_down,
    post_ffw_gain,
):
    dp_size, seq_size, mp_size = (lax.axis_size(axis) for axis in ("dp", "seq", "mp"))
    dp, seq, mp = lax.axis_index("dp"), lax.axis_index("seq"), lax.axis_index("mp")
    both = ("dp", "seq")
    heads = w_query.shape[1] // HEAD_DIM
    group = Q_HEADS // KV_HEADS
    kv_first = mp * heads // group
    q_width = heads * HEAD_DIM
    span = tokens.shape[1]
    width = tokens.shape[2]
    share = span // mp_size
    plan = attention_plan(span, seq_size)

    def gather_weight(x):
        return lax.all_gather(x, both, axis=0, tiled=True)

    w_qkv_own = jnp.concatenate(
        [
            w_query,
            lax.dynamic_slice_in_dim(w_key, kv_first * HEAD_DIM, HEAD_DIM, 1),
            lax.dynamic_slice_in_dim(w_value, kv_first * HEAD_DIM, HEAD_DIM, 1),
        ],
        axis=1,
    )
    w_qkv = gather_weight(w_qkv_own)
    gain_one, gain_two, gain_three, gain_four = gather_gains(
        [pre_attn_gain, post_attn_gain, pre_ffw_gain, post_ffw_gain], dp_size, seq_size
    )

    inputs = tokens[0].astype(F32)
    positions = seq * span + jnp.arange(span, dtype=jnp.int32)
    half_dim = HEAD_DIM // 2
    frequency = ROPE_BASE ** (-jnp.arange(half_dim, dtype=F32) * 2.0 / HEAD_DIM)
    angles = positions.astype(F32)[:, None, None] * frequency
    cosine = jnp.cos(angles)
    sine = jnp.sin(angles)
    scale_one = rms_scale(inputs)
    normed_one = (inputs * scale_one * gain_one).astype(BF16)
    w_out_t = gather_weight(after(w_out.T, w_qkv, normed_one))
    key_lin = dot_nn(normed_one, w_qkv[:, q_width : q_width + HEAD_DIM])
    keys_own = rotary(key_lin, cosine[:, 0], sine[:, 0], 1.0).astype(BF16)
    values_own = dot_nn(normed_one, w_qkv[:, q_width + HEAD_DIM :]).astype(BF16)
    own_pair = jnp.concatenate([keys_own, values_own], axis=1)
    pairs = lax.all_gather(after(own_pair, w_out_t), "seq", axis=0, tiled=True)
    query_lin = dot_nn(normed_one, w_qkv[:, :q_width]).reshape(span, heads, HEAD_DIM)
    queries = (rotary(query_lin, cosine, sine, 1.0) * HEAD_DIM ** (-0.5)).astype(BF16)
    queries = queries.reshape(span, q_width)

    units = w_gate.shape[1]
    gate_up_w = gather_weight(after(jnp.concatenate([w_gate, w_up], axis=1), pairs))

    attn_o, attn_exact, lse = attend(queries, pairs, plan)
    own_first = mp * share
    tokens_own = lax.dynamic_slice_in_dim(tokens[0], own_first, share, 0)
    cotangent_own = lax.dynamic_slice_in_dim(cotangent[0], own_first, share, 0)

    def by_owner(x):
        return jnp.concatenate(
            [lax.dynamic_slice_in_dim(x, (mp ^ k) * share, share, 0) for k in range(mp_size)], axis=0
        )

    attn, resid, normed_two = sum_rows(
        (attn_o,),
        w_out_t,
        after_attention,
        (tokens_own, gain_two, gain_three),
        ((share, F32), (share, F32)),
        True,
        True,
        mp_size,
        3,
    )
    sizes = (dp_size, seq_size, mp_size)
    shard_count = dp_size * seq_size
    steps = width // row_plan(width, share, mp_size)[0]

    def to_steps(x):
        return jnp.swapaxes(x.reshape(x.shape[0], shard_count, steps, -1), 1, 2).reshape(x.shape)

    def to_shards(x):
        return jnp.swapaxes(x.reshape(x.shape[0], steps, shard_count, -1), 1, 2).reshape(x.shape)

    output, grad_gain_four, dmixed_low, hidden, gate_act, slope, down_wt = ffw(
        normed_two,
        gate_up_w,
        w_down.T,
        to_steps(resid),
        to_steps(cotangent_own),
        to_steps(gain_four),
        sizes,
        4,
    )
    output = to_shards(output)
    grad_gain_four = to_shards(grad_gain_four)

    def spread(x):
        return lax.psum_scatter(x, "seq", scatter_dimension=0, tiled=True)

    grad_down_sum = weight_grad(dmixed_low, (hidden,), 7, steps, seq_size)
    grad_down_t = spread(grad_down_sum)
    dgate_low, dup_low = hidden_back(after(dmixed_low, grad_down_sum), down_wt, gate_act, slope)
    grad_gate_up_sum = weight_grad(normed_two, (dgate_low, dup_low), 8)
    dresid, grad_gain_two, grad_gain_three, dattn_low = sum_rows(
        (after(dgate_low, grad_down_t, grad_gate_up_sum), dup_low),
        gate_up_w,
        before_ffw,
        (resid, attn, cotangent_own, gain_two, gain_three),
        ((share, F32), (8, F32), (8, F32)),
        True,
        False,
        mp_size,
        5,
    )
    grad_gate_up = spread(after(grad_gate_up_sum, grad_down_t))

    dattn_o = by_owner(dot_nn(dattn_low, w_out_t)).astype(BF16)
    dquery, dpairs = attend_back(queries, dattn_o, attn_exact, lse, pairs, plan)
    grad_out_sum = weight_grad(dattn_low, (by_owner(attn_o),), 9)
    own_grads = spread(after(dpairs, grad_gate_up, grad_out_sum)).astype(F32)
    dkey_rot = own_grads[:, :HEAD_DIM]
    dkey_low = rotary(dkey_rot, cosine[:, 0], sine[:, 0], -1.0).astype(BF16)
    dvalue_low = own_grads[:, HEAD_DIM:].astype(BF16)
    dquery = dquery.reshape(span, heads, HEAD_DIM)
    dquery_low = (
        rotary(dquery * HEAD_DIM ** (-0.5), cosine, sine, -1.0).reshape(span, q_width).astype(BF16)
    )
    dkv_low = jnp.concatenate([dkey_low, dvalue_low], axis=1)
    grad_qkv_sum = weight_grad(normed_one, (dquery_low, dkv_low), 10)
    grad_qkv = spread(grad_qkv_sum)
    tokens_grad, grad_gain_one = sum_rows(
        (dquery_low, after(dkv_low, grad_qkv_sum)),
        w_qkv,
        before_attention,
        (tokens_own, dresid, gain_one),
        ((share, BF16), (8, F32)),
        False,
        True,
        mp_size,
        6,
    )

    grad_out_t = spread(after(grad_out_sum, grad_qkv, tokens_grad))
    gain_grads, grad_key, grad_value = last_sums(
        [
            jnp.sum(grad, axis=0)
            for grad in (grad_gain_one, grad_gain_two, grad_gain_three, grad_gain_four)
        ],
        grad_qkv[:, q_width:],
        w_key.shape[1],
        heads,
        sizes,
    )
    return (
        output[None],
        tokens_grad[None],
        gain_grads[0],
        grad_qkv[:, :q_width].astype(F32),
        grad_key,
        grad_value,
        grad_out_t.astype(F32).T,
        gain_grads[1],
        gain_grads[2],
        grad_gate_up[:, :units].astype(F32),
        grad_gate_up[:, units:].astype(F32),
        grad_down_t.astype(F32).T,
        gain_grads[3],
    )


def solution(mesh):
    weight = P(("dp", "seq"), "mp")
    whole_rows = P(("dp", "seq"), None)
    columns = P("mp", ("dp", "seq"))
    gain = P(("dp", "seq"))
    tokens = P("dp", "seq", None)
    rows = P("dp", ("seq", "mp"), None)
    in_specs = (
        tokens,
        tokens,
        gain,
        weight,
        whole_rows,
        whole_rows,
        columns,
        gain,
        gain,
        weight,
        weight,
        columns,
        gain,
    )
    out_specs = (
        rows,
        rows,
        gain,
        weight,
        whole_rows,
        whole_rows,
        columns,
        gain,
        gain,
        weight,
        weight,
        columns,
        gain,
    )
    return jax.shard_map(shards, mesh=mesh, in_specs=in_specs, out_specs=out_specs, check_vma=False)
```

```python
import functools

import jax
import jax.numpy as jnp
from jax import lax
from jax.experimental import pallas as pl
from jax.experimental.pallas import tpu as pltpu
from jax.sharding import PartitionSpec as P

Q_HEADS = 8
KV_HEADS = 4
HEAD_DIM = 256
WINDOW = 4096

EPSILON = 1e-06
SOFT_CAP = 50.0
ROPE_BASE = 10000.0
GELU_SCALE = (2.0 / 3.141592653589793) ** 0.5
GELU_CUBE = 0.044715
MESH = pl.DeviceIdType.MESH
VMEM_LIMIT = 56 * 1024 * 1024
LANES = 128
BF16 = jnp.bfloat16
F32 = jnp.float32


def after(value, *earlier):
    return lax.optimization_barrier((value, *earlier))[0]


def dot_nn(left, right):
    return lax.dot_general(left, right, (((1,), (0,)), ((), ())), preferred_element_type=F32)


def dot_nt(left, right):
    return lax.dot_general(left, right, (((1,), (1,)), ((), ())), preferred_element_type=F32)


def dot_tn(left, right):
    return lax.dot_general(left, right, (((0,), (0,)), ((), ())), preferred_element_type=F32)


def rms_scale(vector):
    return lax.rsqrt(jnp.mean(vector * vector, axis=-1, keepdims=True) + EPSILON)


def rotary(vector, cosine, sine, direction):
    half_dim = vector.shape[-1] // 2
    first_half = vector[..., :half_dim]
    second_half = vector[..., half_dim:]
    return jnp.concatenate(
        [
            first_half * cosine - direction * (second_half * sine),
            second_half * cosine + direction * (first_half * sine),
        ],
        axis=-1,
    )


def gather_kernel(sizes, x_ref, o_ref, send_sem, recv_sem):
    dp_size, seq_size = sizes
    count = dp_size * seq_size
    dp, seq, mp = lax.axis_index("dp"), lax.axis_index("seq"), lax.axis_index("mp")
    rank = dp * seq_size + seq

    def peer(k):
        other = lax.rem(rank + k, count)
        return (other // seq_size, lax.rem(other, seq_size), mp)

    barrier = pltpu.get_barrier_semaphore()
    for k in range(1, count):
        pl.semaphore_signal(barrier, inc=1, device_id=peer(k), device_id_type=MESH)
    pl.semaphore_wait(barrier, count - 1)
    copies = []
    for k in range(1, count):
        copies.append(
            pltpu.make_async_remote_copy(
                src_ref=x_ref,
                dst_ref=o_ref.at[rank],
                send_sem=send_sem.at[k],
                recv_sem=recv_sem.at[k],
                device_id=peer(k),
                device_id_type=MESH,
            )
        )
        copies[-1].start()
    o_ref[pl.ds(rank, 1)] = x_ref[...][None]
    for copy in copies:
        copy.wait()


def gather_gains(gains, dp_size, seq_size):
    count = dp_size * seq_size
    local = gains[0].shape[0]
    width = -(-local // LANES) * LANES
    block = jnp.stack([gain.astype(F32) for gain in gains])
    block = jnp.pad(block, ((0, 8 - len(gains)), (0, width - local)))
    full = pl.pallas_call(
        functools.partial(gather_kernel, (dp_size, seq_size)),
        out_shape=jax.ShapeDtypeStruct((count, 8, width), F32),
        in_specs=[pl.BlockSpec(memory_space=pltpu.VMEM)],
        out_specs=pl.BlockSpec(memory_space=pltpu.VMEM),
        scratch_shapes=[
            pltpu.SemaphoreType.DMA((count,)),
            pltpu.SemaphoreType.DMA((count,)),
        ],
        compiler_params=pltpu.CompilerParams(collective_id=1, has_side_effects=True),
    )(block)
    full = jnp.transpose(full[:, : len(gains), :local], (1, 0, 2)).reshape(len(gains), -1)
    return [full[i : i + 1] for i in range(len(gains))]


def flipped(index, k):
    result, bit = index, 1
    while bit <= k:
        if k & bit:
            result = result + bit * (1 - 2 * lax.rem(index // bit, 2))
        bit *= 2
    return result


def last_kernel(sizes, heads, x_ref, kv_ref, o_ref, key_ref, value_ref, mine, from_mp, from_ws, kv_from, sems):
    dp_size, seq_size, mp_size = sizes
    count = dp_size * seq_size
    dp, seq, mp = lax.axis_index("dp"), lax.axis_index("seq"), lax.axis_index("mp")
    rank = dp * seq_size + seq

    def mp_peer(k):
        return (dp, seq, flipped(mp, k))

    def ws_rank(k):
        return lax.rem(rank + k, count)

    def ws_peer(k):
        other = ws_rank(k)
        return (other // seq_size, lax.rem(other, seq_size), mp)

    def remote(src, dst, kind, k, device):
        copy = pltpu.make_async_remote_copy(
            src_ref=src,
            dst_ref=dst,
            send_sem=sems.at[kind, 0, k],
            recv_sem=sems.at[kind, 1, k],
            device_id=device,
            device_id_type=MESH,
        )
        copy.start()
        return copy

    barrier = pltpu.get_barrier_semaphore()
    for k in range(1, mp_size):
        pl.semaphore_signal(barrier, inc=1, device_id=mp_peer(k), device_id_type=MESH)
    for k in range(1, count):
        pl.semaphore_signal(barrier, inc=1, device_id=ws_peer(k), device_id_type=MESH)
    pl.semaphore_wait(barrier, mp_size - 1 + count - 1)
    copies = [remote(x_ref, from_mp.at[k], 0, k, mp_peer(k)) for k in range(1, mp_size)]
    kv_copies = [remote(kv_ref, kv_from.at[k], 1, k, mp_peer(k)) for k in range(1, mp_size)]
    for copy in copies:
        copy.wait()
    total = x_ref[...]
    for k in range(1, mp_size):
        total = total + from_mp[k]
    mine[...] = total
    copies = [remote(mine.at[ws_rank(k)], from_ws.at[k], 2, k, ws_peer(k)) for k in range(1, count)]
    key_ref[...] = jnp.zeros_like(key_ref)
    value_ref[...] = jnp.zeros_like(value_ref)
    for k in range(mp_size):
        if k:
            kv_copies[k - 1].wait()
        piece = (kv_from[k] if k else kv_ref[...]).astype(F32)
        head = flipped(mp, k) * heads // (Q_HEADS // KV_HEADS)
        columns = pl.ds(pl.multiple_of(head * HEAD_DIM, HEAD_DIM), HEAD_DIM)
        key_ref[:, columns] += piece[:, :HEAD_DIM]
        value_ref[:, columns] += piece[:, HEAD_DIM:]
    for copy in copies:
        copy.wait()
    own = mine[pl.ds(rank, 1)][0]
    for k in range(1, count):
        own = own + from_ws[k]
    o_ref[...] = own


def last_sums(grads, kv, kv_width, heads, sizes):
    dp_size, seq_size, mp_size = sizes
    count = dp_size * seq_size
    local = grads[0].shape[0] // count
    width = -(-local // LANES) * LANES
    block = jnp.transpose(jnp.stack(grads).reshape(len(grads), count, local), (1, 0, 2))
    block = jnp.pad(block, ((0, 0), (0, 8 - len(grads)), (0, width - local)))
    kv_out = jax.ShapeDtypeStruct((kv.shape[0], kv_width), F32)
    total, key, value = pl.pallas_call(
        functools.partial(last_kernel, sizes, heads),
        out_shape=(jax.ShapeDtypeStruct((8, width), F32), kv_out, kv_out),
        in_specs=[pl.BlockSpec(memory_space=pltpu.VMEM)] * 2,
        out_specs=(pl.BlockSpec(memory_space=pltpu.VMEM),) * 3,
        scratch_shapes=[
            pltpu.VMEM((count, 8, width), F32),
            pltpu.VMEM((mp_size, count, 8, width), F32),
            pltpu.VMEM((count, 8, width), F32),
            pltpu.VMEM((mp_size, *kv.shape), BF16),
            pltpu.SemaphoreType.DMA((3, 2, max(count, mp_size))),
        ],
        compiler_params=pltpu.CompilerParams(
            collective_id=2, has_side_effects=True, vmem_limit_bytes=VMEM_LIMIT
        ),
    )(block, kv)
    return [total[i, :local] for i in range(len(grads))], key, value


def key_mask(shape, first_key, first_query, tile, far):
    key = first_key + lax.broadcasted_iota(jnp.int32, shape, 0)
    query = first_query + lax.rem(lax.broadcasted_iota(jnp.int32, shape, 1), tile)
    return key > query if far else key <= query


def for_key_tiles(tile_fn, index, tile, span, step, hops, windowed):
    seq = lax.axis_index("seq")
    per_block = span // step
    last = jnp.minimum(seq, hops)
    if windowed:
        @pl.when(seq >= hops)
        def _():
            tile_fn(pl.multiple_of((seq - hops) * span, span), span, "far")

        last = jnp.minimum(seq, hops - 1)

    def past(t, carry):
        tile_fn(pl.multiple_of(t * step, step), step, "")
        return carry

    lax.fori_loop((seq - last) * per_block, seq * per_block, past, 0)
    tile_fn(pl.multiple_of(seq * span, span), (index + 1) * tile, "near")


def head_rows(ref, index, tile):
    block = ref[pl.ds(index * tile, tile), :]
    return jnp.concatenate(
        [block[:, h * HEAD_DIM : (h + 1) * HEAD_DIM] for h in range(ref.shape[1] // HEAD_DIM)], axis=0
    )


def put_head_rows(ref, index, tile, rows):
    for h in range(ref.shape[1] // HEAD_DIM):
        ref[pl.ds(index * tile, tile), h * HEAD_DIM : (h + 1) * HEAD_DIM] = rows[
            h * tile : (h + 1) * tile
        ].astype(ref.dtype)


def attend_kernel(plan, q_ref, kv_ref, o_ref, of_ref, lse_ref, acc, total):
    tile, span, step, hops, windowed = plan
    for i in range(span // tile):
        query = head_rows(q_ref, i, tile)
        rows = query.shape[0]
        acc[...] = jnp.zeros_like(acc)
        total[...] = jnp.zeros_like(total)

        def tile_fn(first, count, mask, i=i, query=query, rows=rows):
            key = kv_ref[pl.ds(first, count), :HEAD_DIM]
            value = kv_ref[pl.ds(first, count), HEAD_DIM:]
            raw = dot_nt(key, query)
            weight = jnp.exp(SOFT_CAP * jnp.tanh(raw * (1.0 / SOFT_CAP)))
            if mask:
                inside = key_mask(weight.shape, 0, i * tile, tile, mask == "far")
                weight = jnp.where(inside, weight, 0.0)
            total[...] += jnp.sum(weight.reshape(count // 8, 8, rows), axis=0)
            acc[...] += dot_tn(value, weight.astype(BF16))

        for_key_tiles(tile_fn, i, tile, span, step, hops, windowed)
        row_total = jnp.sum(total[...], axis=0, keepdims=True)
        out = (acc[...] / row_total).T
        put_head_rows(o_ref, i, tile, out)
        put_head_rows(of_ref, i, tile, out)
        lse_ref[i] = jnp.log(row_total)


def attend_back_kernel(plan, q_ref, do_ref, of_ref, lse_ref, kv_ref, dq_ref, dkv_ref, grads, acc):
    tile, span, step, hops, windowed = plan
    grads[...] = jnp.zeros_like(grads)
    for i in range(span // tile):
        query = head_rows(q_ref, i, tile)
        dout = head_rows(do_ref, i, tile)
        lse = lse_ref[i]
        delta = jnp.sum(dout.astype(F32) * head_rows(of_ref, i, tile), axis=-1, keepdims=True)
        delta = jnp.broadcast_to(delta, (delta.shape[0], LANES)).T[:1]
        acc[...] = jnp.zeros_like(acc)

        def tile_fn(first, count, mask, i=i, query=query, dout=dout, lse=lse, delta=delta):
            key = kv_ref[pl.ds(first, count), :HEAD_DIM]
            value = kv_ref[pl.ds(first, count), HEAD_DIM:]
            bounded = jnp.tanh(dot_nt(key, query) * (1.0 / SOFT_CAP))
            prob = jnp.exp(SOFT_CAP * bounded - lse)
            if mask:
                inside = key_mask(prob.shape, 0, i * tile, tile, mask == "far")
                prob = jnp.where(inside, prob, 0.0)
            dprob = dot_nt(value, dout)
            draw = (prob * (dprob - delta) * (1.0 - bounded * bounded)).astype(BF16)
            grads[pl.ds(first, count), HEAD_DIM:] += dot_nn(prob.astype(BF16), dout)
            grads[pl.ds(first, count), :HEAD_DIM] += dot_nn(draw, query)
            acc[...] += dot_tn(key, draw)

        for_key_tiles(tile_fn, i, tile, span, step, hops, windowed)
        put_head_rows(dq_ref, i, tile, acc[...].T)
    dkv_ref[...] = grads[...].astype(BF16)


def attention_plan(span, seq_size):
    hops = min(WINDOW // span, seq_size - 1)
    return (min(256, span), span, min(512, span), hops, seq_size * span > WINDOW)


def attend(queries, pairs, plan):
    tile, span = plan[:2]
    heads = queries.shape[1] // HEAD_DIM
    rows = heads * tile
    return pl.pallas_call(
        functools.partial(attend_kernel, plan),
        out_shape=(
            jax.ShapeDtypeStruct(queries.shape, BF16),
            jax.ShapeDtypeStruct(queries.shape, F32),
            jax.ShapeDtypeStruct((span // tile, 1, rows), F32),
        ),
        in_specs=[pl.BlockSpec(memory_space=pltpu.VMEM)] * 2,
        out_specs=(pl.BlockSpec(memory_space=pltpu.VMEM),) * 3,
        scratch_shapes=[pltpu.VMEM((HEAD_DIM, rows), F32), pltpu.VMEM((8, rows), F32)],
        compiler_params=pltpu.CompilerParams(vmem_limit_bytes=VMEM_LIMIT),
        cost_estimate=pl.CostEstimate(
            flops=12 * queries.size * span, bytes_accessed=8 * queries.size, transcendentals=0
        ),
    )(queries, pairs)


def attend_back(queries, dout, exact, lse, pairs, plan):
    tile, span = plan[:2]
    rows = queries.shape[1] // HEAD_DIM * tile
    return pl.pallas_call(
        functools.partial(attend_back_kernel, plan),
        out_shape=(
            jax.ShapeDtypeStruct(queries.shape, F32),
            jax.ShapeDtypeStruct(pairs.shape, BF16),
        ),
        in_specs=[pl.BlockSpec(memory_space=pltpu.VMEM)] * 5,
        out_specs=(pl.BlockSpec(memory_space=pltpu.VMEM),) * 2,
        scratch_shapes=[pltpu.VMEM(pairs.shape, F32), pltpu.VMEM((HEAD_DIM, rows), F32)],
        compiler_params=pltpu.CompilerParams(vmem_limit_bytes=VMEM_LIMIT),
        cost_estimate=pl.CostEstimate(
            flops=30 * queries.size * span, bytes_accessed=8 * queries.size, transcendentals=0
        ),
    )(queries, dout, exact, lse, pairs)


def remote_copy(src, dst, sems, index, device):
    copy = pltpu.make_async_remote_copy(
        src_ref=src,
        dst_ref=dst,
        send_sem=sems.at[(0, *index)],
        recv_sem=sems.at[(1, *index)],
        device_id=device,
        device_id_type=MESH,
    )
    copy.start()
    return copy


def sum_direct(parts_at, steps, step, mp_size, peer, total, sent, arrived, sems):
    copies = []
    for t in range(steps):
        for k in range(mp_size - 1, -1, -1):
            part = parts_at(t, k)
            if k == 0:
                total[:, t * step : (t + 1) * step] = part
            else:
                sent[t, k - 1] = part.astype(BF16)
                copies.append(
                    remote_copy(sent.at[t, k - 1], arrived.at[t, k - 1], sems, (t, k - 1), peer(k))
                )
    for t in range(steps):
        for k in range(1, mp_size):
            copies[t * (mp_size - 1) + mp_size - 1 - k].wait_recv()
            total[:, t * step : (t + 1) * step] += arrived[t, k - 1].astype(F32)
    return copies


def sum_square(parts_at, steps, step, peer, total, kept, sent, arrived, sems):
    half = step // 2
    copies, second = [], []

    def second_hop(t):
        copies[2 * t].wait_recv()
        sent[t, 1, 2] = (kept[t, 1] + arrived[t, 0, 1].astype(F32)).astype(BF16)
        second.append(remote_copy(sent.at[t, 1, 2], arrived.at[t, 1, 2], sems, (t, 2), peer(2)))
        copies[2 * t + 1].wait_recv()
        sent[t, 0, 2] = (kept[t, 0] + arrived[t, 1, 1].astype(F32)).astype(BF16)
        second.append(remote_copy(sent.at[t, 0, 2], arrived.at[t, 0, 2], sems, (t, 3), peer(1)))

    for t in range(steps):
        first = t * step
        far = parts_at(t, 3)
        sent[t, 0, 1] = far[:, :half].astype(BF16)
        sent[t, 1, 1] = far[:, half:].astype(BF16)
        part = parts_at(t, 1)
        sent[t, 0, 0] = part[:, :half].astype(BF16)
        kept[t, 0] = part[:, half:]
        copies.append(
            remote_copy(sent.at[t, 0, pl.ds(0, 2)], arrived.at[t, 0, pl.ds(0, 2)], sems, (t, 0), peer(1))
        )
        part = parts_at(t, 2)
        sent[t, 1, 0] = part[:, half:].astype(BF16)
        kept[t, 1] = part[:, :half]
        copies.append(
            remote_copy(sent.at[t, 1, pl.ds(0, 2)], arrived.at[t, 1, pl.ds(0, 2)], sems, (t, 1), peer(2))
        )
        total[:, first : first + step] = parts_at(t, 0)
    for t in range(steps):
        second_hop(t)
    for t in range(steps):
        first = t * step
        second[2 * t].wait_recv()
        total[:, first : first + half] += arrived[t, 0, 0].astype(F32) + arrived[t, 1, 2].astype(F32)
        second[2 * t + 1].wait_recv()
        total[:, first + half : first + step] += arrived[t, 1, 0].astype(F32) + arrived[t, 0, 2].astype(
            F32
        )
    return copies + second


def row_gather(own, gathered, mp_size, peer, sems):
    share = own.shape[0]
    if mp_size != 4:
        copies = [
            remote_copy(own, gathered.at[pl.ds(k * share, share)], sems, (k,), peer(k))
            for k in range(mp_size - 1, 0, -1)
        ]

        def finish():
            for copy in copies:
                copy.wait()

        return lambda: None, finish

    half = share // 2

    def place(k, lower):
        return gathered.at[pl.ds(k * share + lower * half, half)]

    upper, lower = own.at[pl.ds(0, half)], own.at[pl.ds(half, half)]
    to_one = remote_copy(upper, place(1, 0), sems, (0,), peer(1))
    to_two = remote_copy(lower, place(2, 1), sems, (1,), peer(2))
    copies = [
        remote_copy(upper, place(2, 0), sems, (2,), peer(2)),
        remote_copy(lower, place(1, 1), sems, (3,), peer(1)),
    ]

    def pass_on():
        to_one.wait_recv()
        copies.append(remote_copy(place(1, 0), place(3, 0), sems, (4,), peer(2)))
        to_two.wait_recv()
        copies.append(remote_copy(place(2, 1), place(3, 1), sems, (5,), peer(1)))

    def finish():
        to_one.wait_send()
        to_two.wait_send()
        for copy in copies:
            copy.wait()

    return pass_on, finish


def rows_kernel(plan, rows_fn, *refs):
    mp_size, share, step, row_step, natural, n_left, n_aux, n_out, gather = plan
    lefts, weight_ref, refs = refs[:n_left], refs[n_left], refs[n_left + 1 :]
    aux, refs = refs[:n_aux], refs[n_aux:]
    outs, refs = refs[:n_out], refs[n_out:]
    if gather:
        gathered, refs = refs[0], refs[1:]
    left, weight, total, own, kept, sent, arrived, in_sem, sum_sem, row_sem = refs
    steps = total.shape[1] // step
    dp, seq, mp = lax.axis_index("dp"), lax.axis_index("seq"), lax.axis_index("mp")

    def peer(k):
        return (dp, seq, flipped(mp, k))

    left_copies, weight_copies = {}, []
    for k in range(mp_size):
        first = (flipped(mp, k) if natural else k) * share
        left_copies[k] = []
        column = 0
        for i, ref in enumerate(lefts):
            depth = ref.shape[1]
            left_copies[k].append(
                pltpu.make_async_copy(
                    ref.at[pl.ds(first, share)],
                    left.at[k, :, pl.ds(column, depth)],
                    in_sem.at[2 + k * n_left + i],
                )
            )
            column += depth
    for t in range(steps):
        weight_copies.append(
            pltpu.make_async_copy(
                weight_ref.at[pl.ds(t * step, step)], weight.at[t % 2], in_sem.at[t % 2]
            )
        )
    weight_copies[0].start()
    for k in range(mp_size - 1, -1, -1):
        for copy in left_copies[k]:
            copy.start()

    barrier = pltpu.get_barrier_semaphore()
    for k in range(1, mp_size):
        pl.semaphore_signal(barrier, inc=1, device_id=peer(k), device_id_type=MESH)
    pl.semaphore_wait(barrier, mp_size - 1)

    def parts_at(t, k):
        if k == mp_size - 1:
            weight_copies[t].wait()
            if t + 1 < steps:
                weight_copies[t + 1].start()
        if t == 0:
            for copy in left_copies[k]:
                copy.wait()
        return dot_nt(left[k], weight[t % 2])

    finish_rows(
        parts_at,
        (mp_size, share, step, row_step),
        (rows_fn, aux, outs, gathered if gather else None),
        peer,
        (total, own, kept, sent, arrived),
        (sum_sem, row_sem, in_sem.at[0]),
    )


def finish_rows(parts_at, sizes, rows, peer, buffers, sems):
    mp_size, share, step, row_step = sizes
    rows_fn, aux, outs, gathered = rows
    total, own, kept, sent, arrived = buffers
    sum_sem, row_sem, keep_sem = sems
    steps = total.shape[1] // step
    if mp_size == 4:
        sums = sum_square(parts_at, steps, step, peer, total, kept, sent, arrived, sum_sem)
    else:
        sums = sum_direct(parts_at, steps, step, mp_size, peer, total, sent, arrived, sum_sem)

    def rows_at(r, carry):
        rows = pl.ds(pl.multiple_of(r * row_step, row_step), row_step)
        result = rows_fn(total[rows, :], rows, aux, outs)
        if gathered is not None:
            result = result.astype(BF16)
            if len(own.shape) == 2:
                own[rows, :] = result
            else:
                for t in range(steps):
                    own[t, rows, :] = result[:, t * step : (t + 1) * step]
        return carry

    for ref in outs:
        if ref.shape[0] == 8:
            ref[...] = jnp.zeros_like(ref)
    lax.fori_loop(0, share // row_step, rows_at, 0)
    if gathered is not None:
        first = own if len(own.shape) == 2 else own.at[0]
        keep = pltpu.make_async_copy(first, gathered.at[pl.ds(0, share)], keep_sem)
        keep.start()
        pass_on, finish = row_gather(first, gathered, mp_size, peer, row_sem)
        pass_on()
        finish()
        keep.wait()
    for copy in sums:
        copy.wait_send()


def row_plan(width, share, mp_size):
    step = 768 if width % 768 == 0 else width
    steps = width // step
    if mp_size == 4:
        pieces, kept = (steps, 2, 3, share, step // 2), (steps, 2, share, step // 2)
    else:
        pieces, kept = (steps, mp_size - 1, share, step), (8, LANES)
    buffers = [
        pltpu.VMEM((share, width), F32),
        pltpu.VMEM((share, width), BF16),
        pltpu.VMEM(kept, F32),
        pltpu.VMEM(pieces, BF16),
        pltpu.VMEM(pieces, BF16),
    ]
    sems = [
        pltpu.SemaphoreType.DMA((2, steps, max(4, mp_size - 1))),
        pltpu.SemaphoreType.DMA((2, max(6, mp_size))),
    ]
    return step, min(32, share), buffers, sems


def sum_rows(lefts, weight, rows_fn, aux, outs, gather, natural, mp_size, collective_id):
    span = lefts[0].shape[0]
    width, depth = weight.shape
    share = span // mp_size
    step, row_step, buffers, sems = row_plan(width, share, mp_size)
    plan = (mp_size, share, step, row_step, natural, len(lefts), len(aux), len(outs), gather)
    out_shape = [jax.ShapeDtypeStruct((rows, width), dtype) for rows, dtype in outs]
    out_specs = [pl.BlockSpec(memory_space=pltpu.VMEM)] * len(outs)
    if gather:
        out_shape.append(jax.ShapeDtypeStruct((span, width), BF16))
        out_specs.append(pl.BlockSpec(memory_space=pl.ANY))
    return pl.pallas_call(
        functools.partial(rows_kernel, plan, rows_fn),
        out_shape=out_shape,
        in_specs=[pl.BlockSpec(memory_space=pl.ANY)] * (len(lefts) + 1)
        + [pl.BlockSpec(memory_space=pltpu.VMEM)] * len(aux),
        out_specs=out_specs,
        scratch_shapes=[
            pltpu.VMEM((mp_size, share, depth), BF16),
            pltpu.VMEM((2, step, depth), BF16),
            *buffers,
            pltpu.SemaphoreType.DMA((2 + mp_size * len(lefts),)),
            *sems,
        ],
        compiler_params=pltpu.CompilerParams(
            collective_id=collective_id, has_side_effects=True, vmem_limit_bytes=VMEM_LIMIT
        ),
    )(*lefts, weight, *aux)


def weight_grad_kernel(plan, *refs):
    n_right, tile, half, first_column, n_into, next_step, mp_size = plan
    left_ref, rights, refs = refs[0], refs[1 : 1 + n_right], refs[1 + n_right + n_into :]
    if next_step:
        steps_ref, out_ref, gathered, refs = refs[0], refs[1], refs[2], refs[3:]
        own_rows, row_sem, refs = refs[0], refs[1], refs[2:]
    else:
        out_ref, refs = refs[0], refs[1:]
    left, right, sent, arrived, own, result, in_sem, swap_sem, out_sem = refs
    dp, seq, mp = lax.axis_index("dp"), lax.axis_index("seq"), lax.axis_index("mp")
    other = (1 - dp, seq, mp)

    def peer(k):
        return (dp, seq, flipped(mp, k))

    if next_step:
        rows_load = pltpu.make_async_copy(steps_ref.at[next_step], own_rows, in_sem.at[4])
        rows_load.start()
    lefts = []
    for i, side in enumerate((1 - dp, dp)):
        columns = pl.ds(pl.multiple_of(side * half, LANES), half)
        lefts.append(pltpu.make_async_copy(left_ref.at[:, columns], left.at[i], in_sem.at[2 + i]))
        lefts[i].start()
    sources = []
    for ref in rights:
        for first in range(0, ref.shape[1], tile):
            sources.append(ref.at[:, pl.ds(first, tile)])
    tiles = len(sources)
    loads = [
        pltpu.make_async_copy(source, right.at[t % 2], in_sem.at[t % 2])
        for t, source in enumerate(sources)
    ]
    loads[0].start()
    barrier = pltpu.get_barrier_semaphore()
    pl.semaphore_signal(barrier, inc=1, device_id=other, device_id_type=MESH)
    if next_step:
        for k in range(1, mp_size):
            pl.semaphore_signal(barrier, inc=1, device_id=peer(k), device_id_type=MESH)
    pl.semaphore_wait(barrier, mp_size if next_step else 1)
    if next_step:
        rows_load.wait()
        share = own_rows.shape[0]
        keep = pltpu.make_async_copy(own_rows, gathered.at[pl.ds(0, share)], in_sem.at[4])
        keep.start()
        pass_on, end_rows = row_gather(own_rows, gathered, mp_size, peer, row_sem)
    swaps, stores = [], []

    def finish(t):
        swaps[t].wait_recv()
        if t >= 2:
            stores[t - 2].wait()
        result[t % 2] = (own[t % 2] + arrived[t].astype(F32)).astype(BF16)
        stores.append(
            pltpu.make_async_copy(
                result.at[t % 2],
                out_ref.at[:, pl.ds(first_column + t * tile, tile)],
                out_sem.at[t % 2],
            )
        )
        stores[t].start()

    for t in range(tiles):
        loads[t].wait()
        if t + 1 < tiles:
            loads[t + 1].start()
        if t == 0:
            lefts[0].wait()
        sent[t] = dot_tn(left[0], right[t % 2]).astype(BF16)
        swaps.append(remote_copy(sent.at[t], arrived.at[t], swap_sem, (t,), other))
        if t == 0:
            lefts[1].wait()
        own[t % 2] = dot_tn(left[1], right[t % 2])
        if t >= 1:
            finish(t - 1)
        if t == tiles // 2 and next_step:
            pass_on()
    finish(tiles - 1)
    for store in stores[-2:]:
        store.wait()
    for swap in swaps:
        swap.wait_send()
    if next_step:
        keep.wait()
        end_rows()


def weight_grad(left, rights, collective_id, into=None, columns=0, steps=None, next_step=0, mp_size=1):
    rows, width = left.shape
    half = width // 2
    total = sum(right.shape[1] for right in rights)
    tile = next(
        t
        for t in (768, 512, 384, 256, LANES)
        if total >= 2 * t and all(right.shape[1] % t == 0 for right in rights)
    )
    tiles = total // tile
    first = 0 if into is None else into.shape[1] - total
    earlier = () if into is None else (into,)
    out_shape = [jax.ShapeDtypeStruct((half, first + total + columns), BF16)]
    scratch = []
    if next_step:
        earlier = (steps,)
        out_shape.append(jax.ShapeDtypeStruct((steps.shape[1] * mp_size, steps.shape[2]), BF16))
        scratch = [
            pltpu.VMEM(steps.shape[1:], BF16),
            pltpu.SemaphoreType.DMA((2, max(6, mp_size))),
        ]
    plan = (len(rights), tile, half, first, 0 if into is None else 1, next_step, mp_size)
    results = pl.pallas_call(
        functools.partial(weight_grad_kernel, plan),
        out_shape=out_shape,
        in_specs=[pl.BlockSpec(memory_space=pl.ANY)] * (1 + len(rights) + len(earlier)),
        out_specs=[pl.BlockSpec(memory_space=pl.ANY)] * len(out_shape),
        input_output_aliases={} if into is None else {1 + len(rights): 0},
        scratch_shapes=[
            *scratch,
            pltpu.VMEM((2, rows, half), BF16),
            pltpu.VMEM((2, rows, tile), BF16),
            pltpu.VMEM((tiles, half, tile), BF16),
            pltpu.VMEM((tiles, half, tile), BF16),
            pltpu.VMEM((2, half, tile), F32),
            pltpu.VMEM((2, half, tile), BF16),
            pltpu.SemaphoreType.DMA((5,)),
            pltpu.SemaphoreType.DMA((2, tiles)),
            pltpu.SemaphoreType.DMA((2,)),
        ],
        compiler_params=pltpu.CompilerParams(
            collective_id=collective_id, has_side_effects=True, vmem_limit_bytes=VMEM_LIMIT
        ),
    )(left, *rights, *earlier)
    return results if next_step else results[0]


def ffw_kernel(plan, normed_ref, gate_up_ref, shard_ref, resid_ref, cotangent_ref, gain_ref, *refs):
    mp_size, seq_size, share, step, row_step, tile = plan
    output_ref, gain_grad_ref, own_ref, dmixed_ref, hidden_ref, act_ref, slope_ref, down_ref = refs[:8]
    normed, gate_up, hidden, down, staged, *refs = refs[8:]
    buffers, refs = refs[:5], refs[5:]
    load_sem, store_sem, local_sem, line_sem, pair_sem, sum_sem, row_sem = refs
    steps, _, units = down.shape
    piece = step // (2 * seq_size)
    far = seq_size - 1
    dp, seq, mp = lax.axis_index("dp"), lax.axis_index("seq"), lax.axis_index("mp")
    sibling = (1 - dp, seq, mp)

    def peer(k):
        return (dp, seq, flipped(mp, k))

    def along(way):
        return (dp, seq + 1 - 2 * way, mp)

    def goes_on(way):
        return seq < far if way == 0 else seq > 0

    def comes(way, distance):
        return seq >= distance if way == 0 else seq + distance <= far

    def block(t, at):
        first = pl.multiple_of((dp * seq_size + at) * piece, piece)
        return down.at[t, pl.ds(first, piece)]

    def line(t, way, distance):
        at = seq - distance if way == 0 else seq + distance
        return pltpu.make_async_remote_copy(
            src_ref=block(t, at),
            dst_ref=block(t, at),
            send_sem=line_sem.at[0, t, way, distance],
            recv_sem=line_sem.at[1, t, way, distance],
            device_id=along(way),
            device_id_type=MESH,
        )

    def pair(t, way, distance):
        at = seq - distance if way == 0 else seq + distance
        return pltpu.make_async_remote_copy(
            src_ref=block(t, at),
            dst_ref=block(t, at),
            send_sem=pair_sem.at[0, t, way, distance],
            recv_sem=pair_sem.at[1, t, way, distance],
            device_id=sibling,
            device_id_type=MESH,
        )

    normed_load = pltpu.make_async_copy(normed_ref, normed, local_sem.at[0])
    normed_load.start()
    shard_loads = [
        pltpu.make_async_copy(
            shard_ref.at[pl.ds(t * piece, piece)], block(t, seq), local_sem.at[1 + t]
        )
        for t in range(steps)
    ]
    for load in shard_loads:
        load.start()

    def loads(i, slot):
        return [
            pltpu.make_async_copy(
                gate_up_ref.at[:, pl.ds(pl.multiple_of(side * units + i * tile, LANES), tile)],
                gate_up.at[slot, side],
                load_sem.at[slot, side],
            )
            for side in range(2)
        ]

    def stores(i, slot):
        columns = pl.ds(pl.multiple_of(i * tile, LANES), tile)
        return [
            pltpu.make_async_copy(staged.at[slot, 0], act_ref.at[:, columns], store_sem.at[slot, 0]),
            pltpu.make_async_copy(staged.at[slot, 1], slope_ref.at[:, columns], store_sem.at[slot, 1]),
        ]

    for load in loads(0, 0):
        load.start()
    barrier = pltpu.get_barrier_semaphore()
    for k in range(1, mp_size):
        pl.semaphore_signal(barrier, inc=1, device_id=peer(k), device_id_type=MESH)
    pl.semaphore_signal(barrier, inc=1, device_id=sibling, device_id_type=MESH)
    for way in range(2):
        @pl.when(goes_on(way))
        def _(way=way):
            pl.semaphore_signal(barrier, inc=1, device_id=along(way), device_id_type=MESH)

    line_peers = (seq + far) // seq_size + (2 * far - seq) // seq_size
    pl.semaphore_wait(barrier, mp_size + line_peers)

    for t in range(steps):
        shard_loads[t].wait()
        for way in range(2):
            @pl.when(goes_on(way))
            def _(t=t, way=way):
                line(t, way, 0).start()
    for t in range(steps):
        pair(t, 0, 0).start()
    normed_load.wait()

    def arrival(t, distance):
        for way in range(2):
            @pl.when(comes(way, distance))
            def _(way=way):
                line(t, way, distance - 1).wait_recv()
                if distance < far:
                    @pl.when(goes_on(way))
                    def _():
                        line(t, way, distance).start()

                pair(t, way, distance).start()

    arrivals = [(t, distance) for distance in range(1, seq_size) for t in range(steps)]
    tiles = units // tile
    early = [(2 * n + 2, event) for n, event in enumerate(arrivals) if 2 * n + 2 < tiles]
    late = arrivals[len(early) :]

    def units_at(i, carry):
        slot = lax.rem(i, 2)
        for load in loads(i, slot):
            load.wait()

        @pl.when(i + 1 < tiles)
        def _():
            for load in loads(i + 1, 1 - slot):
                load.start()

        @pl.when(i >= 2)
        def _():
            for store in stores(i - 2, slot):
                store.wait()

        gate = dot_nn(normed[...], gate_up[slot, 0])
        up = dot_nn(normed[...], gate_up[slot, 1])
        squared = gate * gate
        bend = jnp.tanh(GELU_SCALE * gate * (1.0 + GELU_CUBE * squared))
        side = 0.5 * (1.0 + bend)
        act = gate * side
        slope = side + (0.5 * GELU_SCALE) * gate * (1.0 - bend * bend) * (1.0 + 3.0 * GELU_CUBE * squared)
        staged[slot, 0] = act.astype(BF16)
        staged[slot, 1] = (slope * up).astype(BF16)
        for store in stores(i, slot):
            store.start()
        product = (act * up).astype(BF16)
        for k in range(mp_size):
            hidden[k, :, pl.ds(pl.multiple_of(i * tile, LANES), tile)] = product[
                k * share : (k + 1) * share
            ]
        for at, event in early:
            @pl.when(i == at)
            def _(event=event):
                arrival(*event)

        return carry

    lax.fori_loop(0, tiles, units_at, 0)
    for i in range(max(0, tiles - 2), tiles):
        for store in stores(i, i % 2):
            store.wait()
    hidden_stores = [
        pltpu.make_async_copy(hidden.at[k], hidden_ref.at[pl.ds(k * share, share)], local_sem.at[1 + k])
        for k in range(mp_size)
    ]
    for store in hidden_stores:
        store.start()
    down_stores = [
        pltpu.make_async_copy(
            down.at[t], down_ref.at[pl.ds(t * step, step)], local_sem.at[1 + mp_size + t]
        )
        for t in range(steps)
    ]
    waiting = list(late)

    def parts_at(t, k):
        if k == mp_size - 1:
            while (t, far) in waiting:
                arrival(*waiting.pop(0))
            pair(t, 0, 0).wait_recv()
            for way in range(2):
                for distance in range(1, seq_size):
                    @pl.when(comes(way, distance))
                    def _(way=way, distance=distance):
                        pair(t, way, distance).wait_recv()

            down_stores[t].start()
        return dot_nt(hidden[k], down[t])

    finish_rows(
        parts_at,
        (mp_size, share, step, row_step),
        (after_ffw, (resid_ref, cotangent_ref, gain_ref), (output_ref, gain_grad_ref), dmixed_ref),
        peer,
        buffers,
        (sum_sem, row_sem, local_sem.at[0]),
    )
    own_store = pltpu.make_async_copy(buffers[1], own_ref, local_sem.at[0])
    own_store.start()
    for store in hidden_stores + down_stores:
        store.wait()
    own_store.wait()
    for t in range(steps):
        pair(t, 0, 0).wait_send()
        for way in range(2):
            for distance in range(seq_size - 1):
                @pl.when(goes_on(way) & comes(way, distance))
                def _(t=t, way=way, distance=distance):
                    line(t, way, distance).wait_send()

            for distance in range(1, seq_size):
                @pl.when(comes(way, distance))
                def _(t=t, way=way, distance=distance):
                    pair(t, way, distance).wait_send()


def ffw(normed, gate_up_w, down_shard, resid, cotangent, gain, sizes, collective_id):
    dp_size, seq_size, mp_size = sizes
    span, width = normed.shape
    units = gate_up_w.shape[1] // 2
    share = span // mp_size
    step, row_step, buffers, sems = row_plan(width, share, mp_size)
    steps = width // step
    buffers[1] = pltpu.VMEM((steps, share, step), BF16)
    tile = 256 if units % 256 == 0 else LANES
    plan = (mp_size, seq_size, share, step, row_step, tile)
    per_unit = jax.ShapeDtypeStruct((span, units), BF16)
    return pl.pallas_call(
        functools.partial(ffw_kernel, plan),
        out_shape=(
            jax.ShapeDtypeStruct((share, width), BF16),
            jax.ShapeDtypeStruct((8, width), F32),
            jax.ShapeDtypeStruct((steps, share, step), BF16),
            jax.ShapeDtypeStruct((span, step), BF16),
            per_unit,
            per_unit,
            per_unit,
            jax.ShapeDtypeStruct((width, units), BF16),
        ),
        in_specs=[pl.BlockSpec(memory_space=pl.ANY)] * 3 + [pl.BlockSpec(memory_space=pltpu.VMEM)] * 3,
        out_specs=(pl.BlockSpec(memory_space=pltpu.VMEM),) * 2 + (pl.BlockSpec(memory_space=pl.ANY),) * 6,
        scratch_shapes=[
            pltpu.VMEM((span, width), BF16),
            pltpu.VMEM((2, 2, width, tile), BF16),
            pltpu.VMEM((mp_size, share, units), BF16),
            pltpu.VMEM((steps, step, units), BF16),
            pltpu.VMEM((2, 2, span, tile), BF16),
            *buffers,
            pltpu.SemaphoreType.DMA((2, 2)),
            pltpu.SemaphoreType.DMA((2, 2)),
            pltpu.SemaphoreType.DMA((1 + mp_size + steps,)),
            pltpu.SemaphoreType.DMA((2, steps, 2, seq_size)),
            pltpu.SemaphoreType.DMA((2, steps, 2, seq_size)),
            *sems,
        ],
        compiler_params=pltpu.CompilerParams(
            collective_id=collective_id, has_side_effects=True, vmem_limit_bytes=VMEM_LIMIT
        ),
    )(normed, gate_up_w, down_shard, resid, cotangent, gain)


def hidden_back_kernel(n_parts, *refs):
    parts, (down_ref, act_ref, slope_ref, dgate_ref, dup_ref) = refs[:n_parts], refs[n_parts:]
    first, dhidden = 0, 0.0
    for part in parts:
        depth = part.shape[1]
        dhidden = dhidden + dot_nn(part[...], down_ref[first : first + depth, :])
        first += depth
    dgate_ref[...] = (dhidden * slope_ref[...].astype(F32)).astype(BF16)
    dup_ref[...] = (dhidden * act_ref[...].astype(F32)).astype(BF16)


def hidden_back(dmixed, down_wt, act, slope):
    rows, depth = dmixed[0].shape
    width, units = down_wt.shape
    tile = 256 if units % 256 == 0 else units
    columns = pl.BlockSpec((rows, tile), lambda i: (0, i))
    return pl.pallas_call(
        functools.partial(hidden_back_kernel, len(dmixed)),
        grid=(units // tile,),
        out_shape=(jax.ShapeDtypeStruct((rows, units), BF16),) * 2,
        in_specs=[pl.BlockSpec((rows, depth), lambda i: (0, 0))] * len(dmixed)
        + [pl.BlockSpec((width, tile), lambda i: (0, i)), columns, columns],
        out_specs=(columns, columns),
        compiler_params=pltpu.CompilerParams(vmem_limit_bytes=VMEM_LIMIT),
    )(*dmixed, down_wt, act, slope)


def fold_rows(x):
    return jnp.sum(x.reshape(x.shape[0] // 8, 8, x.shape[1]), axis=0)


def after_attention(attn, rows, aux, outs):
    tokens, gain_two, gain_three = aux
    attn_out, resid_out = outs
    resid = tokens[rows, :].astype(F32) + attn * rms_scale(attn) * gain_two[...]
    attn_out[rows, :] = attn
    resid_out[rows, :] = resid
    return resid * rms_scale(resid) * gain_three[...]


def after_ffw(mixed, rows, aux, outs):
    resid, cotangent, gain_four = aux
    output, gain_grad = outs
    scale = rms_scale(mixed)
    unit = mixed * scale
    grad_out = cotangent[rows, :].astype(F32)
    output[rows, :] = (resid[rows, :] + unit * gain_four[...]).astype(BF16)
    gain_grad[...] += fold_rows(grad_out * unit)
    return vector_back(grad_out, unit, scale, gain_four[...])


def vector_back(grad_in, unit, scale, gain):
    unit_grad = grad_in * gain
    return scale * (unit_grad - unit * jnp.mean(unit_grad * unit, axis=-1, keepdims=True))


def before_ffw(dnormed_two, rows, aux, outs):
    resid, attn, cotangent, gain_two, gain_three = aux
    dresid_out, gain_two_grad, gain_three_grad = outs
    scale = rms_scale(resid[rows, :])
    unit = resid[rows, :] * scale
    gain_three_grad[...] += fold_rows(dnormed_two * unit)
    dresid = cotangent[rows, :].astype(F32) + vector_back(dnormed_two, unit, scale, gain_three[...])
    dresid_out[rows, :] = dresid
    scale = rms_scale(attn[rows, :])
    unit = attn[rows, :] * scale
    gain_two_grad[...] += fold_rows(dresid * unit)
    return vector_back(dresid, unit, scale, gain_two[...])


def before_attention(dnormed_one, rows, aux, outs):
    tokens, dresid, gain_one = aux
    tokens_grad, gain_grad = outs
    vector = tokens[rows, :].astype(F32)
    scale = rms_scale(vector)
    unit = vector * scale
    gain_grad[...] += fold_rows(dnormed_one * unit)
    back = vector_back(dnormed_one, unit, scale, gain_one[...])
    tokens_grad[rows, :] = (dresid[rows, :] + back).astype(BF16)


def swapped(x, axis, k):
    return lax.ppermute(x, axis, [(i, i ^ k) for i in range(lax.axis_size(axis))])


def shards(
    tokens,
    cotangent,
    pre_attn_gain,
    w_query,
    w_key,
    w_value,
    w_out,
    post_attn_gain,
    pre_ffw_gain,
    w_gate,
    w_up,
    w_down,
    post_ffw_gain,
):
    dp_size, seq_size, mp_size = (lax.axis_size(axis) for axis in ("dp", "seq", "mp"))
    dp, seq, mp = lax.axis_index("dp"), lax.axis_index("seq"), lax.axis_index("mp")
    both = ("dp", "seq")
    heads = w_query.shape[1] // HEAD_DIM
    group = Q_HEADS // KV_HEADS
    kv_first = mp * heads // group
    q_width = heads * HEAD_DIM
    span = tokens.shape[1]
    width = tokens.shape[2]
    share = span // mp_size
    plan = attention_plan(span, seq_size)

    def gather_weight(x):
        return lax.all_gather(x, both, axis=0, tiled=True)

    w_qkv_own = jnp.concatenate(
        [
            w_query,
            lax.dynamic_slice_in_dim(w_key, kv_first * HEAD_DIM, HEAD_DIM, 1),
            lax.dynamic_slice_in_dim(w_value, kv_first * HEAD_DIM, HEAD_DIM, 1),
        ],
        axis=1,
    )
    w_qkv = gather_weight(w_qkv_own)
    gain_one, gain_two, gain_three, gain_four = gather_gains(
        [pre_attn_gain, post_attn_gain, pre_ffw_gain, post_ffw_gain], dp_size, seq_size
    )

    inputs = tokens[0].astype(F32)
    positions = seq * span + jnp.arange(span, dtype=jnp.int32)
    half_dim = HEAD_DIM // 2
    frequency = ROPE_BASE ** (-jnp.arange(half_dim, dtype=F32) * 2.0 / HEAD_DIM)
    angles = positions.astype(F32)[:, None, None] * frequency
    cosine = jnp.cos(angles)
    sine = jnp.sin(angles)
    scale_one = rms_scale(inputs)
    normed_one = (inputs * scale_one * gain_one).astype(BF16)
    w_out_t = gather_weight(after(w_out.T, w_qkv, normed_one))
    key_lin = dot_nn(normed_one, w_qkv[:, q_width : q_width + HEAD_DIM])
    keys_own = rotary(key_lin, cosine[:, 0], sine[:, 0], 1.0).astype(BF16)
    values_own = dot_nn(normed_one, w_qkv[:, q_width + HEAD_DIM :]).astype(BF16)
    own_pair = jnp.concatenate([keys_own, values_own], axis=1)
    pairs = lax.all_gather(after(own_pair, w_out_t), "seq", axis=0, tiled=True)
    query_lin = dot_nn(normed_one, w_qkv[:, :q_width]).reshape(span, heads, HEAD_DIM)
    queries = (rotary(query_lin, cosine, sine, 1.0) * HEAD_DIM ** (-0.5)).astype(BF16)
    queries = queries.reshape(span, q_width)

    units = w_gate.shape[1]
    gate_up_w = gather_weight(after(jnp.concatenate([w_gate, w_up], axis=1), pairs))

    attn_o, attn_exact, lse = attend(queries, pairs, plan)
    own_first = mp * share
    tokens_own = lax.dynamic_slice_in_dim(tokens[0], own_first, share, 0)
    cotangent_own = lax.dynamic_slice_in_dim(cotangent[0], own_first, share, 0)

    def by_owner(x):
        return jnp.concatenate(
            [lax.dynamic_slice_in_dim(x, (mp ^ k) * share, share, 0) for k in range(mp_size)], axis=0
        )

    attn, resid, normed_two = sum_rows(
        (attn_o,),
        w_out_t,
        after_attention,
        (tokens_own, gain_two, gain_three),
        ((share, F32), (share, F32)),
        True,
        True,
        mp_size,
        3,
    )
    sizes = (dp_size, seq_size, mp_size)
    shard_count = dp_size * seq_size
    steps = width // row_plan(width, share, mp_size)[0]

    def to_steps(x):
        return jnp.swapaxes(x.reshape(x.shape[0], shard_count, steps, -1), 1, 2).reshape(x.shape)

    def to_shards(x):
        return jnp.swapaxes(x.reshape(x.shape[0], steps, shard_count, -1), 1, 2).reshape(x.shape)

    output, grad_gain_four, dmixed_own, dmixed_first, hidden, gate_act, slope, down_wt = ffw(
        normed_two,
        gate_up_w,
        w_down.T,
        to_steps(resid),
        to_steps(cotangent_own),
        to_steps(gain_four),
        sizes,
        4,
    )
    output = to_shards(output)
    grad_gain_four = to_shards(grad_gain_four)

    def spread(x):
        return lax.psum_scatter(x, "seq", scatter_dimension=0, tiled=True)

    dmixed_low, grad_sums = [dmixed_first], []
    for t in range(steps):
        into = grad_sums[-1] if t > 1 else None
        columns = units * (steps - 2) if t == 1 else 0
        if t + 1 < steps:
            grad_sum, arrived = weight_grad(
                dmixed_low[t],
                (hidden,),
                20 + t,
                into=into,
                columns=columns,
                steps=dmixed_own,
                next_step=t + 1,
                mp_size=mp_size,
            )
            dmixed_low.append(arrived)
        else:
            grad_sum = weight_grad(dmixed_low[t], (hidden,), 20 + t, into=into, columns=columns)
        grad_sums.append(grad_sum)
    grad_down_first = spread(grad_sums[0])
    grad_down_rest = spread(after(grad_sums[-1], grad_down_first))
    grad_down = [grad_down_first] + [
        grad_down_rest[:, t * units : (t + 1) * units] for t in range(steps - 1)
    ]
    grad_down = jnp.concatenate(grad_down, axis=0).astype(F32).T
    dgate_low, dup_low = hidden_back(
        (after(dmixed_low[0], grad_sum), *dmixed_low[1:]), down_wt, gate_act, slope
    )
    grad_gate_up_sum = weight_grad(normed_two, (dgate_low, dup_low), 8)
    dresid, grad_gain_two, grad_gain_three, dattn_low = sum_rows(
        (after(dgate_low, grad_down_rest, grad_gate_up_sum), dup_low),
        gate_up_w,
        before_ffw,
        (resid, attn, cotangent_own, gain_two, gain_three),
        ((share, F32), (8, F32), (8, F32)),
        True,
        False,
        mp_size,
        5,
    )
    grad_gate_up = spread(after(grad_gate_up_sum, grad_down_rest))

    dattn_o = by_owner(dot_nn(dattn_low, w_out_t)).astype(BF16)
    dquery, dpairs = attend_back(queries, dattn_o, attn_exact, lse, pairs, plan)
    grad_out_sum = weight_grad(dattn_low, (by_owner(attn_o),), 9)
    dquery = dquery.reshape(span, heads, HEAD_DIM)
    dquery_low = (
        rotary(dquery * HEAD_DIM ** (-0.5), cosine, sine, -1.0).reshape(span, q_width).astype(BF16)
    )
    grad_q_sum = weight_grad(normed_one, (dquery_low,), 10, columns=2 * HEAD_DIM)
    own_grads = spread(after(dpairs, grad_gate_up, grad_out_sum, grad_q_sum)).astype(F32)
    grad_gate = grad_gate_up[:, :units].astype(F32)
    grad_up = grad_gate_up[:, units:].astype(F32)
    own_grads = after(own_grads, grad_gate, grad_up, grad_down)
    dkey_rot = own_grads[:, :HEAD_DIM]
    dkey_low = rotary(dkey_rot, cosine[:, 0], sine[:, 0], -1.0).astype(BF16)
    dvalue_low = own_grads[:, HEAD_DIM:].astype(BF16)
    dkv_low = jnp.concatenate([dkey_low, dvalue_low], axis=1)
    grad_qkv_sum = weight_grad(normed_one, (dkv_low,), 11, into=grad_q_sum)
    grad_qkv = spread(grad_qkv_sum)
    tokens_grad, grad_gain_one = sum_rows(
        (dquery_low, after(dkv_low, grad_qkv_sum)),
        w_qkv,
        before_attention,
        (tokens_own, dresid, gain_one),
        ((share, BF16), (8, F32)),
        False,
        True,
        mp_size,
        6,
    )

    grad_out_t = spread(after(grad_out_sum, grad_qkv, tokens_grad))
    gain_grads, grad_key, grad_value = last_sums(
        [
            jnp.sum(grad, axis=0)
            for grad in (grad_gain_one, grad_gain_two, grad_gain_three, grad_gain_four)
        ],
        grad_qkv[:, q_width:],
        w_key.shape[1],
        heads,
        sizes,
    )
    return (
        output[None],
        tokens_grad[None],
        gain_grads[0],
        after(grad_qkv, grad_key)[:, :q_width].astype(F32),
        grad_key,
        grad_value,
        grad_out_t.astype(F32).T,
        gain_grads[1],
        gain_grads[2],
        grad_gate,
        grad_up,
        grad_down,
        gain_grads[3],
    )


def solution(mesh):
    weight = P(("dp", "seq"), "mp")
    whole_rows = P(("dp", "seq"), None)
    columns = P("mp", ("dp", "seq"))
    gain = P(("dp", "seq"))
    tokens = P("dp", "seq", None)
    rows = P("dp", ("seq", "mp"), None)
    in_specs = (
        tokens,
        tokens,
        gain,
        weight,
        whole_rows,
        whole_rows,
        columns,
        gain,
        gain,
        weight,
        weight,
        columns,
        gain,
    )
    out_specs = (
        rows,
        rows,
        gain,
        weight,
        whole_rows,
        whole_rows,
        columns,
        gain,
        gain,
        weight,
        weight,
        columns,
        gain,
    )
    return jax.shard_map(shards, mesh=mesh, in_specs=in_specs, out_specs=out_specs, check_vma=False)
```

```python
import functools

import jax
import jax.numpy as jnp
from jax import lax
from jax.experimental import pallas as pl
from jax.experimental.pallas import tpu as pltpu
from jax.sharding import PartitionSpec as P

Q_HEADS = 8
KV_HEADS = 4
HEAD_DIM = 256
WINDOW = 4096

EPSILON = 1e-06
SOFT_CAP = 50.0
ROPE_BASE = 10000.0
GELU_SCALE = (2.0 / 3.141592653589793) ** 0.5
GELU_CUBE = 0.044715
MESH = pl.DeviceIdType.MESH
VMEM_LIMIT = 56 * 1024 * 1024
LANES = 128
BF16 = jnp.bfloat16
F32 = jnp.float32


def after(value, *earlier):
    return lax.optimization_barrier((value, *earlier))[0]


def dot_nn(left, right):
    return lax.dot_general(left, right, (((1,), (0,)), ((), ())), preferred_element_type=F32)


def dot_nt(left, right):
    return lax.dot_general(left, right, (((1,), (1,)), ((), ())), preferred_element_type=F32)


def dot_tn(left, right):
    return lax.dot_general(left, right, (((0,), (0,)), ((), ())), preferred_element_type=F32)


def rms_scale(vector):
    return lax.rsqrt(jnp.mean(vector * vector, axis=-1, keepdims=True) + EPSILON)


def rotary(vector, cosine, sine, direction):
    half_dim = vector.shape[-1] // 2
    first_half = vector[..., :half_dim]
    second_half = vector[..., half_dim:]
    return jnp.concatenate(
        [
            first_half * cosine - direction * (second_half * sine),
            second_half * cosine + direction * (first_half * sine),
        ],
        axis=-1,
    )


def flipped(index, k):
    result, bit = index, 1
    while bit <= k:
        if k & bit:
            result = result + bit * (1 - 2 * lax.rem(index // bit, 2))
        bit *= 2
    return result


def last_kernel(
    sizes, heads, x_ref, kv_ref, o_ref, key_ref, value_ref, mine, from_mp, from_ws, kv_from, sems, kv_sem
):
    dp_size, seq_size, mp_size = sizes
    count = dp_size * seq_size
    dp, seq, mp = lax.axis_index("dp"), lax.axis_index("seq"), lax.axis_index("mp")
    rank = dp * seq_size + seq

    def mp_peer(k):
        return (dp, seq, flipped(mp, k))

    def ws_rank(k):
        return lax.rem(rank + k, count)

    def ws_peer(k):
        other = ws_rank(k)
        return (other // seq_size, lax.rem(other, seq_size), mp)

    def remote(src, dst, kind, k, device):
        copy = pltpu.make_async_remote_copy(
            src_ref=src,
            dst_ref=dst,
            send_sem=sems.at[kind, 0, k],
            recv_sem=sems.at[kind, 1, k],
            device_id=device,
            device_id_type=MESH,
        )
        copy.start()
        return copy

    barrier = pltpu.get_barrier_semaphore()
    for k in range(1, mp_size):
        pl.semaphore_signal(barrier, inc=1, device_id=mp_peer(k), device_id_type=MESH)
    for k in range(1, count):
        pl.semaphore_signal(barrier, inc=1, device_id=ws_peer(k), device_id_type=MESH)
    pl.semaphore_wait(barrier, mp_size - 1 + count - 1)
    copies = [remote(x_ref.at[ws_rank(k)], from_ws.at[k], 0, k, ws_peer(k)) for k in range(1, count)]
    pass_on, end_rows = row_gather(kv_ref, kv_from, mp_size, mp_peer, kv_sem)
    key_ref[...] = jnp.zeros_like(key_ref)
    value_ref[...] = jnp.zeros_like(value_ref)
    for copy in copies:
        copy.wait()
    total = x_ref[pl.ds(rank, 1)][0]
    for k in range(1, count):
        total = total + from_ws[k]
    mine[...] = total
    copies = [remote(mine, from_mp.at[k], 1, k, mp_peer(k)) for k in range(1, mp_size)]
    pass_on()
    for copy in copies:
        copy.wait()
    for k in range(1, mp_size):
        total = total + from_mp[k]
    o_ref[...] = total
    end_rows()
    rows = kv_ref.shape[0]
    for k in range(mp_size):
        piece = (kv_from[k * rows : (k + 1) * rows, :] if k else kv_ref[...]).astype(F32)
        head = flipped(mp, k) * heads // (Q_HEADS // KV_HEADS)
        columns = pl.ds(pl.multiple_of(head * HEAD_DIM, HEAD_DIM), HEAD_DIM)
        key_ref[:, columns] += piece[:, :HEAD_DIM]
        value_ref[:, columns] += piece[:, HEAD_DIM:]


def last_sums(grads, kv, kv_width, heads, sizes):
    dp_size, seq_size, mp_size = sizes
    count = dp_size * seq_size
    local = grads[0].shape[0] // count
    width = -(-local // LANES) * LANES
    block = jnp.transpose(jnp.stack(grads).reshape(len(grads), count, local), (1, 0, 2))
    block = jnp.pad(block, ((0, 0), (0, 8 - len(grads)), (0, width - local)))
    kv_out = jax.ShapeDtypeStruct((kv.shape[0], kv_width), F32)
    total, key, value = pl.pallas_call(
        functools.partial(last_kernel, sizes, heads),
        out_shape=(jax.ShapeDtypeStruct((8, width), F32), kv_out, kv_out),
        in_specs=[pl.BlockSpec(memory_space=pltpu.VMEM)] * 2,
        out_specs=(pl.BlockSpec(memory_space=pltpu.VMEM),) * 3,
        scratch_shapes=[
            pltpu.VMEM((8, width), F32),
            pltpu.VMEM((mp_size, 8, width), F32),
            pltpu.VMEM((count, 8, width), F32),
            pltpu.VMEM((mp_size * kv.shape[0], kv.shape[1]), BF16),
            pltpu.SemaphoreType.DMA((2, 2, max(count, mp_size))),
            pltpu.SemaphoreType.DMA((2, max(6, mp_size))),
        ],
        compiler_params=pltpu.CompilerParams(
            collective_id=2, has_side_effects=True, vmem_limit_bytes=VMEM_LIMIT
        ),
    )(block, kv)
    return [total[i, :local] for i in range(len(grads))], key, value


def travel(block, line_sem, pair_sem, seq_size):
    far = seq_size - 1
    dp, seq, mp = lax.axis_index("dp"), lax.axis_index("seq"), lax.axis_index("mp")

    def goes_on(way):
        return seq < far if way == 0 else seq > 0

    def comes(way, distance):
        return seq >= distance if way == 0 else seq + distance <= far

    def piece(t, way, distance, sems, device):
        place = block(t, seq - distance if way == 0 else seq + distance)
        return pltpu.make_async_remote_copy(
            src_ref=place,
            dst_ref=place,
            send_sem=sems.at[0, t, way, distance],
            recv_sem=sems.at[1, t, way, distance],
            device_id=device,
            device_id_type=MESH,
        )

    def line(t, way, distance):
        return piece(t, way, distance, line_sem, (dp, seq + 1 - 2 * way, mp))

    def pair(t, way, distance):
        return piece(t, way, distance, pair_sem, (1 - dp, seq, mp))

    def start(t):
        for way in range(2):
            @pl.when(goes_on(way))
            def _(way=way):
                line(t, way, 0).start()

    def share(t):
        pair(t, 0, 0).start()

    def arrival(t, distance):
        for way in range(2):
            @pl.when(comes(way, distance))
            def _(way=way):
                line(t, way, distance - 1).wait_recv()
                if distance < far:
                    @pl.when(goes_on(way))
                    def _():
                        line(t, way, distance).start()

                pair(t, way, distance).start()

    def complete(t):
        pair(t, 0, 0).wait_recv()
        for way in range(2):
            for distance in range(1, seq_size):
                @pl.when(comes(way, distance))
                def _(way=way, distance=distance):
                    pair(t, way, distance).wait_recv()

    def drain(t):
        pair(t, 0, 0).wait_send()
        for way in range(2):
            for distance in range(far):
                @pl.when(goes_on(way) & comes(way, distance))
                def _(way=way, distance=distance):
                    line(t, way, distance).wait_send()

            for distance in range(1, seq_size):
                @pl.when(comes(way, distance))
                def _(way=way, distance=distance):
                    pair(t, way, distance).wait_send()

    return start, share, arrival, complete, drain


def window(rank, local):
    return rank * local // LANES * LANES


def window_width(count, local):
    widest = max(rank * local - window(rank, local) for rank in range(count)) + local
    return -(-widest // LANES) * LANES


def front_kernel(plan, tokens_ref, wq_ref, wk_ref, wv_ref, wo_ref, gains_ref, *refs):
    dp_size, seq_size, heads, pieces, row_step = plan
    gain_rows, qkv_ref, normed_ref, w_qkv_ref, w_out_ref = refs[:5]
    tokens, normed, w_qkv, w_out, gains, refs = *refs[5:10], refs[10:]
    load_sem, gain_sem, line_sem, pair_sem, store_sem = refs
    count = dp_size * seq_size
    span, width = tokens.shape
    shard, q_width = wq_ref.shape
    columns = w_qkv.shape[1]
    dp, seq, mp = lax.axis_index("dp"), lax.axis_index("seq"), lax.axis_index("mp")
    rank = dp * seq_size + seq

    def peer(k):
        other = lax.rem(rank + k, count)
        return (other // seq_size, lax.rem(other, seq_size), mp)

    own = pl.ds(pl.multiple_of(rank * shard, 16), shard)
    head = pl.ds(pl.multiple_of(mp * heads // (Q_HEADS // KV_HEADS) * HEAD_DIM, HEAD_DIM), HEAD_DIM)
    loads = [
        pltpu.make_async_copy(wq_ref, w_qkv.at[own, pl.ds(0, q_width)], load_sem.at[0]),
        pltpu.make_async_copy(wk_ref.at[:, head], w_qkv.at[own, pl.ds(q_width, HEAD_DIM)], load_sem.at[1]),
        pltpu.make_async_copy(
            wv_ref.at[:, head], w_qkv.at[own, pl.ds(q_width + HEAD_DIM, HEAD_DIM)], load_sem.at[2]
        ),
        pltpu.make_async_copy(wo_ref, w_out.at[own], load_sem.at[3]),
        pltpu.make_async_copy(tokens_ref, tokens, load_sem.at[4]),
    ]
    for load in loads:
        load.start()
    barrier = pltpu.get_barrier_semaphore()
    for k in range(1, count):
        pl.semaphore_signal(barrier, inc=1, device_id=peer(k), device_id_type=MESH)
    pl.semaphore_wait(barrier, count - 1)

    def block(t, at):
        first = (dp * seq_size + at) * shard
        if t == pieces:
            return w_out.at[pl.ds(pl.multiple_of(first, 16), shard)]
        piece = shard // pieces
        return w_qkv.at[pl.ds(pl.multiple_of(first + t * piece, 16), piece)]

    start, share, arrival, complete, drain = travel(block, line_sem, pair_sem, seq_size)
    for load in loads[:4]:
        load.wait()
    gain_copies = [remote_copy(gains_ref, gains.at[rank], gain_sem, (k,), peer(k)) for k in range(1, count)]
    for t in range(pieces):
        start(t)
    for t in range(pieces):
        share(t)
    gains[pl.ds(rank, 1)] = gains_ref[...][None]
    gain_rows[...] = jnp.zeros_like(gain_rows)
    for copy in gain_copies:
        copy.wait()
    for r in range(count):
        first = window(r, shard)
        gain_rows[:, first : first + gains.shape[2]] += gains[r]
    loads[4].wait()

    def norm_rows(r, carry):
        rows = pl.ds(pl.multiple_of(r * row_step, row_step), row_step)
        vector = tokens[rows, :].astype(F32)
        normed[rows, :] = (vector * rms_scale(vector) * gain_rows[0:1, :]).astype(BF16)
        return carry

    blocks = span // row_step
    for t in range(pieces):
        lax.fori_loop(blocks * t // pieces, blocks * (t + 1) // pieces, norm_rows, 0)
        arrival(t, 1)
    for distance in range(2, seq_size):
        if distance == seq_size - 1:
            start(pieces)
            share(pieces)
        for t in range(pieces):
            arrival(t, distance)
    for t in range(pieces):
        complete(t)
    stores = [
        pltpu.make_async_copy(w_qkv, w_qkv_ref, store_sem.at[0]),
        pltpu.make_async_copy(normed, normed_ref, store_sem.at[1]),
        pltpu.make_async_copy(w_out, w_out_ref, store_sem.at[2]),
    ]
    stores[0].start()
    stores[1].start()
    tiles = columns // HEAD_DIM
    for i in range(max(tiles, seq_size - 1)):
        if i < tiles:
            part = slice(i * HEAD_DIM, (i + 1) * HEAD_DIM)
            qkv_ref[:, part] = dot_nn(normed[...], w_qkv[:, part])
        if i < seq_size - 1:
            arrival(pieces, i + 1)
    complete(pieces)
    stores[2].start()
    for store in stores:
        store.wait()
    for t in range(pieces + 1):
        drain(t)


def front(tokens, w_query, w_key, w_value, w_out_t, gains, heads, sizes):
    dp_size, seq_size, _ = sizes
    count = dp_size * seq_size
    span, width = tokens.shape
    shard, q_width = w_query.shape
    columns = q_width + 2 * HEAD_DIM
    pieces = 3
    lanes = window_width(count, shard)
    offset = (lax.axis_index("dp") * seq_size + lax.axis_index("seq")) * shard % LANES
    block = jnp.pad(jnp.stack([gain.astype(F32) for gain in gains]), ((0, 8 - len(gains)), (0, 0)))
    block = lax.dynamic_update_slice_in_dim(jnp.zeros((8, lanes), F32), block, offset, 1)
    plan = (dp_size, seq_size, heads, pieces, min(32, span))
    return pl.pallas_call(
        functools.partial(front_kernel, plan),
        out_shape=(
            jax.ShapeDtypeStruct((8, max(width, window(count - 1, shard) + lanes)), F32),
            jax.ShapeDtypeStruct((span, columns), F32),
            jax.ShapeDtypeStruct((span, width), BF16),
            jax.ShapeDtypeStruct((width, columns), BF16),
            jax.ShapeDtypeStruct((width, q_width), BF16),
        ),
        in_specs=[pl.BlockSpec(memory_space=pl.ANY)] * 5 + [pl.BlockSpec(memory_space=pltpu.VMEM)],
        out_specs=(pl.BlockSpec(memory_space=pltpu.VMEM),) * 2 + (pl.BlockSpec(memory_space=pl.ANY),) * 3,
        scratch_shapes=[
            pltpu.VMEM((span, width), BF16),
            pltpu.VMEM((span, width), BF16),
            pltpu.VMEM((width, columns), BF16),
            pltpu.VMEM((width, q_width), BF16),
            pltpu.VMEM((count, 8, lanes), F32),
            pltpu.SemaphoreType.DMA((5,)),
            pltpu.SemaphoreType.DMA((2, count)),
            pltpu.SemaphoreType.DMA((2, pieces + 1, 2, seq_size)),
            pltpu.SemaphoreType.DMA((2, pieces + 1, 2, seq_size)),
            pltpu.SemaphoreType.DMA((3,)),
        ],
        compiler_params=pltpu.CompilerParams(
            collective_id=1, has_side_effects=True, vmem_limit_bytes=VMEM_LIMIT
        ),
    )(tokens, w_query, w_key, w_value, w_out_t, block)


def key_mask(shape, first_key, first_query, tile, far):
    key = first_key + lax.broadcasted_iota(jnp.int32, shape, 0)
    query = first_query + lax.rem(lax.broadcasted_iota(jnp.int32, shape, 1), tile)
    return key > query if far else key <= query


def for_key_tiles(tile_fn, index, tile, span, step, hops, windowed):
    seq = lax.axis_index("seq")
    per_block = span // step
    last = jnp.minimum(seq, hops)
    if windowed:
        @pl.when(seq >= hops)
        def _():
            tile_fn(pl.multiple_of((seq - hops) * span, span), span, "far")

        last = jnp.minimum(seq, hops - 1)

    def past(t, carry):
        tile_fn(pl.multiple_of(t * step, step), step, "")
        return carry

    lax.fori_loop((seq - last) * per_block, seq * per_block, past, 0)
    tile_fn(pl.multiple_of(seq * span, span), (index + 1) * tile, "near")


def head_rows(ref, index, tile):
    block = ref[pl.ds(pl.multiple_of(index * tile, tile), tile), :]
    return jnp.concatenate(
        [block[:, h * HEAD_DIM : (h + 1) * HEAD_DIM] for h in range(ref.shape[1] // HEAD_DIM)], axis=0
    )


def put_head_rows(ref, index, tile, rows):
    for h in range(ref.shape[1] // HEAD_DIM):
        ref[pl.ds(index * tile, tile), h * HEAD_DIM : (h + 1) * HEAD_DIM] = rows[
            h * tile : (h + 1) * tile
        ].astype(ref.dtype)


def attend_kernel(plan, q_ref, kv_ref, o_ref, of_ref, lse_ref, acc, total):
    tile, span, step, hops, windowed = plan
    for i in range(span // tile):
        query = head_rows(q_ref, i, tile)
        rows = query.shape[0]
        acc[...] = jnp.zeros_like(acc)
        total[...] = jnp.zeros_like(total)

        def tile_fn(first, count, mask, i=i, query=query, rows=rows):
            key = kv_ref[pl.ds(first, count), :HEAD_DIM]
            value = kv_ref[pl.ds(first, count), HEAD_DIM:]
            raw = dot_nt(key, query)
            weight = jnp.exp(SOFT_CAP * jnp.tanh(raw * (1.0 / SOFT_CAP)))
            if mask:
                inside = key_mask(weight.shape, 0, i * tile, tile, mask == "far")
                weight = jnp.where(inside, weight, 0.0)
            total[...] += jnp.sum(weight.reshape(count // 8, 8, rows), axis=0)
            acc[...] += dot_tn(value, weight.astype(BF16))

        for_key_tiles(tile_fn, i, tile, span, step, hops, windowed)
        row_total = jnp.sum(total[...], axis=0, keepdims=True)
        out = (acc[...] / row_total).T
        put_head_rows(o_ref, i, tile, out)
        put_head_rows(of_ref, i, tile, out)
        lse_ref[i] = jnp.log(row_total)


def attend_back_kernel(plan, q_ref, do_ref, of_ref, lse_ref, kv_ref, dq_ref, dkv_ref, grads, acc):
    tile, span, step, hops, windowed = plan
    grads[...] = jnp.zeros_like(grads)
    for i in range(span // tile):
        query = head_rows(q_ref, i, tile)
        dout = head_rows(do_ref, i, tile)
        lse = lse_ref[i]
        delta = jnp.sum(dout.astype(F32) * head_rows(of_ref, i, tile), axis=-1, keepdims=True)
        delta = jnp.broadcast_to(delta, (delta.shape[0], LANES)).T[:1]
        acc[...] = jnp.zeros_like(acc)

        def tile_fn(first, count, mask, i=i, query=query, dout=dout, lse=lse, delta=delta):
            key = kv_ref[pl.ds(first, count), :HEAD_DIM]
            value = kv_ref[pl.ds(first, count), HEAD_DIM:]
            bounded = jnp.tanh(dot_nt(key, query) * (1.0 / SOFT_CAP))
            prob = jnp.exp(SOFT_CAP * bounded - lse)
            if mask:
                inside = key_mask(prob.shape, 0, i * tile, tile, mask == "far")
                prob = jnp.where(inside, prob, 0.0)
            dprob = dot_nt(value, dout)
            draw = (prob * (dprob - delta) * (1.0 - bounded * bounded)).astype(BF16)
            grads[pl.ds(first, count), HEAD_DIM:] += dot_nn(prob.astype(BF16), dout)
            grads[pl.ds(first, count), :HEAD_DIM] += dot_nn(draw, query)
            acc[...] += dot_tn(key, draw)

        for_key_tiles(tile_fn, i, tile, span, step, hops, windowed)
        put_head_rows(dq_ref, i, tile, acc[...].T)
    dkv_ref[...] = grads[...].astype(BF16)


def attention_plan(span, seq_size):
    hops = min(WINDOW // span, seq_size - 1)
    return (min(256, span), span, min(512, span), hops, seq_size * span > WINDOW)


def attend(queries, pairs, plan):
    tile, span = plan[:2]
    heads = queries.shape[1] // HEAD_DIM
    rows = heads * tile
    return pl.pallas_call(
        functools.partial(attend_kernel, plan),
        out_shape=(
            jax.ShapeDtypeStruct(queries.shape, BF16),
            jax.ShapeDtypeStruct(queries.shape, F32),
            jax.ShapeDtypeStruct((span // tile, 1, rows), F32),
        ),
        in_specs=[pl.BlockSpec(memory_space=pltpu.VMEM)] * 2,
        out_specs=(pl.BlockSpec(memory_space=pltpu.VMEM),) * 3,
        scratch_shapes=[pltpu.VMEM((HEAD_DIM, rows), F32), pltpu.VMEM((8, rows), F32)],
        compiler_params=pltpu.CompilerParams(vmem_limit_bytes=VMEM_LIMIT),
        cost_estimate=pl.CostEstimate(
            flops=12 * queries.size * span, bytes_accessed=8 * queries.size, transcendentals=0
        ),
    )(queries, pairs)


def attend_back(queries, dout, exact, lse, pairs, plan):
    tile, span = plan[:2]
    rows = queries.shape[1] // HEAD_DIM * tile
    return pl.pallas_call(
        functools.partial(attend_back_kernel, plan),
        out_shape=(
            jax.ShapeDtypeStruct(queries.shape, F32),
            jax.ShapeDtypeStruct(pairs.shape, BF16),
        ),
        in_specs=[pl.BlockSpec(memory_space=pltpu.VMEM)] * 5,
        out_specs=(pl.BlockSpec(memory_space=pltpu.VMEM),) * 2,
        scratch_shapes=[pltpu.VMEM(pairs.shape, F32), pltpu.VMEM((HEAD_DIM, rows), F32)],
        compiler_params=pltpu.CompilerParams(vmem_limit_bytes=VMEM_LIMIT),
    )(queries, dout, exact, lse, pairs)


def remote_copy(src, dst, sems, index, device):
    copy = pltpu.make_async_remote_copy(
        src_ref=src,
        dst_ref=dst,
        send_sem=sems.at[(0, *index)],
        recv_sem=sems.at[(1, *index)],
        device_id=device,
        device_id_type=MESH,
    )
    copy.start()
    return copy


def sum_direct(ready, parts_at, steps, step, mp_size, peer, total, sent, arrived, sems):
    copies = []
    for t in range(steps):
        ready(t)
        for k in range(mp_size - 1, -1, -1):
            part = parts_at(t, k)
            if k == 0:
                total[:, t * step : (t + 1) * step] = part
            else:
                sent[t, k - 1] = part.astype(BF16)
                copies.append(
                    remote_copy(sent.at[t, k - 1], arrived.at[t, k - 1], sems, (t, k - 1), peer(k))
                )
    for t in range(steps):
        for k in range(1, mp_size):
            copies[t * (mp_size - 1) + mp_size - 1 - k].wait_recv()
            total[:, t * step : (t + 1) * step] += arrived[t, k - 1].astype(F32)
    return copies


def sum_square(ready, parts_at, steps, step, peer, total, kept, sent, arrived, sems, eager):
    half = step // 2
    copies, second = [], []

    def second_hop(t):
        copies[2 * t].wait_recv()
        sent[t, 1, 2] = (kept[t, 1] + arrived[t, 0, 1].astype(F32)).astype(BF16)
        second.append(remote_copy(sent.at[t, 1, 2], arrived.at[t, 1, 2], sems, (t, 2), peer(2)))
        copies[2 * t + 1].wait_recv()
        sent[t, 0, 2] = (kept[t, 0] + arrived[t, 1, 1].astype(F32)).astype(BF16)
        second.append(remote_copy(sent.at[t, 0, 2], arrived.at[t, 0, 2], sems, (t, 3), peer(1)))

    for t in range(steps):
        first = t * step
        ready(t)
        if eager and t:
            second_hop(t - 1)
        far = parts_at(t, 3)
        sent[t, 0, 1] = far[:, :half].astype(BF16)
        sent[t, 1, 1] = far[:, half:].astype(BF16)
        part = parts_at(t, 1)
        sent[t, 0, 0] = part[:, :half].astype(BF16)
        kept[t, 0] = part[:, half:]
        copies.append(
            remote_copy(sent.at[t, 0, pl.ds(0, 2)], arrived.at[t, 0, pl.ds(0, 2)], sems, (t, 0), peer(1))
        )
        part = parts_at(t, 2)
        sent[t, 1, 0] = part[:, half:].astype(BF16)
        kept[t, 1] = part[:, :half]
        copies.append(
            remote_copy(sent.at[t, 1, pl.ds(0, 2)], arrived.at[t, 1, pl.ds(0, 2)], sems, (t, 1), peer(2))
        )
        total[:, first : first + step] = parts_at(t, 0)
    for t in range(steps - 1 if eager else 0, steps):
        second_hop(t)
    for t in range(steps):
        first = t * step
        second[2 * t].wait_recv()
        total[:, first : first + half] += arrived[t, 0, 0].astype(F32) + arrived[t, 1, 2].astype(F32)
        second[2 * t + 1].wait_recv()
        total[:, first + half : first + step] += arrived[t, 1, 0].astype(F32) + arrived[t, 0, 2].astype(
            F32
        )
    return copies + second


def row_gather(own, gathered, mp_size, peer, sems):
    share = own.shape[0]
    if mp_size != 4:
        copies = [
            remote_copy(own, gathered.at[pl.ds(k * share, share)], sems, (k,), peer(k))
            for k in range(mp_size - 1, 0, -1)
        ]

        def finish():
            for copy in copies:
                copy.wait()

        return lambda: None, finish

    half = share // 2

    def place(k, lower):
        return gathered.at[pl.ds(k * share + lower * half, half)]

    upper, lower = own.at[pl.ds(0, half)], own.at[pl.ds(half, half)]
    to_one = remote_copy(upper, place(1, 0), sems, (0,), peer(1))
    to_two = remote_copy(lower, place(2, 1), sems, (1,), peer(2))
    copies = [
        remote_copy(upper, place(2, 0), sems, (2,), peer(2)),
        remote_copy(lower, place(1, 1), sems, (3,), peer(1)),
    ]

    def pass_on():
        to_one.wait_recv()
        copies.append(remote_copy(place(1, 0), place(3, 0), sems, (4,), peer(2)))
        to_two.wait_recv()
        copies.append(remote_copy(place(2, 1), place(3, 1), sems, (5,), peer(1)))

    def finish():
        to_one.wait_send()
        to_two.wait_send()
        for copy in copies:
            copy.wait()

    return pass_on, finish


def rows_kernel(plan, rows_fn, *refs):
    mp_size, share, step, row_step, natural, n_left, n_aux, n_out, gather = plan
    lefts, weight_ref, refs = refs[:n_left], refs[n_left], refs[n_left + 1 :]
    aux, refs = refs[:n_aux], refs[n_aux:]
    outs, refs = refs[:n_out], refs[n_out:]
    if gather:
        gathered, refs = refs[0], refs[1:]
    left, weight, total, own, kept, sent, arrived, in_sem, sum_sem, row_sem = refs
    steps = total.shape[1] // step
    dp, seq, mp = lax.axis_index("dp"), lax.axis_index("seq"), lax.axis_index("mp")

    def peer(k):
        return (dp, seq, flipped(mp, k))

    left_copies, weight_copies = {}, []
    for k in range(mp_size):
        first = (flipped(mp, k) if natural else k) * share
        left_copies[k] = []
        column = 0
        for i, ref in enumerate(lefts):
            depth = ref.shape[1]
            left_copies[k].append(
                pltpu.make_async_copy(
                    ref.at[pl.ds(first, share)],
                    left.at[k, :, pl.ds(column, depth)],
                    in_sem.at[2 + k * n_left + i],
                )
            )
            column += depth
    for t in range(steps):
        weight_copies.append(
            pltpu.make_async_copy(
                weight_ref.at[pl.ds(t * step, step)], weight.at[t % 2], in_sem.at[t % 2]
            )
        )
    weight_copies[0].start()
    for k in range(mp_size - 1, -1, -1):
        for copy in left_copies[k]:
            copy.start()

    barrier = pltpu.get_barrier_semaphore()
    for k in range(1, mp_size):
        pl.semaphore_signal(barrier, inc=1, device_id=peer(k), device_id_type=MESH)
    pl.semaphore_wait(barrier, mp_size - 1)

    def ready(t):
        weight_copies[t].wait()
        if t + 1 < steps:
            weight_copies[t + 1].start()

    def parts_at(t, k):
        if t == 0:
            for copy in left_copies[k]:
                copy.wait()
        return dot_nt(left[k], weight[t % 2])

    finish_rows(
        ready,
        parts_at,
        (mp_size, share, step, row_step),
        (rows_fn, aux, outs, gathered if gather else None),
        peer,
        (total, own, kept, sent, arrived),
        (sum_sem, row_sem, in_sem.at[0]),
    )


def finish_rows(ready, parts_at, sizes, rows, peer, buffers, sems, eager=False):
    mp_size, share, step, row_step = sizes
    rows_fn, aux, outs, gathered = rows
    total, own, kept, sent, arrived = buffers
    sum_sem, row_sem, keep_sem = sems
    steps = total.shape[1] // step
    if mp_size == 4:
        sums = sum_square(
            ready, parts_at, steps, step, peer, total, kept, sent, arrived, sum_sem, eager
        )
    else:
        sums = sum_direct(
            ready, parts_at, steps, step, mp_size, peer, total, sent, arrived, sum_sem
        )

    def rows_at(r, carry):
        rows = pl.ds(pl.multiple_of(r * row_step, row_step), row_step)
        result = rows_fn(total[rows, :], rows, aux, outs)
        if gathered is not None:
            result = result.astype(BF16)
            if len(own.shape) == 2:
                own[rows, :] = result
            else:
                for t in range(steps):
                    own[t, rows, :] = result[:, t * step : (t + 1) * step]
        return carry

    for ref in outs:
        if ref.shape[0] == 8:
            ref[...] = jnp.zeros_like(ref)
    lax.fori_loop(0, share // row_step, rows_at, 0)
    if gathered is not None:
        first = own if len(own.shape) == 2 else own.at[0]
        keep = pltpu.make_async_copy(first, gathered.at[pl.ds(0, share)], keep_sem)
        keep.start()
        pass_on, finish = row_gather(first, gathered, mp_size, peer, row_sem)
        pass_on()
        finish()
        keep.wait()
    for copy in sums:
        copy.wait_send()


def row_plan(width, share, mp_size):
    step = 768 if width % 768 == 0 else width
    steps = width // step
    if mp_size == 4:
        pieces, kept = (steps, 2, 3, share, step // 2), (steps, 2, share, step // 2)
    else:
        pieces, kept = (steps, mp_size - 1, share, step), (8, LANES)
    buffers = [
        pltpu.VMEM((share, width), F32),
        pltpu.VMEM((share, width), BF16),
        pltpu.VMEM(kept, F32),
        pltpu.VMEM(pieces, BF16),
        pltpu.VMEM(pieces, BF16),
    ]
    sems = [
        pltpu.SemaphoreType.DMA((2, steps, max(4, mp_size - 1))),
        pltpu.SemaphoreType.DMA((2, max(6, mp_size))),
    ]
    return step, min(32, share), buffers, sems


def sum_rows(lefts, weight, rows_fn, aux, outs, gather, natural, mp_size, collective_id):
    span = lefts[0].shape[0]
    width, depth = weight.shape
    share = span // mp_size
    step, row_step, buffers, sems = row_plan(width, share, mp_size)
    plan = (mp_size, share, step, row_step, natural, len(lefts), len(aux), len(outs), gather)
    out_shape = [jax.ShapeDtypeStruct((rows, width), dtype) for rows, dtype in outs]
    out_specs = [pl.BlockSpec(memory_space=pltpu.VMEM)] * len(outs)
    if gather:
        out_shape.append(jax.ShapeDtypeStruct((span, width), BF16))
        out_specs.append(pl.BlockSpec(memory_space=pl.ANY))
    return pl.pallas_call(
        functools.partial(rows_kernel, plan, rows_fn),
        out_shape=out_shape,
        in_specs=[pl.BlockSpec(memory_space=pl.ANY)] * (len(lefts) + 1)
        + [pl.BlockSpec(memory_space=pltpu.VMEM)] * len(aux),
        out_specs=out_specs,
        scratch_shapes=[
            pltpu.VMEM((mp_size, share, depth), BF16),
            pltpu.VMEM((2, step, depth), BF16),
            *buffers,
            pltpu.SemaphoreType.DMA((2 + mp_size * len(lefts),)),
            *sems,
        ],
        compiler_params=pltpu.CompilerParams(
            collective_id=collective_id, has_side_effects=True, vmem_limit_bytes=VMEM_LIMIT
        ),
    )(*lefts, weight, *aux)


def weight_grad_kernel(plan, *refs):
    n_right, tile, half, first_column, n_into, steps, mp_size = plan
    left_ref, rights, refs = refs[0], refs[1 : 1 + n_right], refs[1 + n_right + n_into :]
    out_ref, refs = refs[0], refs[1:]
    if steps:
        steps_ref, gathered, refs = left_ref, refs[: len(steps)], refs[len(steps) :]
        own_rows, row_sems, refs = refs[0], refs[1 : 1 + len(steps)], refs[1 + len(steps) :]
        left_ref = gathered[0]
    left, right, sent, arrived, own, result, in_sem, swap_sem, out_sem = refs
    dp, seq, mp = lax.axis_index("dp"), lax.axis_index("seq"), lax.axis_index("mp")
    other = (1 - dp, seq, mp)

    def peer(k):
        return (dp, seq, flipped(mp, k))

    if steps:
        rows_load = pltpu.make_async_copy(
            steps_ref.at[pl.ds(steps[0], len(steps))], own_rows, in_sem.at[4]
        )
        rows_load.start()
    lefts = []
    for i, side in enumerate((1 - dp, dp)):
        columns = pl.ds(pl.multiple_of(side * half, LANES), half)
        lefts.append(pltpu.make_async_copy(left_ref.at[:, columns], left.at[i], in_sem.at[2 + i]))
    sources = []
    for ref in rights:
        for first in range(0, ref.shape[1], tile):
            sources.append(ref.at[:, pl.ds(first, tile)])
    tiles = len(sources)
    loads = [
        pltpu.make_async_copy(source, right.at[t % 2], in_sem.at[t % 2])
        for t, source in enumerate(sources)
    ]
    loads[0].start()
    barrier = pltpu.get_barrier_semaphore()
    pl.semaphore_signal(barrier, inc=1, device_id=other, device_id_type=MESH)
    if steps:
        for k in range(1, mp_size):
            pl.semaphore_signal(barrier, inc=1, device_id=peer(k), device_id_type=MESH)
    pl.semaphore_wait(barrier, mp_size if steps else 1)
    if steps:
        rows_load.wait()
        share = own_rows.shape[1]
        keeps = [
            pltpu.make_async_copy(own_rows.at[n], gathered[n].at[pl.ds(0, share)], in_sem.at[4 + n])
            for n in range(len(steps))
        ]
        for copy in keeps:
            copy.start()
        pass_on, end_rows = row_gather(own_rows.at[0], gathered[0], mp_size, peer, row_sems[0])
        pass_on()
        end_rows()
        keeps[0].wait()
        rest = [
            row_gather(own_rows.at[n], gathered[n], mp_size, peer, row_sems[n])
            for n in range(1, len(steps))
        ]
    for copy in lefts:
        copy.start()
    swaps, stores = [], []

    def finish(t):
        swaps[t].wait_recv()
        if t >= 2:
            stores[t - 2].wait()
        result[t % 2] = (own[t % 2] + arrived[t].astype(F32)).astype(BF16)
        stores.append(
            pltpu.make_async_copy(
                result.at[t % 2],
                out_ref.at[:, pl.ds(first_column + t * tile, tile)],
                out_sem.at[t % 2],
            )
        )
        stores[t].start()

    for t in range(tiles):
        loads[t].wait()
        if t + 1 < tiles:
            loads[t + 1].start()
        if t == 0:
            lefts[0].wait()
        sent[t] = dot_tn(left[0], right[t % 2]).astype(BF16)
        swaps.append(remote_copy(sent.at[t], arrived.at[t], swap_sem, (t,), other))
        if t == 0:
            lefts[1].wait()
        own[t % 2] = dot_tn(left[1], right[t % 2])
        if t >= 1:
            finish(t - 1)
        if t == tiles // 2 and steps:
            for pass_on, _ in rest:
                pass_on()
    finish(tiles - 1)
    for store in stores[-2:]:
        store.wait()
    for swap in swaps:
        swap.wait_send()
    if steps:
        for copy in keeps[1:]:
            copy.wait()
        for _, end_rows in rest:
            end_rows()


def weight_grad(left, rights, collective_id, into=None, columns=0, steps=(), mp_size=1):
    rows, width = rights[0].shape[0], left.shape[-1]
    half = width // 2
    total = sum(right.shape[1] for right in rights)
    tile = next(
        t
        for t in (768, 512, 384, 256, LANES)
        if total >= 2 * t and all(right.shape[1] % t == 0 for right in rights)
    )
    tiles = total // tile
    first = 0 if into is None else into.shape[1] - total
    earlier = () if into is None else (into,)
    out_shape = [jax.ShapeDtypeStruct((half, first + total + columns), BF16)]
    scratch = []
    if steps:
        out_shape += [jax.ShapeDtypeStruct((rows, width), BF16)] * len(steps)
        scratch = [pltpu.VMEM((len(steps), *left.shape[1:]), BF16)]
        scratch += [pltpu.SemaphoreType.DMA((2, max(6, mp_size)))] * len(steps)
    plan = (len(rights), tile, half, first, len(earlier), tuple(steps), mp_size)
    results = pl.pallas_call(
        functools.partial(weight_grad_kernel, plan),
        out_shape=out_shape,
        in_specs=[pl.BlockSpec(memory_space=pl.ANY)] * (1 + len(rights) + len(earlier)),
        out_specs=[pl.BlockSpec(memory_space=pl.ANY)] * len(out_shape),
        input_output_aliases={} if into is None else {1 + len(rights): 0},
        scratch_shapes=[
            *scratch,
            pltpu.VMEM((2, rows, half), BF16),
            pltpu.VMEM((2, rows, tile), BF16),
            pltpu.VMEM((tiles, half, tile), BF16),
            pltpu.VMEM((tiles, half, tile), BF16),
            pltpu.VMEM((2, half, tile), F32),
            pltpu.VMEM((2, half, tile), BF16),
            pltpu.SemaphoreType.DMA((4 + max(1, len(steps)),)),
            pltpu.SemaphoreType.DMA((2, tiles)),
            pltpu.SemaphoreType.DMA((2,)),
        ],
        compiler_params=pltpu.CompilerParams(
            collective_id=collective_id, has_side_effects=True, vmem_limit_bytes=VMEM_LIMIT
        ),
    )(left, *rights, *earlier)
    return results if steps else results[0]


def ffw_kernel(plan, normed_ref, gate_up_ref, shard_ref, resid_ref, cotangent_ref, gain_ref, *refs):
    mp_size, seq_size, share, step, row_step, tile = plan
    output_ref, gain_grad_ref, own_ref, dmixed_ref, hidden_ref, act_ref, slope_ref, down_ref = refs[:8]
    normed, gate_up, hidden, down, staged, *refs = refs[8:]
    buffers, refs = refs[:5], refs[5:]
    load_sem, store_sem, local_sem, line_sem, pair_sem, sum_sem, row_sem = refs
    steps, _, units = down.shape
    piece = step // (2 * seq_size)
    far = seq_size - 1
    dp, seq, mp = lax.axis_index("dp"), lax.axis_index("seq"), lax.axis_index("mp")
    sibling = (1 - dp, seq, mp)

    def peer(k):
        return (dp, seq, flipped(mp, k))

    def block(t, at):
        first = pl.multiple_of((dp * seq_size + at) * piece, piece)
        return down.at[t, pl.ds(first, piece)]

    start, share_piece, arrival, complete, drain = travel(block, line_sem, pair_sem, seq_size)
    normed_load = pltpu.make_async_copy(normed_ref, normed, local_sem.at[0])
    normed_load.start()
    shard_loads = [
        pltpu.make_async_copy(
            shard_ref.at[pl.ds(t * piece, piece)], block(t, seq), local_sem.at[1 + t]
        )
        for t in range(steps)
    ]
    for load in shard_loads:
        load.start()

    def loads(i, slot):
        return [
            pltpu.make_async_copy(
                gate_up_ref.at[:, pl.ds(pl.multiple_of(side * units + i * tile, LANES), tile)],
                gate_up.at[slot, side],
                load_sem.at[slot, side],
            )
            for side in range(2)
        ]

    def stores(i, slot):
        columns = pl.ds(pl.multiple_of(i * tile, LANES), tile)
        return [
            pltpu.make_async_copy(staged.at[slot, 0], act_ref.at[:, columns], store_sem.at[slot, 0]),
            pltpu.make_async_copy(staged.at[slot, 1], slope_ref.at[:, columns], store_sem.at[slot, 1]),
        ]

    for load in loads(0, 0):
        load.start()
    barrier = pltpu.get_barrier_semaphore()
    for k in range(1, mp_size):
        pl.semaphore_signal(barrier, inc=1, device_id=peer(k), device_id_type=MESH)
    pl.semaphore_signal(barrier, inc=1, device_id=sibling, device_id_type=MESH)
    for way in range(2):
        @pl.when(seq < far if way == 0 else seq > 0)
        def _(way=way):
            pl.semaphore_signal(
                barrier, inc=1, device_id=(dp, seq + 1 - 2 * way, mp), device_id_type=MESH
            )

    line_peers = (seq + far) // seq_size + (2 * far - seq) // seq_size
    pl.semaphore_wait(barrier, mp_size + line_peers)

    for t in range(steps):
        shard_loads[t].wait()
        start(t)
    for t in range(steps):
        share_piece(t)
    normed_load.wait()
    arrivals = [(t, distance) for distance in range(1, seq_size) for t in range(steps)]
    tiles = units // tile
    early = [(2 * n + 2, event) for n, event in enumerate(arrivals) if 2 * n + 2 < tiles]
    late = arrivals[len(early) :]

    def units_at(i, carry):
        slot = lax.rem(i, 2)
        for load in loads(i, slot):
            load.wait()

        @pl.when(i + 1 < tiles)
        def _():
            for load in loads(i + 1, 1 - slot):
                load.start()

        @pl.when(i >= 2)
        def _():
            for store in stores(i - 2, slot):
                store.wait()

        gate = dot_nn(normed[...], gate_up[slot, 0])
        up = dot_nn(normed[...], gate_up[slot, 1])
        squared = gate * gate
        bend = jnp.tanh(GELU_SCALE * gate * (1.0 + GELU_CUBE * squared))
        side = 0.5 * (1.0 + bend)
        act = gate * side
        slope = side + (0.5 * GELU_SCALE) * gate * (1.0 - bend * bend) * (1.0 + 3.0 * GELU_CUBE * squared)
        staged[slot, 0] = act.astype(BF16)
        staged[slot, 1] = (slope * up).astype(BF16)
        for store in stores(i, slot):
            store.start()
        product = (act * up).astype(BF16)
        for k in range(mp_size):
            hidden[k, :, pl.ds(pl.multiple_of(i * tile, LANES), tile)] = product[
                k * share : (k + 1) * share
            ]
        for at, event in early:
            @pl.when(i == at)
            def _(event=event):
                arrival(*event)

        return carry

    lax.fori_loop(0, tiles, units_at, 0)
    for i in range(max(0, tiles - 2), tiles):
        for store in stores(i, i % 2):
            store.wait()
    hidden_stores = [
        pltpu.make_async_copy(hidden.at[k], hidden_ref.at[pl.ds(k * share, share)], local_sem.at[1 + k])
        for k in range(mp_size)
    ]
    for store in hidden_stores:
        store.start()
    down_stores = [
        pltpu.make_async_copy(
            down.at[t], down_ref.at[pl.ds(t * step, step)], local_sem.at[1 + mp_size + t]
        )
        for t in range(steps)
    ]
    waiting = list(late)

    def ready(t):
        while (t, far) in waiting:
            arrival(*waiting.pop(0))
        complete(t)
        down_stores[t].start()

    def parts_at(t, k):
        return dot_nt(hidden[k], down[t])

    finish_rows(
        ready,
        parts_at,
        (mp_size, share, step, row_step),
        (after_ffw, (resid_ref, cotangent_ref, gain_ref), (output_ref, gain_grad_ref), dmixed_ref),
        peer,
        buffers,
        (sum_sem, row_sem, local_sem.at[0]),
        eager=True,
    )
    own_store = pltpu.make_async_copy(buffers[1], own_ref, local_sem.at[0])
    own_store.start()
    for store in hidden_stores + down_stores:
        store.wait()
    own_store.wait()
    for t in range(steps):
        drain(t)


def ffw(normed, gate_up_w, down_shard, resid, cotangent, gain, sizes, collective_id):
    dp_size, seq_size, mp_size = sizes
    span, width = normed.shape
    units = gate_up_w.shape[1] // 2
    share = span // mp_size
    step, row_step, buffers, sems = row_plan(width, share, mp_size)
    steps = width // step
    buffers[1] = pltpu.VMEM((steps, share, step), BF16)
    tile = 256 if units % 256 == 0 else LANES
    plan = (mp_size, seq_size, share, step, row_step, tile)
    per_unit = jax.ShapeDtypeStruct((span, units), BF16)
    return pl.pallas_call(
        functools.partial(ffw_kernel, plan),
        out_shape=(
            jax.ShapeDtypeStruct((share, width), BF16),
            jax.ShapeDtypeStruct((8, width), F32),
            jax.ShapeDtypeStruct((steps, share, step), BF16),
            jax.ShapeDtypeStruct((span, step), BF16),
            per_unit,
            per_unit,
            per_unit,
            jax.ShapeDtypeStruct((width, units), BF16),
        ),
        in_specs=[pl.BlockSpec(memory_space=pl.ANY)] * 3 + [pl.BlockSpec(memory_space=pltpu.VMEM)] * 3,
        out_specs=(pl.BlockSpec(memory_space=pltpu.VMEM),) * 2 + (pl.BlockSpec(memory_space=pl.ANY),) * 6,
        scratch_shapes=[
            pltpu.VMEM((span, width), BF16),
            pltpu.VMEM((2, 2, width, tile), BF16),
            pltpu.VMEM((mp_size, share, units), BF16),
            pltpu.VMEM((steps, step, units), BF16),
            pltpu.VMEM((2, 2, span, tile), BF16),
            *buffers,
            pltpu.SemaphoreType.DMA((2, 2)),
            pltpu.SemaphoreType.DMA((2, 2)),
            pltpu.SemaphoreType.DMA((1 + mp_size + steps,)),
            pltpu.SemaphoreType.DMA((2, steps, 2, seq_size)),
            pltpu.SemaphoreType.DMA((2, steps, 2, seq_size)),
            *sems,
        ],
        compiler_params=pltpu.CompilerParams(
            collective_id=collective_id, has_side_effects=True, vmem_limit_bytes=VMEM_LIMIT
        ),
    )(normed, gate_up_w, down_shard, resid, cotangent, gain)


def hidden_back_kernel(n_parts, *refs):
    parts, (down_ref, act_ref, slope_ref, dgate_ref, dup_ref) = refs[:n_parts], refs[n_parts:]
    first, dhidden = 0, 0.0
    for part in parts:
        depth = part.shape[1]
        dhidden = dhidden + dot_nn(part[...], down_ref[first : first + depth, :])
        first += depth
    dgate_ref[...] = (dhidden * slope_ref[...].astype(F32)).astype(BF16)
    dup_ref[...] = (dhidden * act_ref[...].astype(F32)).astype(BF16)


def hidden_back(dmixed, down_wt, act, slope):
    rows, depth = dmixed[0].shape
    width, units = down_wt.shape
    tile = 256 if units % 256 == 0 else units
    columns = pl.BlockSpec((rows, tile), lambda i: (0, i))
    return pl.pallas_call(
        functools.partial(hidden_back_kernel, len(dmixed)),
        grid=(units // tile,),
        out_shape=(jax.ShapeDtypeStruct((rows, units), BF16),) * 2,
        in_specs=[pl.BlockSpec((rows, depth), lambda i: (0, 0))] * len(dmixed)
        + [pl.BlockSpec((width, tile), lambda i: (0, i)), columns, columns],
        out_specs=(columns, columns),
        compiler_params=pltpu.CompilerParams(vmem_limit_bytes=VMEM_LIMIT),
    )(*dmixed, down_wt, act, slope)


def fold_rows(x):
    return jnp.sum(x.reshape(x.shape[0] // 8, 8, x.shape[1]), axis=0)


def after_attention(attn, rows, aux, outs):
    tokens, gain_two, gain_three = aux
    attn_out, resid_out = outs
    resid = tokens[rows, :].astype(F32) + attn * rms_scale(attn) * gain_two[...]
    attn_out[rows, :] = attn
    resid_out[rows, :] = resid
    return resid * rms_scale(resid) * gain_three[...]


def after_ffw(mixed, rows, aux, outs):
    resid, cotangent, gain_four = aux
    output, gain_grad = outs
    scale = rms_scale(mixed)
    unit = mixed * scale
    grad_out = cotangent[rows, :].astype(F32)
    output[rows, :] = (resid[rows, :] + unit * gain_four[...]).astype(BF16)
    gain_grad[...] += fold_rows(grad_out * unit)
    return vector_back(grad_out, unit, scale, gain_four[...])


def vector_back(grad_in, unit, scale, gain):
    unit_grad = grad_in * gain
    return scale * (unit_grad - unit * jnp.mean(unit_grad * unit, axis=-1, keepdims=True))


def before_ffw(dnormed_two, rows, aux, outs):
    resid, attn, cotangent, gain_two, gain_three = aux
    dresid_out, gain_two_grad, gain_three_grad = outs
    scale = rms_scale(resid[rows, :])
    unit = resid[rows, :] * scale
    gain_three_grad[...] += fold_rows(dnormed_two * unit)
    dresid = cotangent[rows, :].astype(F32) + vector_back(dnormed_two, unit, scale, gain_three[...])
    dresid_out[rows, :] = dresid
    scale = rms_scale(attn[rows, :])
    unit = attn[rows, :] * scale
    gain_two_grad[...] += fold_rows(dresid * unit)
    return vector_back(dresid, unit, scale, gain_two[...])


def before_attention(dnormed_one, rows, aux, outs):
    tokens, dresid, gain_one = aux
    tokens_grad, gain_grad = outs
    vector = tokens[rows, :].astype(F32)
    scale = rms_scale(vector)
    unit = vector * scale
    gain_grad[...] += fold_rows(dnormed_one * unit)
    back = vector_back(dnormed_one, unit, scale, gain_one[...])
    tokens_grad[rows, :] = (dresid[rows, :] + back).astype(BF16)


def swapped(x, axis, k):
    return lax.ppermute(x, axis, [(i, i ^ k) for i in range(lax.axis_size(axis))])


def shards(
    tokens,
    cotangent,
    pre_attn_gain,
    w_query,
    w_key,
    w_value,
    w_out,
    post_attn_gain,
    pre_ffw_gain,
    w_gate,
    w_up,
    w_down,
    post_ffw_gain,
):
    dp_size, seq_size, mp_size = (lax.axis_size(axis) for axis in ("dp", "seq", "mp"))
    dp, seq, mp = lax.axis_index("dp"), lax.axis_index("seq"), lax.axis_index("mp")
    both = ("dp", "seq")
    heads = w_query.shape[1] // HEAD_DIM
    q_width = heads * HEAD_DIM
    span = tokens.shape[1]
    width = tokens.shape[2]
    share = span // mp_size
    plan = attention_plan(span, seq_size)

    def gather_weight(x):
        return lax.all_gather(x, both, axis=0, tiled=True)

    sizes = (dp_size, seq_size, mp_size)
    gain_rows, qkv, normed_one, w_qkv, w_out_t = front(
        tokens[0],
        w_query,
        w_key,
        w_value,
        w_out.T,
        [pre_attn_gain, post_attn_gain, pre_ffw_gain, post_ffw_gain],
        heads,
        sizes,
    )
    gain_one, gain_two, gain_three, gain_four = (gain_rows[i : i + 1, :width] for i in range(4))
    positions = seq * span + jnp.arange(span, dtype=jnp.int32)
    half_dim = HEAD_DIM // 2
    frequency = ROPE_BASE ** (-jnp.arange(half_dim, dtype=F32) * 2.0 / HEAD_DIM)
    angles = positions.astype(F32)[:, None, None] * frequency
    cosine = jnp.cos(angles)
    sine = jnp.sin(angles)
    keys_own = rotary(qkv[:, q_width : q_width + HEAD_DIM], cosine[:, 0], sine[:, 0], 1.0)
    own_pair = jnp.concatenate([keys_own, qkv[:, q_width + HEAD_DIM :]], axis=1).astype(BF16)
    pairs = lax.all_gather(own_pair, "seq", axis=0, tiled=True)
    query_lin = qkv[:, :q_width].reshape(span, heads, HEAD_DIM)
    queries = (rotary(query_lin, cosine, sine, 1.0) * HEAD_DIM ** (-0.5)).astype(BF16)
    queries = queries.reshape(span, q_width)

    units = w_gate.shape[1]
    gate_up_w = gather_weight(after(jnp.concatenate([w_gate, w_up], axis=1), pairs))

    attn_o, attn_exact, lse = attend(queries, pairs, plan)
    own_first = mp * share
    tokens_own = lax.dynamic_slice_in_dim(tokens[0], own_first, share, 0)
    cotangent_own = lax.dynamic_slice_in_dim(cotangent[0], own_first, share, 0)

    def by_owner(x):
        return jnp.concatenate(
            [lax.dynamic_slice_in_dim(x, (mp ^ k) * share, share, 0) for k in range(mp_size)], axis=0
        )

    attn, resid, normed_two = sum_rows(
        (attn_o,),
        w_out_t,
        after_attention,
        (tokens_own, gain_two, gain_three),
        ((share, F32), (share, F32)),
        True,
        True,
        mp_size,
        3,
    )
    shard_count = dp_size * seq_size
    steps = width // row_plan(width, share, mp_size)[0]

    def to_steps(x):
        return jnp.swapaxes(x.reshape(x.shape[0], shard_count, steps, -1), 1, 2).reshape(x.shape)

    def to_shards(x):
        return jnp.swapaxes(x.reshape(x.shape[0], steps, shard_count, -1), 1, 2).reshape(x.shape)

    output, grad_gain_four, dmixed_own, dmixed_first, hidden, gate_act, slope, down_wt = ffw(
        normed_two,
        gate_up_w,
        w_down.T,
        to_steps(resid),
        to_steps(cotangent_own),
        to_steps(gain_four),
        sizes,
        4,
    )
    output = to_shards(output)
    grad_gain_four = to_shards(grad_gain_four)

    def spread(x):
        return lax.psum_scatter(x, "seq", scatter_dimension=0, tiled=True)

    grad_sums = [weight_grad(dmixed_first, (hidden,), 20)]
    grad_sum, *arrived = weight_grad(
        after(dmixed_own, grad_sums[0]),
        (hidden,),
        21,
        columns=units * (steps - 2),
        steps=tuple(range(1, steps)),
        mp_size=mp_size,
    )
    for t in range(2, steps):
        grad_sum = weight_grad(
            arrived[t - 1], (hidden,), 20 + t, into=grad_sum, columns=units * (steps - 1 - t)
        )
    grad_sums.append(grad_sum)
    dmixed_low = [dmixed_first, *arrived]
    grad_down_first = spread(grad_sums[0])
    grad_down_rest = spread(after(grad_sums[-1], grad_down_first))
    grad_down = [grad_down_first] + [
        grad_down_rest[:, t * units : (t + 1) * units] for t in range(steps - 1)
    ]
    grad_down = jnp.concatenate(grad_down, axis=0).astype(F32).T
    dgate_low, dup_low = hidden_back(
        (after(dmixed_low[0], grad_sum), *dmixed_low[1:]), down_wt, gate_act, slope
    )
    grad_gate_up_sum = weight_grad(normed_two, (dgate_low, dup_low), 8)
    dresid, grad_gain_two, grad_gain_three, dattn_low = sum_rows(
        (after(dgate_low, grad_down_rest, grad_gate_up_sum), dup_low),
        gate_up_w,
        before_ffw,
        (resid, attn, cotangent_own, gain_two, gain_three),
        ((share, F32), (8, F32), (8, F32)),
        True,
        False,
        mp_size,
        5,
    )
    grad_gate_up = spread(after(grad_gate_up_sum, grad_down_rest))

    dattn_o = by_owner(dot_nn(dattn_low, w_out_t)).astype(BF16)
    dquery, dpairs = attend_back(queries, dattn_o, attn_exact, lse, pairs, plan)
    grad_out_sum = weight_grad(dattn_low, (by_owner(attn_o),), 9)
    dquery = dquery.reshape(span, heads, HEAD_DIM)
    dquery_low = (
        rotary(dquery * HEAD_DIM ** (-0.5), cosine, sine, -1.0).reshape(span, q_width).astype(BF16)
    )
    grad_q_sum = weight_grad(normed_one, (dquery_low,), 10, columns=2 * HEAD_DIM)
    own_grads = spread(after(dpairs, grad_gate_up, grad_out_sum, grad_q_sum)).astype(F32)
    grad_gate = grad_gate_up[:, :units].astype(F32)
    grad_up = grad_gate_up[:, units:].astype(F32)
    own_grads = after(own_grads, grad_gate, grad_up, grad_down)
    dkey_rot = own_grads[:, :HEAD_DIM]
    dkey_low = rotary(dkey_rot, cosine[:, 0], sine[:, 0], -1.0).astype(BF16)
    dvalue_low = own_grads[:, HEAD_DIM:].astype(BF16)
    dkv_low = jnp.concatenate([dkey_low, dvalue_low], axis=1)
    grad_qkv_sum = weight_grad(normed_one, (dkv_low,), 11, into=grad_q_sum)
    grad_qkv = spread(grad_qkv_sum)
    tokens_grad, grad_gain_one = sum_rows(
        (dquery_low, after(dkv_low, grad_qkv_sum)),
        w_qkv,
        before_attention,
        (tokens_own, dresid, gain_one),
        ((share, BF16), (8, F32)),
        False,
        True,
        mp_size,
        6,
    )

    grad_out_t = spread(after(grad_out_sum, grad_qkv, tokens_grad))
    gain_grads, grad_key, grad_value = last_sums(
        [
            jnp.sum(grad, axis=0)
            for grad in (grad_gain_one, grad_gain_two, grad_gain_three, grad_gain_four)
        ],
        grad_qkv[:, q_width:],
        w_key.shape[1],
        heads,
        sizes,
    )
    return (
        output[None],
        tokens_grad[None],
        gain_grads[0],
        after(grad_qkv, grad_key)[:, :q_width].astype(F32),
        grad_key,
        grad_value,
        grad_out_t.astype(F32).T,
        gain_grads[1],
        gain_grads[2],
        grad_gate,
        grad_up,
        grad_down,
        gain_grads[3],
    )


def solution(mesh):
    weight = P(("dp", "seq"), "mp")
    whole_rows = P(("dp", "seq"), None)
    columns = P("mp", ("dp", "seq"))
    gain = P(("dp", "seq"))
    tokens = P("dp", "seq", None)
    rows = P("dp", ("seq", "mp"), None)
    in_specs = (
        tokens,
        tokens,
        gain,
        weight,
        whole_rows,
        whole_rows,
        columns,
        gain,
        gain,
        weight,
        weight,
        columns,
        gain,
    )
    out_specs = (
        rows,
        rows,
        gain,
        weight,
        whole_rows,
        whole_rows,
        columns,
        gain,
        gain,
        weight,
        weight,
        columns,
        gain,
    )
    return jax.shard_map(shards, mesh=mesh, in_specs=in_specs, out_specs=out_specs, check_vma=False)
```

```python
import functools

import jax
import jax.numpy as jnp
from jax import lax
from jax.experimental import pallas as pl
from jax.experimental.pallas import tpu as pltpu
from jax.sharding import PartitionSpec as P

Q_HEADS = 8
KV_HEADS = 4
HEAD_DIM = 256
WINDOW = 4096

EPSILON = 1e-06
SOFT_CAP = 50.0
ROPE_BASE = 10000.0
GELU_SCALE = (2.0 / 3.141592653589793) ** 0.5
GELU_CUBE = 0.044715
MESH = pl.DeviceIdType.MESH
VMEM_LIMIT = 56 * 1024 * 1024
LANES = 128
BF16 = jnp.bfloat16
F32 = jnp.float32


def after(value, *earlier):
    return lax.optimization_barrier((value, *earlier))[0]


def dot_nn(left, right):
    return lax.dot_general(left, right, (((1,), (0,)), ((), ())), preferred_element_type=F32)


def dot_nt(left, right):
    return lax.dot_general(left, right, (((1,), (1,)), ((), ())), preferred_element_type=F32)


def dot_tn(left, right):
    return lax.dot_general(left, right, (((0,), (0,)), ((), ())), preferred_element_type=F32)


def rms_scale(vector):
    return lax.rsqrt(jnp.mean(vector * vector, axis=-1, keepdims=True) + EPSILON)


def rotary(vector, cosine, sine, direction):
    half_dim = vector.shape[-1] // 2
    first_half = vector[..., :half_dim]
    second_half = vector[..., half_dim:]
    return jnp.concatenate(
        [
            first_half * cosine - direction * (second_half * sine),
            second_half * cosine + direction * (first_half * sine),
        ],
        axis=-1,
    )


def flipped(index, k):
    result, bit = index, 1
    while bit <= k:
        if k & bit:
            result = result + bit * (1 - 2 * lax.rem(index // bit, 2))
        bit *= 2
    return result


def last_kernel(
    sizes, heads, x_ref, kv_ref, o_ref, key_ref, value_ref, mine, from_mp, from_ws, kv_from, sems, kv_sem
):
    dp_size, seq_size, mp_size = sizes
    count = dp_size * seq_size
    dp, seq, mp = lax.axis_index("dp"), lax.axis_index("seq"), lax.axis_index("mp")
    rank = dp * seq_size + seq

    def mp_peer(k):
        return (dp, seq, flipped(mp, k))

    def ws_rank(k):
        return lax.rem(rank + k, count)

    def ws_peer(k):
        other = ws_rank(k)
        return (other // seq_size, lax.rem(other, seq_size), mp)

    def remote(src, dst, kind, k, device):
        copy = pltpu.make_async_remote_copy(
            src_ref=src,
            dst_ref=dst,
            send_sem=sems.at[kind, 0, k],
            recv_sem=sems.at[kind, 1, k],
            device_id=device,
            device_id_type=MESH,
        )
        copy.start()
        return copy

    barrier = pltpu.get_barrier_semaphore()
    for k in range(1, mp_size):
        pl.semaphore_signal(barrier, inc=1, device_id=mp_peer(k), device_id_type=MESH)
    for k in range(1, count):
        pl.semaphore_signal(barrier, inc=1, device_id=ws_peer(k), device_id_type=MESH)
    pl.semaphore_wait(barrier, mp_size - 1 + count - 1)
    copies = [remote(x_ref.at[ws_rank(k)], from_ws.at[k], 0, k, ws_peer(k)) for k in range(1, count)]
    pass_on, end_rows = row_gather(kv_ref, kv_from, mp_size, mp_peer, kv_sem)
    key_ref[...] = jnp.zeros_like(key_ref)
    value_ref[...] = jnp.zeros_like(value_ref)
    for copy in copies:
        copy.wait()
    total = x_ref[pl.ds(rank, 1)][0]
    for k in range(1, count):
        total = total + from_ws[k]
    mine[...] = total
    copies = [remote(mine, from_mp.at[k], 1, k, mp_peer(k)) for k in range(1, mp_size)]
    pass_on()
    for copy in copies:
        copy.wait()
    for k in range(1, mp_size):
        total = total + from_mp[k]
    o_ref[...] = total
    end_rows()
    rows = kv_ref.shape[0]
    for k in range(mp_size):
        piece = (kv_from[k * rows : (k + 1) * rows, :] if k else kv_ref[...]).astype(F32)
        head = flipped(mp, k) * heads // (Q_HEADS // KV_HEADS)
        columns = pl.ds(pl.multiple_of(head * HEAD_DIM, HEAD_DIM), HEAD_DIM)
        key_ref[:, columns] += piece[:, :HEAD_DIM]
        value_ref[:, columns] += piece[:, HEAD_DIM:]


def last_sums(grads, kv, kv_width, heads, sizes):
    dp_size, seq_size, mp_size = sizes
    count = dp_size * seq_size
    local = grads[0].shape[0] // count
    width = -(-local // LANES) * LANES
    block = jnp.transpose(jnp.stack(grads).reshape(len(grads), count, local), (1, 0, 2))
    block = jnp.pad(block, ((0, 0), (0, 8 - len(grads)), (0, width - local)))
    kv_out = jax.ShapeDtypeStruct((kv.shape[0], kv_width), F32)
    total, key, value = pl.pallas_call(
        functools.partial(last_kernel, sizes, heads),
        out_shape=(jax.ShapeDtypeStruct((8, width), F32), kv_out, kv_out),
        in_specs=[pl.BlockSpec(memory_space=pltpu.VMEM)] * 2,
        out_specs=(pl.BlockSpec(memory_space=pltpu.VMEM),) * 3,
        scratch_shapes=[
            pltpu.VMEM((8, width), F32),
            pltpu.VMEM((mp_size, 8, width), F32),
            pltpu.VMEM((count, 8, width), F32),
            pltpu.VMEM((mp_size * kv.shape[0], kv.shape[1]), BF16),
            pltpu.SemaphoreType.DMA((2, 2, max(count, mp_size))),
            pltpu.SemaphoreType.DMA((2, max(6, mp_size))),
        ],
        compiler_params=pltpu.CompilerParams(
            collective_id=2, has_side_effects=True, vmem_limit_bytes=VMEM_LIMIT
        ),
    )(block, kv)
    return [total[i, :local] for i in range(len(grads))], key, value


def travel(block, line_sem, pair_sem, seq_size):
    far = seq_size - 1
    dp, seq, mp = lax.axis_index("dp"), lax.axis_index("seq"), lax.axis_index("mp")

    def goes_on(way):
        return seq < far if way == 0 else seq > 0

    def comes(way, distance):
        return seq >= distance if way == 0 else seq + distance <= far

    def piece(t, way, distance, sems, device):
        place = block(t, seq - distance if way == 0 else seq + distance)
        return pltpu.make_async_remote_copy(
            src_ref=place,
            dst_ref=place,
            send_sem=sems.at[0, t, way, distance],
            recv_sem=sems.at[1, t, way, distance],
            device_id=device,
            device_id_type=MESH,
        )

    def line(t, way, distance):
        return piece(t, way, distance, line_sem, (dp, seq + 1 - 2 * way, mp))

    def pair(t, way, distance):
        return piece(t, way, distance, pair_sem, (1 - dp, seq, mp))

    def start(t):
        for way in range(2):
            @pl.when(goes_on(way))
            def _(way=way):
                line(t, way, 0).start()

    def share(t):
        pair(t, 0, 0).start()

    def arrival(t, distance):
        for way in range(2):
            @pl.when(comes(way, distance))
            def _(way=way):
                line(t, way, distance - 1).wait_recv()
                if distance < far:
                    @pl.when(goes_on(way))
                    def _():
                        line(t, way, distance).start()

                pair(t, way, distance).start()

    def complete(t):
        pair(t, 0, 0).wait_recv()
        for way in range(2):
            for distance in range(1, seq_size):
                @pl.when(comes(way, distance))
                def _(way=way, distance=distance):
                    pair(t, way, distance).wait_recv()

    def drain(t):
        pair(t, 0, 0).wait_send()
        for way in range(2):
            for distance in range(far):
                @pl.when(goes_on(way) & comes(way, distance))
                def _(way=way, distance=distance):
                    line(t, way, distance).wait_send()

            for distance in range(1, seq_size):
                @pl.when(comes(way, distance))
                def _(way=way, distance=distance):
                    pair(t, way, distance).wait_send()

    return start, share, arrival, complete, drain


def window(rank, local):
    return rank * local // LANES * LANES


def window_width(count, local):
    widest = max(rank * local - window(rank, local) for rank in range(count)) + local
    return -(-widest // LANES) * LANES


def front_kernel(plan, tokens_ref, wq_ref, wk_ref, wv_ref, gains_ref, frequency_ref, *refs):
    dp_size, seq_size, heads, pieces, row_step = plan
    gain_rows, pair_ref, cosine_ref, sine_ref, normed_ref, w_qkv_ref = refs[:6]
    tokens, normed, w_qkv, gains, refs = *refs[6:10], refs[10:]
    load_sem, gain_sem, line_sem, pair_sem, store_sem = refs
    count = dp_size * seq_size
    span, width = tokens.shape
    shard, q_width = wq_ref.shape
    dp, seq, mp = lax.axis_index("dp"), lax.axis_index("seq"), lax.axis_index("mp")
    rank = dp * seq_size + seq

    def peer(k):
        other = lax.rem(rank + k, count)
        return (other // seq_size, lax.rem(other, seq_size), mp)

    own = pl.ds(pl.multiple_of(rank * shard, 16), shard)
    head = pl.ds(pl.multiple_of(mp * heads // (Q_HEADS // KV_HEADS) * HEAD_DIM, HEAD_DIM), HEAD_DIM)
    loads = [
        pltpu.make_async_copy(wq_ref, w_qkv.at[own, pl.ds(0, q_width)], load_sem.at[0]),
        pltpu.make_async_copy(wk_ref.at[:, head], w_qkv.at[own, pl.ds(q_width, HEAD_DIM)], load_sem.at[1]),
        pltpu.make_async_copy(
            wv_ref.at[:, head], w_qkv.at[own, pl.ds(q_width + HEAD_DIM, HEAD_DIM)], load_sem.at[2]
        ),
        pltpu.make_async_copy(tokens_ref, tokens, load_sem.at[3]),
    ]
    for load in loads:
        load.start()
    barrier = pltpu.get_barrier_semaphore()
    for k in range(1, count):
        pl.semaphore_signal(barrier, inc=1, device_id=peer(k), device_id_type=MESH)
    pl.semaphore_wait(barrier, count - 1)

    def block(t, at):
        piece = shard // pieces
        first = (dp * seq_size + at) * shard
        return w_qkv.at[pl.ds(pl.multiple_of(first + t * piece, 16), piece)]

    start, share, arrival, complete, drain = travel(block, line_sem, pair_sem, seq_size)
    for load in loads[:3]:
        load.wait()
    gain_copies = [remote_copy(gains_ref, gains.at[rank], gain_sem, (k,), peer(k)) for k in range(1, count)]
    for t in range(pieces):
        start(t)
    for t in range(pieces):
        share(t)
    position = seq * span + lax.broadcasted_iota(jnp.int32, cosine_ref.shape, 0)
    angle = position.astype(F32) * frequency_ref[0:1, :]
    cosine_ref[...] = jnp.cos(angle)
    sine_ref[...] = jnp.sin(angle)
    gains[pl.ds(rank, 1)] = gains_ref[...][None]
    gain_rows[...] = jnp.zeros_like(gain_rows)
    for copy in gain_copies:
        copy.wait()
    for r in range(count):
        first = window(r, shard)
        gain_rows[:, first : first + gains.shape[2]] += gains[r]
    loads[3].wait()

    def norm_rows(r, carry):
        rows = pl.ds(pl.multiple_of(r * row_step, row_step), row_step)
        vector = tokens[rows, :].astype(F32)
        normed[rows, :] = (vector * rms_scale(vector) * gain_rows[0:1, :]).astype(BF16)
        return carry

    blocks = span // row_step
    for t in range(pieces):
        lax.fori_loop(blocks * t // pieces, blocks * (t + 1) // pieces, norm_rows, 0)
        arrival(t, 1)
    for distance in range(2, seq_size):
        for t in range(pieces):
            arrival(t, distance)
    for t in range(pieces):
        complete(t)
    stores = [
        pltpu.make_async_copy(w_qkv, w_qkv_ref, store_sem.at[0]),
        pltpu.make_async_copy(normed, normed_ref, store_sem.at[1]),
    ]
    for store in stores:
        store.start()

    def project(first):
        return dot_nn(normed[...], w_qkv[:, first : first + HEAD_DIM])

    key = rotary(project(q_width), cosine_ref[...], sine_ref[...], 1.0)
    pair_ref[:, :HEAD_DIM] = key.astype(BF16)
    pair_ref[:, HEAD_DIM:] = project(q_width + HEAD_DIM).astype(BF16)
    for store in stores:
        store.wait()
    for t in range(pieces):
        drain(t)


def front(tokens, w_query, w_key, w_value, gains, heads, sizes):
    dp_size, seq_size, _ = sizes
    count = dp_size * seq_size
    span, width = tokens.shape
    shard, q_width = w_query.shape
    columns = q_width + 2 * HEAD_DIM
    half_dim = HEAD_DIM // 2
    pieces = 3
    lanes = window_width(count, shard)
    offset = (lax.axis_index("dp") * seq_size + lax.axis_index("seq")) * shard % LANES
    block = jnp.pad(jnp.stack([gain.astype(F32) for gain in gains]), ((0, 8 - len(gains)), (0, 0)))
    block = lax.dynamic_update_slice_in_dim(jnp.zeros((8, lanes), F32), block, offset, 1)
    frequency = ROPE_BASE ** (-jnp.arange(half_dim, dtype=F32) * 2.0 / HEAD_DIM)
    frequency = jnp.broadcast_to(frequency, (8, half_dim))
    plan = (dp_size, seq_size, heads, pieces, min(32, span))
    return pl.pallas_call(
        functools.partial(front_kernel, plan),
        out_shape=(
            jax.ShapeDtypeStruct((8, max(width, window(count - 1, shard) + lanes)), F32),
            jax.ShapeDtypeStruct((span, 2 * HEAD_DIM), BF16),
            jax.ShapeDtypeStruct((span, half_dim), F32),
            jax.ShapeDtypeStruct((span, half_dim), F32),
            jax.ShapeDtypeStruct((span, width), BF16),
            jax.ShapeDtypeStruct((width, columns), BF16),
        ),
        in_specs=[pl.BlockSpec(memory_space=pl.ANY)] * 4 + [pl.BlockSpec(memory_space=pltpu.VMEM)] * 2,
        out_specs=(pl.BlockSpec(memory_space=pltpu.VMEM),) * 4 + (pl.BlockSpec(memory_space=pl.ANY),) * 2,
        scratch_shapes=[
            pltpu.VMEM((span, width), BF16),
            pltpu.VMEM((span, width), BF16),
            pltpu.VMEM((width, columns), BF16),
            pltpu.VMEM((count, 8, lanes), F32),
            pltpu.SemaphoreType.DMA((4,)),
            pltpu.SemaphoreType.DMA((2, count)),
            pltpu.SemaphoreType.DMA((2, pieces, 2, seq_size)),
            pltpu.SemaphoreType.DMA((2, pieces, 2, seq_size)),
            pltpu.SemaphoreType.DMA((2,)),
        ],
        compiler_params=pltpu.CompilerParams(
            collective_id=1, has_side_effects=True, vmem_limit_bytes=VMEM_LIMIT
        ),
    )(tokens, w_query, w_key, w_value, block, frequency)


def carry_kernel(seq_size, shard_ref, full_ref, load_sem, line_sem, pair_sem):
    dp, seq, mp = lax.axis_index("dp"), lax.axis_index("seq"), lax.axis_index("mp")
    far = seq_size - 1
    shard = shard_ref.shape[0]

    def block(t, at):
        first = pl.multiple_of((dp * seq_size + at) * shard, 16)
        return full_ref.at[pl.ds(first, shard)]

    load = pltpu.make_async_copy(shard_ref, block(0, seq), load_sem)
    load.start()
    barrier = pltpu.get_barrier_semaphore()
    pl.semaphore_signal(barrier, inc=1, device_id=(1 - dp, seq, mp), device_id_type=MESH)
    for way in range(2):
        @pl.when(seq < far if way == 0 else seq > 0)
        def _(way=way):
            pl.semaphore_signal(
                barrier, inc=1, device_id=(dp, seq + 1 - 2 * way, mp), device_id_type=MESH
            )

    pl.semaphore_wait(barrier, 1 + (seq + far) // seq_size + (2 * far - seq) // seq_size)
    load.wait()
    start, share, arrival, complete, drain = travel(block, line_sem, pair_sem, seq_size)
    start(0)
    share(0)
    for distance in range(1, seq_size):
        arrival(0, distance)
    complete(0)
    drain(0)


def carry(shard, sizes, collective_id):
    dp_size, seq_size, _ = sizes
    return pl.pallas_call(
        functools.partial(carry_kernel, seq_size),
        out_shape=jax.ShapeDtypeStruct((shard.shape[0] * dp_size * seq_size, shard.shape[1]), BF16),
        in_specs=[pl.BlockSpec(memory_space=pl.ANY)],
        out_specs=pl.BlockSpec(memory_space=pl.ANY),
        scratch_shapes=[
            pltpu.SemaphoreType.DMA,
            pltpu.SemaphoreType.DMA((2, 1, 2, seq_size)),
            pltpu.SemaphoreType.DMA((2, 1, 2, seq_size)),
        ],
        compiler_params=pltpu.CompilerParams(collective_id=collective_id, has_side_effects=True),
    )(shard)


def key_mask(shape, first_key, first_query, tile, far):
    key = first_key + lax.broadcasted_iota(jnp.int32, shape, 0)
    query = first_query + lax.rem(lax.broadcasted_iota(jnp.int32, shape, 1), tile)
    return key > query if far else key <= query


def for_key_tiles(tile_fn, index, tile, span, step, hops, windowed):
    seq = lax.axis_index("seq")
    per_block = span // step
    last = jnp.minimum(seq, hops)
    if windowed:
        @pl.when(seq >= hops)
        def _():
            tile_fn(pl.multiple_of((seq - hops) * span, span), span, "far")

        last = jnp.minimum(seq, hops - 1)

    def past(t, carry):
        tile_fn(pl.multiple_of(t * step, step), step, "")
        return carry

    lax.fori_loop((seq - last) * per_block, seq * per_block, past, 0)
    tile_fn(pl.multiple_of(seq * span, span), (index + 1) * tile, "near")


def head_rows(ref, index, tile):
    block = ref[pl.ds(pl.multiple_of(index * tile, tile), tile), :]
    return jnp.concatenate(
        [block[:, h * HEAD_DIM : (h + 1) * HEAD_DIM] for h in range(ref.shape[1] // HEAD_DIM)], axis=0
    )


def put_head_rows(ref, index, tile, rows):
    for h in range(ref.shape[1] // HEAD_DIM):
        ref[pl.ds(index * tile, tile), h * HEAD_DIM : (h + 1) * HEAD_DIM] = rows[
            h * tile : (h + 1) * tile
        ].astype(ref.dtype)


def attend_kernel(plan, q_ref, kv_ref, o_ref, of_ref, lse_ref, acc, total):
    tile, span, step, hops, windowed = plan
    for i in range(span // tile):
        query = head_rows(q_ref, i, tile)
        rows = query.shape[0]
        acc[...] = jnp.zeros_like(acc)
        total[...] = jnp.zeros_like(total)

        def tile_fn(first, count, mask, i=i, query=query, rows=rows):
            key = kv_ref[pl.ds(first, count), :HEAD_DIM]
            value = kv_ref[pl.ds(first, count), HEAD_DIM:]
            raw = dot_nt(key, query)
            weight = jnp.exp(SOFT_CAP * jnp.tanh(raw * (1.0 / SOFT_CAP)))
            if mask:
                inside = key_mask(weight.shape, 0, i * tile, tile, mask == "far")
                weight = jnp.where(inside, weight, 0.0)
            total[...] += jnp.sum(weight.reshape(count // 8, 8, rows), axis=0)
            acc[...] += dot_tn(value, weight.astype(BF16))

        for_key_tiles(tile_fn, i, tile, span, step, hops, windowed)
        row_total = jnp.sum(total[...], axis=0, keepdims=True)
        out = (acc[...] / row_total).T
        put_head_rows(o_ref, i, tile, out)
        put_head_rows(of_ref, i, tile, out)
        lse_ref[i] = jnp.log(row_total)


def attend_back_kernel(plan, q_ref, do_ref, of_ref, lse_ref, kv_ref, dq_ref, dkv_ref, grads, acc):
    tile, span, step, hops, windowed = plan
    grads[...] = jnp.zeros_like(grads)
    for i in range(span // tile):
        query = head_rows(q_ref, i, tile)
        dout = head_rows(do_ref, i, tile)
        lse = lse_ref[i]
        delta = jnp.sum(dout.astype(F32) * head_rows(of_ref, i, tile), axis=-1, keepdims=True)
        delta = jnp.broadcast_to(delta, (delta.shape[0], LANES)).T[:1]
        acc[...] = jnp.zeros_like(acc)

        def tile_fn(first, count, mask, i=i, query=query, dout=dout, lse=lse, delta=delta):
            key = kv_ref[pl.ds(first, count), :HEAD_DIM]
            value = kv_ref[pl.ds(first, count), HEAD_DIM:]
            bounded = jnp.tanh(dot_nt(key, query) * (1.0 / SOFT_CAP))
            prob = jnp.exp(SOFT_CAP * bounded - lse)
            if mask:
                inside = key_mask(prob.shape, 0, i * tile, tile, mask == "far")
                prob = jnp.where(inside, prob, 0.0)
            dprob = dot_nt(value, dout)
            draw = (prob * (dprob - delta) * (1.0 - bounded * bounded)).astype(BF16)
            grads[pl.ds(first, count), HEAD_DIM:] += dot_nn(prob.astype(BF16), dout)
            grads[pl.ds(first, count), :HEAD_DIM] += dot_nn(draw, query)
            acc[...] += dot_tn(key, draw)

        for_key_tiles(tile_fn, i, tile, span, step, hops, windowed)
        put_head_rows(dq_ref, i, tile, acc[...].T)
    dkv_ref[...] = grads[...].astype(BF16)


def attention_plan(span, seq_size):
    hops = min(WINDOW // span, seq_size - 1)
    return (min(256, span), span, min(512, span), hops, seq_size * span > WINDOW)


def attend(queries, pairs, plan):
    tile, span = plan[:2]
    heads = queries.shape[1] // HEAD_DIM
    rows = heads * tile
    return pl.pallas_call(
        functools.partial(attend_kernel, plan),
        out_shape=(
            jax.ShapeDtypeStruct(queries.shape, BF16),
            jax.ShapeDtypeStruct(queries.shape, F32),
            jax.ShapeDtypeStruct((span // tile, 1, rows), F32),
        ),
        in_specs=[pl.BlockSpec(memory_space=pltpu.VMEM)] * 2,
        out_specs=(pl.BlockSpec(memory_space=pltpu.VMEM),) * 3,
        scratch_shapes=[pltpu.VMEM((HEAD_DIM, rows), F32), pltpu.VMEM((8, rows), F32)],
        compiler_params=pltpu.CompilerParams(vmem_limit_bytes=VMEM_LIMIT),
        cost_estimate=pl.CostEstimate(
            flops=12 * queries.size * span, bytes_accessed=8 * queries.size, transcendentals=0
        ),
    )(queries, pairs)


def attend_back(queries, dout, exact, lse, pairs, plan):
    tile, span = plan[:2]
    rows = queries.shape[1] // HEAD_DIM * tile
    return pl.pallas_call(
        functools.partial(attend_back_kernel, plan),
        out_shape=(
            jax.ShapeDtypeStruct(queries.shape, F32),
            jax.ShapeDtypeStruct(pairs.shape, BF16),
        ),
        in_specs=[pl.BlockSpec(memory_space=pltpu.VMEM)] * 5,
        out_specs=(pl.BlockSpec(memory_space=pltpu.VMEM),) * 2,
        scratch_shapes=[pltpu.VMEM(pairs.shape, F32), pltpu.VMEM((HEAD_DIM, rows), F32)],
        compiler_params=pltpu.CompilerParams(vmem_limit_bytes=VMEM_LIMIT),
    )(queries, dout, exact, lse, pairs)


def remote_copy(src, dst, sems, index, device):
    copy = pltpu.make_async_remote_copy(
        src_ref=src,
        dst_ref=dst,
        send_sem=sems.at[(0, *index)],
        recv_sem=sems.at[(1, *index)],
        device_id=device,
        device_id_type=MESH,
    )
    copy.start()
    return copy


def sum_direct(ready, parts_at, steps, step, mp_size, peer, total, sent, arrived, sems):
    copies = []
    for t in range(steps):
        ready(t)
        for k in range(mp_size - 1, -1, -1):
            part = parts_at(t, k)
            if k == 0:
                total[:, t * step : (t + 1) * step] = part
            else:
                sent[t, k - 1] = part.astype(BF16)
                copies.append(
                    remote_copy(sent.at[t, k - 1], arrived.at[t, k - 1], sems, (t, k - 1), peer(k))
                )
    for t in range(steps):
        for k in range(1, mp_size):
            copies[t * (mp_size - 1) + mp_size - 1 - k].wait_recv()
            total[:, t * step : (t + 1) * step] += arrived[t, k - 1].astype(F32)
    return copies


def sum_square(ready, parts_at, steps, step, peer, total, kept, sent, arrived, sems):
    half = step // 2
    copies, second = [], []

    def second_hop(t):
        copies[2 * t].wait_recv()
        sent[t, 1, 2] = (kept[t, 1] + arrived[t, 0, 1].astype(F32)).astype(BF16)
        second.append(remote_copy(sent.at[t, 1, 2], arrived.at[t, 1, 2], sems, (t, 2), peer(2)))
        copies[2 * t + 1].wait_recv()
        sent[t, 0, 2] = (kept[t, 0] + arrived[t, 1, 1].astype(F32)).astype(BF16)
        second.append(remote_copy(sent.at[t, 0, 2], arrived.at[t, 0, 2], sems, (t, 3), peer(1)))

    for t in range(steps):
        first = t * step
        ready(t)
        far = parts_at(t, 3)
        sent[t, 0, 1] = far[:, :half].astype(BF16)
        sent[t, 1, 1] = far[:, half:].astype(BF16)
        part = parts_at(t, 1)
        sent[t, 0, 0] = part[:, :half].astype(BF16)
        kept[t, 0] = part[:, half:]
        copies.append(
            remote_copy(sent.at[t, 0, pl.ds(0, 2)], arrived.at[t, 0, pl.ds(0, 2)], sems, (t, 0), peer(1))
        )
        part = parts_at(t, 2)
        sent[t, 1, 0] = part[:, half:].astype(BF16)
        kept[t, 1] = part[:, :half]
        copies.append(
            remote_copy(sent.at[t, 1, pl.ds(0, 2)], arrived.at[t, 1, pl.ds(0, 2)], sems, (t, 1), peer(2))
        )
        total[:, first : first + step] = parts_at(t, 0)
    for t in range(steps):
        second_hop(t)
    for t in range(steps):
        first = t * step
        second[2 * t].wait_recv()
        total[:, first : first + half] += arrived[t, 0, 0].astype(F32) + arrived[t, 1, 2].astype(F32)
        second[2 * t + 1].wait_recv()
        total[:, first + half : first + step] += arrived[t, 1, 0].astype(F32) + arrived[t, 0, 2].astype(
            F32
        )
    return copies + second


def row_gather(own, gathered, mp_size, peer, sems):
    share = own.shape[0]
    if mp_size != 4:
        copies = [
            remote_copy(own, gathered.at[pl.ds(k * share, share)], sems, (k,), peer(k))
            for k in range(mp_size - 1, 0, -1)
        ]

        def finish():
            for copy in copies:
                copy.wait()

        return lambda: None, finish

    half = share // 2

    def place(k, lower):
        return gathered.at[pl.ds(k * share + lower * half, half)]

    upper, lower = own.at[pl.ds(0, half)], own.at[pl.ds(half, half)]
    to_one = remote_copy(upper, place(1, 0), sems, (0,), peer(1))
    to_two = remote_copy(lower, place(2, 1), sems, (1,), peer(2))
    copies = [
        remote_copy(upper, place(2, 0), sems, (2,), peer(2)),
        remote_copy(lower, place(1, 1), sems, (3,), peer(1)),
    ]

    def pass_on():
        to_one.wait_recv()
        copies.append(remote_copy(place(1, 0), place(3, 0), sems, (4,), peer(2)))
        to_two.wait_recv()
        copies.append(remote_copy(place(2, 1), place(3, 1), sems, (5,), peer(1)))

    def finish():
        to_one.wait_send()
        to_two.wait_send()
        for copy in copies:
            copy.wait()

    return pass_on, finish


def rows_kernel(plan, rows_fn, *refs):
    mp_size, share, step, row_step, natural, n_left, n_aux, n_out, gather = plan
    lefts, weight_ref, refs = refs[:n_left], refs[n_left], refs[n_left + 1 :]
    aux, refs = refs[:n_aux], refs[n_aux:]
    outs, refs = refs[:n_out], refs[n_out:]
    if gather:
        gathered, refs = refs[0], refs[1:]
    left, weight, total, own, kept, sent, arrived, in_sem, sum_sem, row_sem = refs
    steps = total.shape[1] // step
    dp, seq, mp = lax.axis_index("dp"), lax.axis_index("seq"), lax.axis_index("mp")

    def peer(k):
        return (dp, seq, flipped(mp, k))

    left_copies, weight_copies = {}, []
    for k in range(mp_size):
        first = (flipped(mp, k) if natural else k) * share
        left_copies[k] = []
        column = 0
        for i, ref in enumerate(lefts):
            depth = ref.shape[1]
            left_copies[k].append(
                pltpu.make_async_copy(
                    ref.at[pl.ds(first, share)],
                    left.at[k, :, pl.ds(column, depth)],
                    in_sem.at[2 + k * n_left + i],
                )
            )
            column += depth
    for t in range(steps):
        weight_copies.append(
            pltpu.make_async_copy(
                weight_ref.at[pl.ds(t * step, step)], weight.at[t % 2], in_sem.at[t % 2]
            )
        )
    weight_copies[0].start()
    for k in range(mp_size - 1, -1, -1):
        for copy in left_copies[k]:
            copy.start()

    barrier = pltpu.get_barrier_semaphore()
    for k in range(1, mp_size):
        pl.semaphore_signal(barrier, inc=1, device_id=peer(k), device_id_type=MESH)
    pl.semaphore_wait(barrier, mp_size - 1)

    def ready(t):
        weight_copies[t].wait()
        if t + 1 < steps:
            weight_copies[t + 1].start()

    def parts_at(t, k):
        if t == 0:
            for copy in left_copies[k]:
                copy.wait()
        return dot_nt(left[k], weight[t % 2])

    finish_rows(
        ready,
        parts_at,
        (mp_size, share, step, row_step),
        (rows_fn, aux, outs, gathered if gather else None),
        peer,
        (total, own, kept, sent, arrived),
        (sum_sem, row_sem, in_sem.at[0]),
    )


def finish_rows(ready, parts_at, sizes, rows, peer, buffers, sems):
    mp_size, share, step, row_step = sizes
    rows_fn, aux, outs, gathered = rows
    total, own, kept, sent, arrived = buffers
    sum_sem, row_sem, keep_sem = sems
    steps = total.shape[1] // step
    if mp_size == 4:
        sums = sum_square(
            ready, parts_at, steps, step, peer, total, kept, sent, arrived, sum_sem
        )
    else:
        sums = sum_direct(
            ready, parts_at, steps, step, mp_size, peer, total, sent, arrived, sum_sem
        )

    def rows_at(r, carry):
        rows = pl.ds(pl.multiple_of(r * row_step, row_step), row_step)
        result = rows_fn(total[rows, :], rows, aux, outs)
        if gathered is not None:
            result = result.astype(BF16)
            if len(own.shape) == 2:
                own[rows, :] = result
            else:
                for t in range(steps):
                    own[t, rows, :] = result[:, t * step : (t + 1) * step]
        return carry

    for ref in outs:
        if ref.shape[0] == 8:
            ref[...] = jnp.zeros_like(ref)
    lax.fori_loop(0, share // row_step, rows_at, 0)
    if gathered is not None:
        first = own if len(own.shape) == 2 else own.at[0]
        keep = pltpu.make_async_copy(first, gathered.at[pl.ds(0, share)], keep_sem)
        keep.start()
        pass_on, finish = row_gather(first, gathered, mp_size, peer, row_sem)
        pass_on()
        finish()
        keep.wait()
    for copy in sums:
        copy.wait_send()


def row_plan(width, share, mp_size):
    step = 768 if width % 768 == 0 else width
    steps = width // step
    if mp_size == 4:
        pieces, kept = (steps, 2, 3, share, step // 2), (steps, 2, share, step // 2)
    else:
        pieces, kept = (steps, mp_size - 1, share, step), (8, LANES)
    buffers = [
        pltpu.VMEM((share, width), F32),
        pltpu.VMEM((share, width), BF16),
        pltpu.VMEM(kept, F32),
        pltpu.VMEM(pieces, BF16),
        pltpu.VMEM(pieces, BF16),
    ]
    sems = [
        pltpu.SemaphoreType.DMA((2, steps, max(4, mp_size - 1))),
        pltpu.SemaphoreType.DMA((2, max(6, mp_size))),
    ]
    return step, min(64, share), buffers, sems


def sum_rows(lefts, weight, rows_fn, aux, outs, gather, natural, mp_size, collective_id):
    span = lefts[0].shape[0]
    width, depth = weight.shape
    share = span // mp_size
    step, row_step, buffers, sems = row_plan(width, share, mp_size)
    plan = (mp_size, share, step, row_step, natural, len(lefts), len(aux), len(outs), gather)
    out_shape = [jax.ShapeDtypeStruct((rows, width), dtype) for rows, dtype in outs]
    out_specs = [pl.BlockSpec(memory_space=pltpu.VMEM)] * len(outs)
    if gather:
        out_shape.append(jax.ShapeDtypeStruct((span, width), BF16))
        out_specs.append(pl.BlockSpec(memory_space=pl.ANY))
    return pl.pallas_call(
        functools.partial(rows_kernel, plan, rows_fn),
        out_shape=out_shape,
        in_specs=[pl.BlockSpec(memory_space=pl.ANY)] * (len(lefts) + 1)
        + [pl.BlockSpec(memory_space=pltpu.VMEM)] * len(aux),
        out_specs=out_specs,
        scratch_shapes=[
            pltpu.VMEM((mp_size, share, depth), BF16),
            pltpu.VMEM((2, step, depth), BF16),
            *buffers,
            pltpu.SemaphoreType.DMA((2 + mp_size * len(lefts),)),
            *sems,
        ],
        compiler_params=pltpu.CompilerParams(
            collective_id=collective_id, has_side_effects=True, vmem_limit_bytes=VMEM_LIMIT
        ),
    )(*lefts, weight, *aux)


def weight_grad_kernel(plan, *refs):
    n_right, tile, half, first_column, n_into, steps, mp_size = plan
    left_ref, rights, refs = refs[0], refs[1 : 1 + n_right], refs[1 + n_right + n_into :]
    out_ref, refs = refs[0], refs[1:]
    if steps:
        steps_ref, gathered, refs = left_ref, refs[: len(steps)], refs[len(steps) :]
        own_rows, row_sems, refs = refs[0], refs[1 : 1 + len(steps)], refs[1 + len(steps) :]
        left_ref = gathered[0]
    left, right, sent, arrived, own, result, in_sem, swap_sem, out_sem = refs
    dp, seq, mp = lax.axis_index("dp"), lax.axis_index("seq"), lax.axis_index("mp")
    other = (1 - dp, seq, mp)

    def peer(k):
        return (dp, seq, flipped(mp, k))

    if steps:
        rows_load = pltpu.make_async_copy(
            steps_ref.at[pl.ds(steps[0], len(steps))], own_rows, in_sem.at[4]
        )
        rows_load.start()
    lefts = []
    for i, side in enumerate((1 - dp, dp)):
        columns = pl.ds(pl.multiple_of(side * half, LANES), half)
        lefts.append(pltpu.make_async_copy(left_ref.at[:, columns], left.at[i], in_sem.at[2 + i]))
    sources = []
    for ref in rights:
        for first in range(0, ref.shape[1], tile):
            sources.append(ref.at[:, pl.ds(first, tile)])
    tiles = len(sources)
    loads = [
        pltpu.make_async_copy(source, right.at[t % 2], in_sem.at[t % 2])
        for t, source in enumerate(sources)
    ]
    loads[0].start()
    barrier = pltpu.get_barrier_semaphore()
    pl.semaphore_signal(barrier, inc=1, device_id=other, device_id_type=MESH)
    if steps:
        for k in range(1, mp_size):
            pl.semaphore_signal(barrier, inc=1, device_id=peer(k), device_id_type=MESH)
    pl.semaphore_wait(barrier, mp_size if steps else 1)
    if steps:
        rows_load.wait()
        share = own_rows.shape[1]
        keeps = [
            pltpu.make_async_copy(own_rows.at[n], gathered[n].at[pl.ds(0, share)], in_sem.at[4 + n])
            for n in range(len(steps))
        ]
        for copy in keeps:
            copy.start()
        pass_on, end_rows = row_gather(own_rows.at[0], gathered[0], mp_size, peer, row_sems[0])
        pass_on()
        end_rows()
        keeps[0].wait()
        rest = [
            row_gather(own_rows.at[n], gathered[n], mp_size, peer, row_sems[n])
            for n in range(1, len(steps))
        ]
    for copy in lefts:
        copy.start()
    swaps, stores = [], []

    def finish(t):
        swaps[t].wait_recv()
        if t >= 2:
            stores[t - 2].wait()
        result[t % 2] = (own[t % 2] + arrived[t].astype(F32)).astype(BF16)
        stores.append(
            pltpu.make_async_copy(
                result.at[t % 2],
                out_ref.at[:, pl.ds(first_column + t * tile, tile)],
                out_sem.at[t % 2],
            )
        )
        stores[t].start()

    for t in range(tiles):
        loads[t].wait()
        if t + 1 < tiles:
            loads[t + 1].start()
        if t == 0:
            lefts[0].wait()
        sent[t] = dot_tn(left[0], right[t % 2]).astype(BF16)
        swaps.append(remote_copy(sent.at[t], arrived.at[t], swap_sem, (t,), other))
        if t == 0:
            lefts[1].wait()
        own[t % 2] = dot_tn(left[1], right[t % 2])
        if t >= 1:
            finish(t - 1)
        if t == tiles // 2 and steps:
            for pass_on, _ in rest:
                pass_on()
    finish(tiles - 1)
    for store in stores[-2:]:
        store.wait()
    for swap in swaps:
        swap.wait_send()
    if steps:
        for copy in keeps[1:]:
            copy.wait()
        for _, end_rows in rest:
            end_rows()


def weight_grad(left, rights, collective_id, into=None, columns=0, steps=(), mp_size=1):
    rows, width = rights[0].shape[0], left.shape[-1]
    half = width // 2
    total = sum(right.shape[1] for right in rights)
    tile = next(
        t
        for t in (768, 512, 384, 256, LANES)
        if total >= 2 * t and all(right.shape[1] % t == 0 for right in rights)
    )
    tiles = total // tile
    first = 0 if into is None else into.shape[1] - total
    earlier = () if into is None else (into,)
    out_shape = [jax.ShapeDtypeStruct((half, first + total + columns), BF16)]
    scratch = []
    if steps:
        out_shape += [jax.ShapeDtypeStruct((rows, width), BF16)] * len(steps)
        scratch = [pltpu.VMEM((len(steps), *left.shape[1:]), BF16)]
        scratch += [pltpu.SemaphoreType.DMA((2, max(6, mp_size)))] * len(steps)
    plan = (len(rights), tile, half, first, len(earlier), tuple(steps), mp_size)
    results = pl.pallas_call(
        functools.partial(weight_grad_kernel, plan),
        out_shape=out_shape,
        in_specs=[pl.BlockSpec(memory_space=pl.ANY)] * (1 + len(rights) + len(earlier)),
        out_specs=[pl.BlockSpec(memory_space=pl.ANY)] * len(out_shape),
        input_output_aliases={} if into is None else {1 + len(rights): 0},
        scratch_shapes=[
            *scratch,
            pltpu.VMEM((2, rows, half), BF16),
            pltpu.VMEM((2, rows, tile), BF16),
            pltpu.VMEM((tiles, half, tile), BF16),
            pltpu.VMEM((tiles, half, tile), BF16),
            pltpu.VMEM((2, half, tile), F32),
            pltpu.VMEM((2, half, tile), BF16),
            pltpu.SemaphoreType.DMA((4 + max(1, len(steps)),)),
            pltpu.SemaphoreType.DMA((2, tiles)),
            pltpu.SemaphoreType.DMA((2,)),
        ],
        compiler_params=pltpu.CompilerParams(
            collective_id=collective_id, has_side_effects=True, vmem_limit_bytes=VMEM_LIMIT
        ),
    )(left, *rights, *earlier)
    return results if steps else results[0]


def ffw_kernel(plan, normed_ref, gate_up_ref, shard_ref, resid_ref, cotangent_ref, gain_ref, *refs):
    mp_size, seq_size, share, step, row_step, tile = plan
    output_ref, gain_grad_ref, own_ref, dmixed_ref, hidden_ref, act_ref, slope_ref, down_ref = refs[:8]
    normed, gate_up, hidden, down, staged, *refs = refs[8:]
    buffers, refs = refs[:5], refs[5:]
    load_sem, store_sem, local_sem, line_sem, pair_sem, sum_sem, row_sem = refs
    steps, _, units = down.shape
    piece = step // (2 * seq_size)
    far = seq_size - 1
    dp, seq, mp = lax.axis_index("dp"), lax.axis_index("seq"), lax.axis_index("mp")
    sibling = (1 - dp, seq, mp)

    def peer(k):
        return (dp, seq, flipped(mp, k))

    def block(t, at):
        first = pl.multiple_of((dp * seq_size + at) * piece, piece)
        return down.at[t, pl.ds(first, piece)]

    start, share_piece, arrival, complete, drain = travel(block, line_sem, pair_sem, seq_size)
    normed_load = pltpu.make_async_copy(normed_ref, normed, local_sem.at[0])
    normed_load.start()
    shard_loads = [
        pltpu.make_async_copy(
            shard_ref.at[pl.ds(t * piece, piece)], block(t, seq), local_sem.at[1 + t]
        )
        for t in range(steps)
    ]
    for load in shard_loads:
        load.start()

    def loads(i, slot):
        return [
            pltpu.make_async_copy(
                gate_up_ref.at[:, pl.ds(pl.multiple_of(side * units + i * tile, LANES), tile)],
                gate_up.at[slot, side],
                load_sem.at[slot, side],
            )
            for side in range(2)
        ]

    def stores(i, slot):
        columns = pl.ds(pl.multiple_of(i * tile, LANES), tile)
        return [
            pltpu.make_async_copy(staged.at[slot, 0], act_ref.at[:, columns], store_sem.at[slot, 0]),
            pltpu.make_async_copy(staged.at[slot, 1], slope_ref.at[:, columns], store_sem.at[slot, 1]),
        ]

    for load in loads(0, 0):
        load.start()
    barrier = pltpu.get_barrier_semaphore()
    for k in range(1, mp_size):
        pl.semaphore_signal(barrier, inc=1, device_id=peer(k), device_id_type=MESH)
    pl.semaphore_signal(barrier, inc=1, device_id=sibling, device_id_type=MESH)
    for way in range(2):
        @pl.when(seq < far if way == 0 else seq > 0)
        def _(way=way):
            pl.semaphore_signal(
                barrier, inc=1, device_id=(dp, seq + 1 - 2 * way, mp), device_id_type=MESH
            )

    line_peers = (seq + far) // seq_size + (2 * far - seq) // seq_size
    pl.semaphore_wait(barrier, mp_size + line_peers)

    for t in range(steps):
        shard_loads[t].wait()
        start(t)
    for t in range(steps):
        share_piece(t)
    normed_load.wait()
    arrivals = [(t, distance) for distance in range(1, seq_size) for t in range(steps)]
    tiles = units // tile
    early = [(2 * n + 2, event) for n, event in enumerate(arrivals) if 2 * n + 2 < tiles]
    late = arrivals[len(early) :]

    def units_at(i, carry):
        slot = lax.rem(i, 2)
        for load in loads(i, slot):
            load.wait()

        @pl.when(i + 1 < tiles)
        def _():
            for load in loads(i + 1, 1 - slot):
                load.start()

        @pl.when(i >= 2)
        def _():
            for store in stores(i - 2, slot):
                store.wait()

        gate = dot_nn(normed[...], gate_up[slot, 0])
        up = dot_nn(normed[...], gate_up[slot, 1])
        squared = gate * gate
        bend = jnp.tanh(GELU_SCALE * gate * (1.0 + GELU_CUBE * squared))
        side = 0.5 * (1.0 + bend)
        act = gate * side
        slope = side + (0.5 * GELU_SCALE) * gate * (1.0 - bend * bend) * (1.0 + 3.0 * GELU_CUBE * squared)
        staged[slot, 0] = act.astype(BF16)
        staged[slot, 1] = (slope * up).astype(BF16)
        for store in stores(i, slot):
            store.start()
        product = (act * up).astype(BF16)
        for k in range(mp_size):
            hidden[k, :, pl.ds(pl.multiple_of(i * tile, LANES), tile)] = product[
                k * share : (k + 1) * share
            ]
        for at, event in early:
            @pl.when(i == at)
            def _(event=event):
                arrival(*event)

        return carry

    lax.fori_loop(0, tiles, units_at, 0)
    for i in range(max(0, tiles - 2), tiles):
        for store in stores(i, i % 2):
            store.wait()
    hidden_stores = [
        pltpu.make_async_copy(hidden.at[k], hidden_ref.at[pl.ds(k * share, share)], local_sem.at[1 + k])
        for k in range(mp_size)
    ]
    for store in hidden_stores:
        store.start()
    down_stores = [
        pltpu.make_async_copy(
            down.at[t], down_ref.at[pl.ds(t * step, step)], local_sem.at[1 + mp_size + t]
        )
        for t in range(steps)
    ]
    waiting = list(late)

    def ready(t):
        while (t, far) in waiting:
            arrival(*waiting.pop(0))
        complete(t)
        down_stores[t].start()

    def parts_at(t, k):
        return dot_nt(hidden[k], down[t])

    finish_rows(
        ready,
        parts_at,
        (mp_size, share, step, row_step),
        (after_ffw, (resid_ref, cotangent_ref, gain_ref), (output_ref, gain_grad_ref), dmixed_ref),
        peer,
        buffers,
        (sum_sem, row_sem, local_sem.at[0]),
    )
    own_store = pltpu.make_async_copy(buffers[1], own_ref, local_sem.at[0])
    own_store.start()
    for store in hidden_stores + down_stores:
        store.wait()
    own_store.wait()
    for t in range(steps):
        drain(t)


def ffw(normed, gate_up_w, down_shard, resid, cotangent, gain, sizes, collective_id):
    dp_size, seq_size, mp_size = sizes
    span, width = normed.shape
    units = gate_up_w.shape[1] // 2
    share = span // mp_size
    step, row_step, buffers, sems = row_plan(width, share, mp_size)
    steps = width // step
    buffers[1] = pltpu.VMEM((steps, share, step), BF16)
    tile = 256 if units % 256 == 0 else LANES
    plan = (mp_size, seq_size, share, step, row_step, tile)
    per_unit = jax.ShapeDtypeStruct((span, units), BF16)
    return pl.pallas_call(
        functools.partial(ffw_kernel, plan),
        out_shape=(
            jax.ShapeDtypeStruct((share, width), BF16),
            jax.ShapeDtypeStruct((8, width), F32),
            jax.ShapeDtypeStruct((steps, share, step), BF16),
            jax.ShapeDtypeStruct((span, step), BF16),
            per_unit,
            per_unit,
            per_unit,
            jax.ShapeDtypeStruct((width, units), BF16),
        ),
        in_specs=[pl.BlockSpec(memory_space=pl.ANY)] * 3 + [pl.BlockSpec(memory_space=pltpu.VMEM)] * 3,
        out_specs=(pl.BlockSpec(memory_space=pltpu.VMEM),) * 2 + (pl.BlockSpec(memory_space=pl.ANY),) * 6,
        scratch_shapes=[
            pltpu.VMEM((span, width), BF16),
            pltpu.VMEM((2, 2, width, tile), BF16),
            pltpu.VMEM((mp_size, share, units), BF16),
            pltpu.VMEM((steps, step, units), BF16),
            pltpu.VMEM((2, 2, span, tile), BF16),
            *buffers,
            pltpu.SemaphoreType.DMA((2, 2)),
            pltpu.SemaphoreType.DMA((2, 2)),
            pltpu.SemaphoreType.DMA((1 + mp_size + steps,)),
            pltpu.SemaphoreType.DMA((2, steps, 2, seq_size)),
            pltpu.SemaphoreType.DMA((2, steps, 2, seq_size)),
            *sems,
        ],
        compiler_params=pltpu.CompilerParams(
            collective_id=collective_id, has_side_effects=True, vmem_limit_bytes=VMEM_LIMIT
        ),
    )(normed, gate_up_w, down_shard, resid, cotangent, gain)


def hidden_back_kernel(n_parts, *refs):
    parts, (down_ref, act_ref, slope_ref, dgate_ref, dup_ref) = refs[:n_parts], refs[n_parts:]
    first, dhidden = 0, 0.0
    for part in parts:
        depth = part.shape[1]
        dhidden = dhidden + dot_nn(part[...], down_ref[first : first + depth, :])
        first += depth
    dgate_ref[...] = (dhidden * slope_ref[...].astype(F32)).astype(BF16)
    dup_ref[...] = (dhidden * act_ref[...].astype(F32)).astype(BF16)


def hidden_back(dmixed, down_wt, act, slope):
    rows, depth = dmixed[0].shape
    width, units = down_wt.shape
    tile = 256 if units % 256 == 0 else units
    columns = pl.BlockSpec((rows, tile), lambda i: (0, i))
    return pl.pallas_call(
        functools.partial(hidden_back_kernel, len(dmixed)),
        grid=(units // tile,),
        out_shape=(jax.ShapeDtypeStruct((rows, units), BF16),) * 2,
        in_specs=[pl.BlockSpec((rows, depth), lambda i: (0, 0))] * len(dmixed)
        + [pl.BlockSpec((width, tile), lambda i: (0, i)), columns, columns],
        out_specs=(columns, columns),
        compiler_params=pltpu.CompilerParams(vmem_limit_bytes=VMEM_LIMIT),
    )(*dmixed, down_wt, act, slope)


def fold_rows(x):
    return jnp.sum(x.reshape(x.shape[0] // 8, 8, x.shape[1]), axis=0)


def after_attention(attn, rows, aux, outs):
    tokens, gain_two, gain_three = aux
    attn_out, resid_out = outs
    resid = tokens[rows, :].astype(F32) + attn * rms_scale(attn) * gain_two[...]
    attn_out[rows, :] = attn
    resid_out[rows, :] = resid
    return resid * rms_scale(resid) * gain_three[...]


def after_ffw(mixed, rows, aux, outs):
    resid, cotangent, gain_four = aux
    output, gain_grad = outs
    scale = rms_scale(mixed)
    unit = mixed * scale
    grad_out = cotangent[rows, :].astype(F32)
    output[rows, :] = (resid[rows, :] + unit * gain_four[...]).astype(BF16)
    gain_grad[...] += fold_rows(grad_out * unit)
    return vector_back(grad_out, unit, scale, gain_four[...])


def vector_back(grad_in, unit, scale, gain):
    unit_grad = grad_in * gain
    return scale * (unit_grad - unit * jnp.mean(unit_grad * unit, axis=-1, keepdims=True))


def before_ffw(dnormed_two, rows, aux, outs):
    resid, attn, cotangent, gain_two, gain_three = aux
    dresid_out, gain_two_grad, gain_three_grad = outs
    scale = rms_scale(resid[rows, :])
    unit = resid[rows, :] * scale
    gain_three_grad[...] += fold_rows(dnormed_two * unit)
    dresid = cotangent[rows, :].astype(F32) + vector_back(dnormed_two, unit, scale, gain_three[...])
    dresid_out[rows, :] = dresid
    scale = rms_scale(attn[rows, :])
    unit = attn[rows, :] * scale
    gain_two_grad[...] += fold_rows(dresid * unit)
    return vector_back(dresid, unit, scale, gain_two[...])


def before_attention(dnormed_one, rows, aux, outs):
    tokens, dresid, gain_one = aux
    tokens_grad, gain_grad = outs
    vector = tokens[rows, :].astype(F32)
    scale = rms_scale(vector)
    unit = vector * scale
    gain_grad[...] += fold_rows(dnormed_one * unit)
    back = vector_back(dnormed_one, unit, scale, gain_one[...])
    tokens_grad[rows, :] = (dresid[rows, :] + back).astype(BF16)


def swapped(x, axis, k):
    return lax.ppermute(x, axis, [(i, i ^ k) for i in range(lax.axis_size(axis))])


def shards(
    tokens,
    cotangent,
    pre_attn_gain,
    w_query,
    w_key,
    w_value,
    w_out,
    post_attn_gain,
    pre_ffw_gain,
    w_gate,
    w_up,
    w_down,
    post_ffw_gain,
):
    dp_size, seq_size, mp_size = (lax.axis_size(axis) for axis in ("dp", "seq", "mp"))
    dp, seq, mp = lax.axis_index("dp"), lax.axis_index("seq"), lax.axis_index("mp")
    both = ("dp", "seq")
    heads = w_query.shape[1] // HEAD_DIM
    q_width = heads * HEAD_DIM
    span = tokens.shape[1]
    width = tokens.shape[2]
    share = span // mp_size
    plan = attention_plan(span, seq_size)

    def gather_weight(x):
        return lax.all_gather(x, both, axis=0, tiled=True)

    sizes = (dp_size, seq_size, mp_size)
    gain_rows, own_pair, cosine, sine, normed_one, w_qkv = front(
        tokens[0],
        w_query,
        w_key,
        w_value,
        [pre_attn_gain, post_attn_gain, pre_ffw_gain, post_ffw_gain],
        heads,
        sizes,
    )
    gain_one, gain_two, gain_three, gain_four = (gain_rows[i : i + 1, :width] for i in range(4))
    pairs = lax.all_gather(own_pair, "seq", axis=0, tiled=True)
    w_out_t = carry(after(w_out.T, own_pair), sizes, 30)
    query_lin = dot_nn(after(normed_one, pairs), w_qkv[:, :q_width]).reshape(span, heads, HEAD_DIM)
    queries = rotary(query_lin, cosine[:, None], sine[:, None], 1.0) * HEAD_DIM ** (-0.5)
    queries = queries.astype(BF16).reshape(span, q_width)

    units = w_gate.shape[1]
    gate_up_w = gather_weight(after(jnp.concatenate([w_gate, w_up], axis=1), pairs, w_out_t))

    attn_o, attn_exact, lse = attend(queries, pairs, plan)
    own_first = mp * share
    tokens_own = lax.dynamic_slice_in_dim(tokens[0], own_first, share, 0)
    cotangent_own = lax.dynamic_slice_in_dim(cotangent[0], own_first, share, 0)

    def by_owner(x):
        return jnp.concatenate(
            [lax.dynamic_slice_in_dim(x, (mp ^ k) * share, share, 0) for k in range(mp_size)], axis=0
        )

    attn, resid, normed_two = sum_rows(
        (attn_o,),
        w_out_t,
        after_attention,
        (tokens_own, gain_two, gain_three),
        ((share, F32), (share, F32)),
        True,
        True,
        mp_size,
        3,
    )
    shard_count = dp_size * seq_size
    steps = width // row_plan(width, share, mp_size)[0]

    def to_steps(x):
        return jnp.swapaxes(x.reshape(x.shape[0], shard_count, steps, -1), 1, 2).reshape(x.shape)

    def to_shards(x):
        return jnp.swapaxes(x.reshape(x.shape[0], steps, shard_count, -1), 1, 2).reshape(x.shape)

    output, grad_gain_four, dmixed_own, dmixed_first, hidden, gate_act, slope, down_wt = ffw(
        normed_two,
        gate_up_w,
        w_down.T,
        to_steps(resid),
        to_steps(cotangent_own),
        to_steps(gain_four),
        sizes,
        4,
    )
    output = to_shards(output)
    grad_gain_four = to_shards(grad_gain_four)

    def spread(x):
        return lax.psum_scatter(x, "seq", scatter_dimension=0, tiled=True)

    grad_sums = [weight_grad(dmixed_first, (hidden,), 20)]
    grad_sum, *arrived = weight_grad(
        after(dmixed_own, grad_sums[0]),
        (hidden,),
        21,
        columns=units * (steps - 2),
        steps=tuple(range(1, steps)),
        mp_size=mp_size,
    )
    for t in range(2, steps):
        grad_sum = weight_grad(
            arrived[t - 1], (hidden,), 20 + t, into=grad_sum, columns=units * (steps - 1 - t)
        )
    grad_sums.append(grad_sum)
    dmixed_low = [dmixed_first, *arrived]
    grad_down_first = spread(grad_sums[0])
    grad_down_rest = spread(after(grad_sums[-1], grad_down_first))
    grad_down = [grad_down_first] + [
        grad_down_rest[:, t * units : (t + 1) * units] for t in range(steps - 1)
    ]
    grad_down = jnp.concatenate(grad_down, axis=0).astype(F32).T
    dgate_low, dup_low = hidden_back(
        (after(dmixed_low[0], grad_sum), *dmixed_low[1:]), down_wt, gate_act, slope
    )
    grad_gate_up_sum = weight_grad(normed_two, (dgate_low, dup_low), 8)
    dresid, grad_gain_two, grad_gain_three, dattn_low = sum_rows(
        (after(dgate_low, grad_down_rest, grad_gate_up_sum), dup_low),
        gate_up_w,
        before_ffw,
        (resid, attn, cotangent_own, gain_two, gain_three),
        ((share, F32), (8, F32), (8, F32)),
        True,
        False,
        mp_size,
        5,
    )
    grad_gate_up = spread(after(grad_gate_up_sum, grad_down_rest))

    dattn_o = by_owner(dot_nn(dattn_low, w_out_t)).astype(BF16)
    dquery, dpairs = attend_back(queries, dattn_o, attn_exact, lse, pairs, plan)
    grad_out_sum = weight_grad(dattn_low, (by_owner(attn_o),), 9)
    dquery = dquery.reshape(span, heads, HEAD_DIM)
    dquery_low = (
        rotary(dquery * HEAD_DIM ** (-0.5), cosine[:, None], sine[:, None], -1.0).reshape(span, q_width).astype(BF16)
    )
    grad_q_sum = weight_grad(normed_one, (dquery_low,), 10, columns=2 * HEAD_DIM)
    own_grads = spread(after(dpairs, grad_gate_up, grad_out_sum, grad_q_sum)).astype(F32)
    grad_gate = grad_gate_up[:, :units].astype(F32)
    grad_up = grad_gate_up[:, units:].astype(F32)
    own_grads = after(own_grads, grad_gate, grad_up, grad_down)
    dkey_rot = own_grads[:, :HEAD_DIM]
    dkey_low = rotary(dkey_rot, cosine, sine, -1.0).astype(BF16)
    dvalue_low = own_grads[:, HEAD_DIM:].astype(BF16)
    dkv_low = jnp.concatenate([dkey_low, dvalue_low], axis=1)
    grad_qkv_sum = weight_grad(normed_one, (dkv_low,), 11, into=grad_q_sum)
    grad_qkv = spread(grad_qkv_sum)
    tokens_grad, grad_gain_one = sum_rows(
        (dquery_low, after(dkv_low, grad_qkv_sum)),
        w_qkv,
        before_attention,
        (tokens_own, dresid, gain_one),
        ((share, BF16), (8, F32)),
        False,
        True,
        mp_size,
        6,
    )

    grad_out_t = spread(after(grad_out_sum, grad_qkv, tokens_grad))
    gain_grads, grad_key, grad_value = last_sums(
        [
            jnp.sum(grad, axis=0)
            for grad in (grad_gain_one, grad_gain_two, grad_gain_three, grad_gain_four)
        ],
        grad_qkv[:, q_width:],
        w_key.shape[1],
        heads,
        sizes,
    )
    return (
        output[None],
        tokens_grad[None],
        gain_grads[0],
        after(grad_qkv, grad_key)[:, :q_width].astype(F32),
        grad_key,
        grad_value,
        grad_out_t.astype(F32).T,
        gain_grads[1],
        gain_grads[2],
        grad_gate,
        grad_up,
        grad_down,
        gain_grads[3],
    )


def solution(mesh):
    weight = P(("dp", "seq"), "mp")
    whole_rows = P(("dp", "seq"), None)
    columns = P("mp", ("dp", "seq"))
    gain = P(("dp", "seq"))
    tokens = P("dp", "seq", None)
    rows = P("dp", ("seq", "mp"), None)
    in_specs = (
        tokens,
        tokens,
        gain,
        weight,
        whole_rows,
        whole_rows,
        columns,
        gain,
        gain,
        weight,
        weight,
        columns,
        gain,
    )
    out_specs = (
        rows,
        rows,
        gain,
        weight,
        whole_rows,
        whole_rows,
        columns,
        gain,
        gain,
        weight,
        weight,
        columns,
        gain,
    )
    return jax.shard_map(shards, mesh=mesh, in_specs=in_specs, out_specs=out_specs, check_vma=False)
```

```python
import functools

import jax
import jax.numpy as jnp
import numpy as np
from jax import lax
from jax.experimental import pallas as pl
from jax.experimental.pallas import tpu as pltpu
from jax.sharding import PartitionSpec as P

Q_HEADS = 8
KV_HEADS = 4
HEAD_DIM = 256
WINDOW = 4096

EPSILON = 1e-06
SOFT_CAP = 50.0
ROPE_BASE = 10000.0
GELU_SCALE = (2.0 / 3.141592653589793) ** 0.5
GELU_CUBE = 0.044715
MESH = pl.DeviceIdType.MESH
VMEM_LIMIT = 56 * 1024 * 1024
LANES = 128
BF16 = jnp.bfloat16
F32 = jnp.float32


def after(value, *earlier):
    return lax.optimization_barrier((value, *earlier))[0]


def dot_nn(left, right):
    return lax.dot_general(left, right, (((1,), (0,)), ((), ())), preferred_element_type=F32)


def dot_nt(left, right):
    return lax.dot_general(left, right, (((1,), (1,)), ((), ())), preferred_element_type=F32)


def dot_tn(left, right):
    return lax.dot_general(left, right, (((0,), (0,)), ((), ())), preferred_element_type=F32)


def rms_scale(vector):
    return lax.rsqrt(jnp.mean(vector * vector, axis=-1, keepdims=True) + EPSILON)


def rotary(vector, cosine, sine, direction):
    half_dim = vector.shape[-1] // 2
    first_half = vector[..., :half_dim]
    second_half = vector[..., half_dim:]
    return jnp.concatenate(
        [
            first_half * cosine - direction * (second_half * sine),
            second_half * cosine + direction * (first_half * sine),
        ],
        axis=-1,
    )


def flipped(index, k):
    result, bit = index, 1
    while bit <= k:
        if k & bit:
            result = result + bit * (1 - 2 * lax.rem(index // bit, 2))
        bit *= 2
    return result


def last_kernel(
    sizes, heads, x_ref, kv_ref, o_ref, key_ref, value_ref, mine, from_mp, from_ws, kv_from, sems, kv_sem
):
    dp_size, seq_size, mp_size = sizes
    count = dp_size * seq_size
    dp, seq, mp = lax.axis_index("dp"), lax.axis_index("seq"), lax.axis_index("mp")
    rank = dp * seq_size + seq

    def mp_peer(k):
        return (dp, seq, flipped(mp, k))

    def ws_rank(k):
        return lax.rem(rank + k, count)

    def ws_peer(k):
        other = ws_rank(k)
        return (other // seq_size, lax.rem(other, seq_size), mp)

    def remote(src, dst, kind, k, device):
        copy = pltpu.make_async_remote_copy(
            src_ref=src,
            dst_ref=dst,
            send_sem=sems.at[kind, 0, k],
            recv_sem=sems.at[kind, 1, k],
            device_id=device,
            device_id_type=MESH,
        )
        copy.start()
        return copy

    barrier = pltpu.get_barrier_semaphore()
    for k in range(1, mp_size):
        pl.semaphore_signal(barrier, inc=1, device_id=mp_peer(k), device_id_type=MESH)
    for k in range(1, count):
        pl.semaphore_signal(barrier, inc=1, device_id=ws_peer(k), device_id_type=MESH)
    pl.semaphore_wait(barrier, mp_size - 1 + count - 1)
    copies = [remote(x_ref.at[ws_rank(k)], from_ws.at[k], 0, k, ws_peer(k)) for k in range(1, count)]
    pass_on, end_rows = row_gather(kv_ref, kv_from, mp_size, mp_peer, kv_sem)
    key_ref[...] = jnp.zeros_like(key_ref)
    value_ref[...] = jnp.zeros_like(value_ref)
    for copy in copies:
        copy.wait()
    total = x_ref[pl.ds(rank, 1)][0]
    for k in range(1, count):
        total = total + from_ws[k]
    mine[...] = total
    copies = [remote(mine, from_mp.at[k], 1, k, mp_peer(k)) for k in range(1, mp_size)]
    pass_on()
    for copy in copies:
        copy.wait()
    for k in range(1, mp_size):
        total = total + from_mp[k]
    o_ref[...] = total
    end_rows()
    rows = kv_ref.shape[0]
    for k in range(mp_size):
        piece = (kv_from[k * rows : (k + 1) * rows, :] if k else kv_ref[...]).astype(F32)
        head = flipped(mp, k) * heads // (Q_HEADS // KV_HEADS)
        columns = pl.ds(pl.multiple_of(head * HEAD_DIM, HEAD_DIM), HEAD_DIM)
        key_ref[:, columns] = (key_ref[:, columns].astype(F32) + piece[:, :HEAD_DIM]).astype(BF16)
        value_ref[:, columns] = (value_ref[:, columns].astype(F32) + piece[:, HEAD_DIM:]).astype(BF16)


def last_sums(grads, kv, kv_width, heads, sizes):
    dp_size, seq_size, mp_size = sizes
    count = dp_size * seq_size
    local = grads[0].shape[0] // count
    width = -(-local // LANES) * LANES
    block = jnp.transpose(jnp.stack(grads).reshape(len(grads), count, local), (1, 0, 2))
    block = jnp.pad(block, ((0, 0), (0, 8 - len(grads)), (0, width - local)))
    kv_out = jax.ShapeDtypeStruct((kv.shape[0], kv_width), BF16)
    total, key, value = pl.pallas_call(
        functools.partial(last_kernel, sizes, heads),
        out_shape=(jax.ShapeDtypeStruct((8, width), F32), kv_out, kv_out),
        in_specs=[pl.BlockSpec(memory_space=pltpu.VMEM)] * 2,
        out_specs=(pl.BlockSpec(memory_space=pltpu.VMEM),) * 3,
        scratch_shapes=[
            pltpu.VMEM((8, width), F32),
            pltpu.VMEM((mp_size, 8, width), F32),
            pltpu.VMEM((count, 8, width), F32),
            pltpu.VMEM((mp_size * kv.shape[0], kv.shape[1]), BF16),
            pltpu.SemaphoreType.DMA((2, 2, max(count, mp_size))),
            pltpu.SemaphoreType.DMA((2, max(6, mp_size))),
        ],
        compiler_params=pltpu.CompilerParams(
            collective_id=2, has_side_effects=True, vmem_limit_bytes=VMEM_LIMIT
        ),
    )(block, kv)
    return [total[i, :local] for i in range(len(grads))], key, value


def travel(block, line_sem, pair_sem, seq_size):
    far = seq_size - 1
    dp, seq, mp = lax.axis_index("dp"), lax.axis_index("seq"), lax.axis_index("mp")

    def goes_on(way):
        return seq < far if way == 0 else seq > 0

    def comes(way, distance):
        return seq >= distance if way == 0 else seq + distance <= far

    def piece(t, way, distance, sems, device):
        place = block(t, seq - distance if way == 0 else seq + distance)
        return pltpu.make_async_remote_copy(
            src_ref=place,
            dst_ref=place,
            send_sem=sems.at[0, t, way, distance],
            recv_sem=sems.at[1, t, way, distance],
            device_id=device,
            device_id_type=MESH,
        )

    def line(t, way, distance):
        return piece(t, way, distance, line_sem, (dp, seq + 1 - 2 * way, mp))

    def pair(t, way, distance):
        return piece(t, way, distance, pair_sem, (1 - dp, seq, mp))

    def start(t):
        for way in range(2):
            @pl.when(goes_on(way))
            def _(way=way):
                line(t, way, 0).start()

    def share(t):
        pair(t, 0, 0).start()

    def arrival(t, distance):
        for way in range(2):
            @pl.when(comes(way, distance))
            def _(way=way):
                line(t, way, distance - 1).wait_recv()
                if distance < far:
                    @pl.when(goes_on(way))
                    def _():
                        line(t, way, distance).start()

                pair(t, way, distance).start()

    def complete(t):
        pair(t, 0, 0).wait_recv()
        for way in range(2):
            for distance in range(1, seq_size):
                @pl.when(comes(way, distance))
                def _(way=way, distance=distance):
                    pair(t, way, distance).wait_recv()

    def drain(t):
        pair(t, 0, 0).wait_send()
        for way in range(2):
            for distance in range(far):
                @pl.when(goes_on(way) & comes(way, distance))
                def _(way=way, distance=distance):
                    line(t, way, distance).wait_send()

            for distance in range(1, seq_size):
                @pl.when(comes(way, distance))
                def _(way=way, distance=distance):
                    pair(t, way, distance).wait_send()

    return start, share, arrival, complete, drain


def window(rank, local):
    return rank * local // LANES * LANES


def window_width(count, local):
    widest = max(rank * local - window(rank, local) for rank in range(count)) + local
    return -(-widest // LANES) * LANES


def front_kernel(plan, tokens_ref, wq_ref, wk_ref, wv_ref, gains_ref, frequency_ref, *refs):
    dp_size, seq_size, heads, pieces, row_step = plan
    gain_rows, pair_ref, cosine_ref, sine_ref, normed_ref, w_qkv_ref = refs[:6]
    tokens, normed, w_qkv, gains, refs = *refs[6:10], refs[10:]
    load_sem, gain_sem, line_sem, pair_sem, store_sem = refs
    count = dp_size * seq_size
    span, width = tokens.shape
    shard, q_width = wq_ref.shape
    dp, seq, mp = lax.axis_index("dp"), lax.axis_index("seq"), lax.axis_index("mp")
    rank = dp * seq_size + seq

    def peer(k):
        other = lax.rem(rank + k, count)
        return (other // seq_size, lax.rem(other, seq_size), mp)

    own = pl.ds(pl.multiple_of(rank * shard, 16), shard)
    head = pl.ds(pl.multiple_of(mp * heads // (Q_HEADS // KV_HEADS) * HEAD_DIM, HEAD_DIM), HEAD_DIM)
    loads = [
        pltpu.make_async_copy(wq_ref, w_qkv.at[own, pl.ds(0, q_width)], load_sem.at[0]),
        pltpu.make_async_copy(wk_ref.at[:, head], w_qkv.at[own, pl.ds(q_width, HEAD_DIM)], load_sem.at[1]),
        pltpu.make_async_copy(
            wv_ref.at[:, head], w_qkv.at[own, pl.ds(q_width + HEAD_DIM, HEAD_DIM)], load_sem.at[2]
        ),
        pltpu.make_async_copy(tokens_ref, tokens, load_sem.at[3]),
    ]
    for load in loads:
        load.start()
    barrier = pltpu.get_barrier_semaphore()
    for k in range(1, count):
        pl.semaphore_signal(barrier, inc=1, device_id=peer(k), device_id_type=MESH)
    pl.semaphore_wait(barrier, count - 1)

    def block(t, at):
        piece = shard // pieces
        first = (dp * seq_size + at) * shard
        return w_qkv.at[pl.ds(pl.multiple_of(first + t * piece, 16), piece)]

    start, share, arrival, complete, drain = travel(block, line_sem, pair_sem, seq_size)
    for load in loads[:3]:
        load.wait()
    gain_copies = [remote_copy(gains_ref, gains.at[rank], gain_sem, (k,), peer(k)) for k in range(1, count)]
    for t in range(pieces):
        start(t)
    for t in range(pieces):
        share(t)
    position = seq * span + lax.broadcasted_iota(jnp.int32, cosine_ref.shape, 0)
    angle = position.astype(F32) * frequency_ref[0:1, :]
    cosine_ref[...] = jnp.cos(angle)
    sine_ref[...] = jnp.sin(angle)
    gains[pl.ds(rank, 1)] = gains_ref[...][None]
    gain_rows[...] = jnp.zeros_like(gain_rows)
    for copy in gain_copies:
        copy.wait()
    for r in range(count):
        first = window(r, shard)
        gain_rows[:, first : first + gains.shape[2]] += gains[r]
    loads[3].wait()

    def norm_rows(r, carry):
        rows = pl.ds(pl.multiple_of(r * row_step, row_step), row_step)
        vector = tokens[rows, :].astype(F32)
        normed[rows, :] = (vector * rms_scale(vector) * gain_rows[0:1, :]).astype(BF16)
        return carry

    blocks = span // row_step
    for t in range(pieces):
        lax.fori_loop(blocks * t // pieces, blocks * (t + 1) // pieces, norm_rows, 0)
        arrival(t, 1)
    for distance in range(2, seq_size):
        for t in range(pieces):
            arrival(t, distance)
    for t in range(pieces):
        complete(t)
    stores = [
        pltpu.make_async_copy(w_qkv, w_qkv_ref, store_sem.at[0]),
        pltpu.make_async_copy(normed, normed_ref, store_sem.at[1]),
    ]
    for store in stores:
        store.start()

    def project(first):
        return dot_nn(normed[...], w_qkv[:, first : first + HEAD_DIM])

    key = rotary(project(q_width), cosine_ref[...], sine_ref[...], 1.0)
    pair_ref[:, :HEAD_DIM] = key.astype(BF16)
    pair_ref[:, HEAD_DIM:] = project(q_width + HEAD_DIM).astype(BF16)
    for store in stores:
        store.wait()
    for t in range(pieces):
        drain(t)


def front(tokens, w_query, w_key, w_value, gains, heads, sizes):
    dp_size, seq_size, _ = sizes
    count = dp_size * seq_size
    span, width = tokens.shape
    shard, q_width = w_query.shape
    columns = q_width + 2 * HEAD_DIM
    half_dim = HEAD_DIM // 2
    pieces = 3
    lanes = window_width(count, shard)
    offset = (lax.axis_index("dp") * seq_size + lax.axis_index("seq")) * shard % LANES
    block = jnp.concatenate(gains).reshape(len(gains), shard).astype(F32)
    block = jnp.pad(block, ((0, 8 - len(gains)), (0, 0)))
    block = lax.dynamic_update_slice_in_dim(jnp.zeros((8, lanes), F32), block, offset, 1)
    frequency = ROPE_BASE ** (-np.arange(half_dim) * 2.0 / HEAD_DIM)
    frequency = jnp.asarray(np.tile(frequency.astype(np.float32), (8, 1)))
    plan = (dp_size, seq_size, heads, pieces, min(32, span))
    return pl.pallas_call(
        functools.partial(front_kernel, plan),
        out_shape=(
            jax.ShapeDtypeStruct((8, max(width, window(count - 1, shard) + lanes)), F32),
            jax.ShapeDtypeStruct((span, 2 * HEAD_DIM), BF16),
            jax.ShapeDtypeStruct((span, half_dim), F32),
            jax.ShapeDtypeStruct((span, half_dim), F32),
            jax.ShapeDtypeStruct((span, width), BF16),
            jax.ShapeDtypeStruct((width, columns), BF16),
        ),
        in_specs=[pl.BlockSpec(memory_space=pl.ANY)] * 4 + [pl.BlockSpec(memory_space=pltpu.VMEM)] * 2,
        out_specs=(pl.BlockSpec(memory_space=pltpu.VMEM),) * 4 + (pl.BlockSpec(memory_space=pl.ANY),) * 2,
        scratch_shapes=[
            pltpu.VMEM((span, width), BF16),
            pltpu.VMEM((span, width), BF16),
            pltpu.VMEM((width, columns), BF16),
            pltpu.VMEM((count, 8, lanes), F32),
            pltpu.SemaphoreType.DMA((4,)),
            pltpu.SemaphoreType.DMA((2, count)),
            pltpu.SemaphoreType.DMA((2, pieces, 2, seq_size)),
            pltpu.SemaphoreType.DMA((2, pieces, 2, seq_size)),
            pltpu.SemaphoreType.DMA((2,)),
        ],
        compiler_params=pltpu.CompilerParams(
            collective_id=1, has_side_effects=True, vmem_limit_bytes=VMEM_LIMIT
        ),
    )(tokens, w_query, w_key, w_value, block, frequency)


def carry_kernel(seq_size, shard_ref, full_ref, load_sem, line_sem, pair_sem):
    dp, seq, mp = lax.axis_index("dp"), lax.axis_index("seq"), lax.axis_index("mp")
    far = seq_size - 1
    shard = shard_ref.shape[0]

    def block(t, at):
        first = pl.multiple_of((dp * seq_size + at) * shard, 16)
        return full_ref.at[pl.ds(first, shard)]

    load = pltpu.make_async_copy(shard_ref, block(0, seq), load_sem)
    load.start()
    barrier = pltpu.get_barrier_semaphore()
    pl.semaphore_signal(barrier, inc=1, device_id=(1 - dp, seq, mp), device_id_type=MESH)
    for way in range(2):
        @pl.when(seq < far if way == 0 else seq > 0)
        def _(way=way):
            pl.semaphore_signal(
                barrier, inc=1, device_id=(dp, seq + 1 - 2 * way, mp), device_id_type=MESH
            )

    pl.semaphore_wait(barrier, 1 + (seq + far) // seq_size + (2 * far - seq) // seq_size)
    load.wait()
    start, share, arrival, complete, drain = travel(block, line_sem, pair_sem, seq_size)
    start(0)
    share(0)
    for distance in range(1, seq_size):
        arrival(0, distance)
    complete(0)
    drain(0)


def carry(shard, sizes, collective_id):
    dp_size, seq_size, _ = sizes
    return pl.pallas_call(
        functools.partial(carry_kernel, seq_size),
        out_shape=jax.ShapeDtypeStruct((shard.shape[0] * dp_size * seq_size, shard.shape[1]), BF16),
        in_specs=[pl.BlockSpec(memory_space=pl.ANY)],
        out_specs=pl.BlockSpec(memory_space=pl.ANY),
        scratch_shapes=[
            pltpu.SemaphoreType.DMA,
            pltpu.SemaphoreType.DMA((2, 1, 2, seq_size)),
            pltpu.SemaphoreType.DMA((2, 1, 2, seq_size)),
        ],
        compiler_params=pltpu.CompilerParams(collective_id=collective_id, has_side_effects=True),
    )(shard)


def key_mask(shape, first_key, first_query, tile, far):
    key = first_key + lax.broadcasted_iota(jnp.int32, shape, 0)
    query = first_query + lax.rem(lax.broadcasted_iota(jnp.int32, shape, 1), tile)
    return key > query if far else key <= query


def for_key_tiles(tile_fn, index, tile, span, step, hops, windowed):
    seq = lax.axis_index("seq")
    per_block = span // step
    last = jnp.minimum(seq, hops)
    if windowed:
        @pl.when(seq >= hops)
        def _():
            tile_fn(pl.multiple_of((seq - hops) * span, span), span, "far")

        last = jnp.minimum(seq, hops - 1)

    def past(t, carry):
        tile_fn(pl.multiple_of(t * step, step), step, "")
        return carry

    lax.fori_loop((seq - last) * per_block, seq * per_block, past, 0)
    tile_fn(pl.multiple_of(seq * span, span), (index + 1) * tile, "near")


def head_rows(ref, index, tile):
    block = ref[pl.ds(pl.multiple_of(index * tile, tile), tile), :]
    return jnp.concatenate(
        [block[:, h * HEAD_DIM : (h + 1) * HEAD_DIM] for h in range(ref.shape[1] // HEAD_DIM)], axis=0
    )


def put_head_rows(ref, index, tile, rows):
    for h in range(ref.shape[1] // HEAD_DIM):
        ref[pl.ds(index * tile, tile), h * HEAD_DIM : (h + 1) * HEAD_DIM] = rows[
            h * tile : (h + 1) * tile
        ].astype(ref.dtype)


def attend_kernel(plan, q_ref, kv_ref, o_ref, of_ref, lse_ref, acc, total):
    tile, span, step, hops, windowed = plan
    for i in range(span // tile):
        query = head_rows(q_ref, i, tile)
        rows = query.shape[0]
        acc[...] = jnp.zeros_like(acc)
        total[...] = jnp.zeros_like(total)

        def tile_fn(first, count, mask, i=i, query=query, rows=rows):
            key = kv_ref[pl.ds(first, count), :HEAD_DIM]
            value = kv_ref[pl.ds(first, count), HEAD_DIM:]
            raw = dot_nt(key, query)
            weight = jnp.exp(SOFT_CAP * jnp.tanh(raw * (1.0 / SOFT_CAP)))
            if mask:
                inside = key_mask(weight.shape, 0, i * tile, tile, mask == "far")
                weight = jnp.where(inside, weight, 0.0)
            total[...] += jnp.sum(weight.reshape(count // 8, 8, rows), axis=0)
            acc[...] += dot_tn(value, weight.astype(BF16))

        for_key_tiles(tile_fn, i, tile, span, step, hops, windowed)
        row_total = jnp.sum(total[...], axis=0, keepdims=True)
        out = (acc[...] / row_total).T
        put_head_rows(o_ref, i, tile, out)
        put_head_rows(of_ref, i, tile, out)
        lse_ref[i] = jnp.log(row_total)


def attend_back_kernel(plan, q_ref, do_ref, of_ref, lse_ref, kv_ref, dq_ref, dkv_ref, grads, acc):
    tile, span, step, hops, windowed = plan
    grads[...] = jnp.zeros_like(grads)
    for i in range(span // tile):
        query = head_rows(q_ref, i, tile)
        dout = head_rows(do_ref, i, tile)
        lse = lse_ref[i]
        delta = jnp.sum(dout.astype(F32) * head_rows(of_ref, i, tile), axis=-1, keepdims=True)
        delta = jnp.broadcast_to(delta, (delta.shape[0], LANES)).T[:1]
        acc[...] = jnp.zeros_like(acc)

        def tile_fn(first, count, mask, i=i, query=query, dout=dout, lse=lse, delta=delta):
            key = kv_ref[pl.ds(first, count), :HEAD_DIM]
            value = kv_ref[pl.ds(first, count), HEAD_DIM:]
            bounded = jnp.tanh(dot_nt(key, query) * (1.0 / SOFT_CAP))
            prob = jnp.exp(SOFT_CAP * bounded - lse)
            if mask:
                inside = key_mask(prob.shape, 0, i * tile, tile, mask == "far")
                prob = jnp.where(inside, prob, 0.0)
            dprob = dot_nt(value, dout)
            draw = (prob * (dprob - delta) * (1.0 - bounded * bounded)).astype(BF16)
            grads[pl.ds(first, count), HEAD_DIM:] += dot_nn(prob.astype(BF16), dout)
            grads[pl.ds(first, count), :HEAD_DIM] += dot_nn(draw, query)
            acc[...] += dot_tn(key, draw)

        for_key_tiles(tile_fn, i, tile, span, step, hops, windowed)
        put_head_rows(dq_ref, i, tile, acc[...].T)
    dkv_ref[...] = grads[...].astype(BF16)


def attention_plan(span, seq_size):
    hops = min(WINDOW // span, seq_size - 1)
    return (min(256, span), span, min(512, span), hops, seq_size * span > WINDOW)


def attend(queries, pairs, plan):
    tile, span = plan[:2]
    heads = queries.shape[1] // HEAD_DIM
    rows = heads * tile
    return pl.pallas_call(
        functools.partial(attend_kernel, plan),
        out_shape=(
            jax.ShapeDtypeStruct(queries.shape, BF16),
            jax.ShapeDtypeStruct(queries.shape, F32),
            jax.ShapeDtypeStruct((span // tile, 1, rows), F32),
        ),
        in_specs=[pl.BlockSpec(memory_space=pltpu.VMEM)] * 2,
        out_specs=(pl.BlockSpec(memory_space=pltpu.VMEM),) * 3,
        scratch_shapes=[pltpu.VMEM((HEAD_DIM, rows), F32), pltpu.VMEM((8, rows), F32)],
        compiler_params=pltpu.CompilerParams(vmem_limit_bytes=VMEM_LIMIT),
        cost_estimate=pl.CostEstimate(
            flops=12 * queries.size * span, bytes_accessed=8 * queries.size, transcendentals=0
        ),
    )(queries, pairs)


def attend_back(queries, dout, exact, lse, pairs, plan):
    tile, span = plan[:2]
    rows = queries.shape[1] // HEAD_DIM * tile
    return pl.pallas_call(
        functools.partial(attend_back_kernel, plan),
        out_shape=(
            jax.ShapeDtypeStruct(queries.shape, F32),
            jax.ShapeDtypeStruct(pairs.shape, BF16),
        ),
        in_specs=[pl.BlockSpec(memory_space=pltpu.VMEM)] * 5,
        out_specs=(pl.BlockSpec(memory_space=pltpu.VMEM),) * 2,
        scratch_shapes=[pltpu.VMEM(pairs.shape, F32), pltpu.VMEM((HEAD_DIM, rows), F32)],
        compiler_params=pltpu.CompilerParams(vmem_limit_bytes=VMEM_LIMIT),
    )(queries, dout, exact, lse, pairs)


def remote_copy(src, dst, sems, index, device):
    copy = pltpu.make_async_remote_copy(
        src_ref=src,
        dst_ref=dst,
        send_sem=sems.at[(0, *index)],
        recv_sem=sems.at[(1, *index)],
        device_id=device,
        device_id_type=MESH,
    )
    copy.start()
    return copy


def sum_direct(ready, parts_at, steps, step, mp_size, peer, total, sent, arrived, sems):
    copies = []
    for t in range(steps):
        ready(t)
        for k in range(mp_size - 1, -1, -1):
            part = parts_at(t, k)
            if k == 0:
                total[:, t * step : (t + 1) * step] = part
            else:
                sent[t, k - 1] = part.astype(BF16)
                copies.append(
                    remote_copy(sent.at[t, k - 1], arrived.at[t, k - 1], sems, (t, k - 1), peer(k))
                )
    for t in range(steps):
        for k in range(1, mp_size):
            copies[t * (mp_size - 1) + mp_size - 1 - k].wait_recv()
            total[:, t * step : (t + 1) * step] += arrived[t, k - 1].astype(F32)
    return copies


def sum_square(ready, parts_at, steps, step, peer, total, kept, sent, arrived, sems):
    half = step // 2
    copies, second = [], []

    def second_hop(t):
        copies[2 * t].wait_recv()
        sent[t, 1, 2] = (kept[t, 1] + arrived[t, 0, 1].astype(F32)).astype(BF16)
        second.append(remote_copy(sent.at[t, 1, 2], arrived.at[t, 1, 2], sems, (t, 2), peer(2)))
        copies[2 * t + 1].wait_recv()
        sent[t, 0, 2] = (kept[t, 0] + arrived[t, 1, 1].astype(F32)).astype(BF16)
        second.append(remote_copy(sent.at[t, 0, 2], arrived.at[t, 0, 2], sems, (t, 3), peer(1)))

    for t in range(steps):
        first = t * step
        ready(t)
        far = parts_at(t, 3)
        sent[t, 0, 1] = far[:, :half].astype(BF16)
        sent[t, 1, 1] = far[:, half:].astype(BF16)
        part = parts_at(t, 1)
        sent[t, 0, 0] = part[:, :half].astype(BF16)
        kept[t, 0] = part[:, half:]
        copies.append(
            remote_copy(sent.at[t, 0, pl.ds(0, 2)], arrived.at[t, 0, pl.ds(0, 2)], sems, (t, 0), peer(1))
        )
        part = parts_at(t, 2)
        sent[t, 1, 0] = part[:, half:].astype(BF16)
        kept[t, 1] = part[:, :half]
        copies.append(
            remote_copy(sent.at[t, 1, pl.ds(0, 2)], arrived.at[t, 1, pl.ds(0, 2)], sems, (t, 1), peer(2))
        )
        total[:, first : first + step] = parts_at(t, 0)
    for t in range(steps):
        second_hop(t)
    for t in range(steps):
        first = t * step
        second[2 * t].wait_recv()
        total[:, first : first + half] += arrived[t, 0, 0].astype(F32) + arrived[t, 1, 2].astype(F32)
        second[2 * t + 1].wait_recv()
        total[:, first + half : first + step] += arrived[t, 1, 0].astype(F32) + arrived[t, 0, 2].astype(
            F32
        )
    return copies + second


def row_gather(own, gathered, mp_size, peer, sems):
    share = own.shape[0]
    if mp_size != 4:
        copies = [
            remote_copy(own, gathered.at[pl.ds(k * share, share)], sems, (k,), peer(k))
            for k in range(mp_size - 1, 0, -1)
        ]

        def finish():
            for copy in copies:
                copy.wait()

        return lambda: None, finish

    half = share // 2

    def place(k, lower):
        return gathered.at[pl.ds(k * share + lower * half, half)]

    upper, lower = own.at[pl.ds(0, half)], own.at[pl.ds(half, half)]
    to_one = remote_copy(upper, place(1, 0), sems, (0,), peer(1))
    to_two = remote_copy(lower, place(2, 1), sems, (1,), peer(2))
    copies = [
        remote_copy(upper, place(2, 0), sems, (2,), peer(2)),
        remote_copy(lower, place(1, 1), sems, (3,), peer(1)),
    ]

    def pass_on():
        to_one.wait_recv()
        copies.append(remote_copy(place(1, 0), place(3, 0), sems, (4,), peer(2)))
        to_two.wait_recv()
        copies.append(remote_copy(place(2, 1), place(3, 1), sems, (5,), peer(1)))

    def finish():
        to_one.wait_send()
        to_two.wait_send()
        for copy in copies:
            copy.wait()

    return pass_on, finish


def rows_kernel(plan, rows_fn, *refs):
    mp_size, share, step, row_step, natural, n_left, n_aux, n_out, gather = plan
    lefts, weight_ref, refs = refs[:n_left], refs[n_left], refs[n_left + 1 :]
    aux, refs = refs[:n_aux], refs[n_aux:]
    outs, refs = refs[:n_out], refs[n_out:]
    if gather:
        gathered, refs = refs[0], refs[1:]
    left, weight, total, own, kept, sent, arrived, in_sem, sum_sem, row_sem = refs
    steps = total.shape[1] // step
    dp, seq, mp = lax.axis_index("dp"), lax.axis_index("seq"), lax.axis_index("mp")

    def peer(k):
        return (dp, seq, flipped(mp, k))

    left_copies, weight_copies = {}, []
    for k in range(mp_size):
        first = (flipped(mp, k) if natural else k) * share
        left_copies[k] = []
        column = 0
        for i, ref in enumerate(lefts):
            depth = ref.shape[1]
            left_copies[k].append(
                pltpu.make_async_copy(
                    ref.at[pl.ds(first, share)],
                    left.at[k, :, pl.ds(column, depth)],
                    in_sem.at[2 + k * n_left + i],
                )
            )
            column += depth
    for t in range(steps):
        weight_copies.append(
            pltpu.make_async_copy(
                weight_ref.at[pl.ds(t * step, step)], weight.at[t % 2], in_sem.at[t % 2]
            )
        )
    weight_copies[0].start()
    for k in range(mp_size - 1, -1, -1):
        for copy in left_copies[k]:
            copy.start()

    barrier = pltpu.get_barrier_semaphore()
    for k in range(1, mp_size):
        pl.semaphore_signal(barrier, inc=1, device_id=peer(k), device_id_type=MESH)
    pl.semaphore_wait(barrier, mp_size - 1)

    def ready(t):
        weight_copies[t].wait()
        if t + 1 < steps:
            weight_copies[t + 1].start()

    def parts_at(t, k):
        if t == 0:
            for copy in left_copies[k]:
                copy.wait()
        return dot_nt(left[k], weight[t % 2])

    finish_rows(
        ready,
        parts_at,
        (mp_size, share, step, row_step),
        (rows_fn, aux, outs, gathered if gather else None),
        peer,
        (total, own, kept, sent, arrived),
        (sum_sem, row_sem, in_sem.at[0]),
    )


def finish_rows(ready, parts_at, sizes, rows, peer, buffers, sems):
    mp_size, share, step, row_step = sizes
    rows_fn, aux, outs, gathered = rows
    total, own, kept, sent, arrived = buffers
    sum_sem, row_sem, keep_sem = sems
    steps = total.shape[1] // step
    if mp_size == 4:
        sums = sum_square(
            ready, parts_at, steps, step, peer, total, kept, sent, arrived, sum_sem
        )
    else:
        sums = sum_direct(
            ready, parts_at, steps, step, mp_size, peer, total, sent, arrived, sum_sem
        )

    def rows_at(r, carry):
        rows = pl.ds(pl.multiple_of(r * row_step, row_step), row_step)
        result = rows_fn(total[rows, :], rows, aux, outs)
        if gathered is not None:
            result = result.astype(BF16)
            if len(own.shape) == 2:
                own[rows, :] = result
            else:
                for t in range(steps):
                    own[t, rows, :] = result[:, t * step : (t + 1) * step]
        return carry

    for ref in outs:
        if ref.shape[0] == 8:
            ref[...] = jnp.zeros_like(ref)
    lax.fori_loop(0, share // row_step, rows_at, 0)
    if gathered is not None:
        first = own if len(own.shape) == 2 else own.at[0]
        keep = pltpu.make_async_copy(first, gathered.at[pl.ds(0, share)], keep_sem)
        keep.start()
        pass_on, finish = row_gather(first, gathered, mp_size, peer, row_sem)
        pass_on()
        finish()
        keep.wait()
    for copy in sums:
        copy.wait_send()


def row_plan(width, share, mp_size):
    step = 768 if width % 768 == 0 else width
    steps = width // step
    if mp_size == 4:
        pieces, kept = (steps, 2, 3, share, step // 2), (steps, 2, share, step // 2)
    else:
        pieces, kept = (steps, mp_size - 1, share, step), (8, LANES)
    buffers = [
        pltpu.VMEM((share, width), F32),
        pltpu.VMEM((share, width), BF16),
        pltpu.VMEM(kept, F32),
        pltpu.VMEM(pieces, BF16),
        pltpu.VMEM(pieces, BF16),
    ]
    sems = [
        pltpu.SemaphoreType.DMA((2, steps, max(4, mp_size - 1))),
        pltpu.SemaphoreType.DMA((2, max(6, mp_size))),
    ]
    return step, min(64, share), buffers, sems


def sum_rows(lefts, weight, rows_fn, aux, outs, gather, natural, mp_size, collective_id):
    span = lefts[0].shape[0]
    width, depth = weight.shape
    share = span // mp_size
    step, row_step, buffers, sems = row_plan(width, share, mp_size)
    plan = (mp_size, share, step, row_step, natural, len(lefts), len(aux), len(outs), gather)
    out_shape = [jax.ShapeDtypeStruct((rows, width), dtype) for rows, dtype in outs]
    out_specs = [pl.BlockSpec(memory_space=pltpu.VMEM)] * len(outs)
    if gather:
        out_shape.append(jax.ShapeDtypeStruct((span, width), BF16))
        out_specs.append(pl.BlockSpec(memory_space=pl.ANY))
    return pl.pallas_call(
        functools.partial(rows_kernel, plan, rows_fn),
        out_shape=out_shape,
        in_specs=[pl.BlockSpec(memory_space=pl.ANY)] * (len(lefts) + 1)
        + [pl.BlockSpec(memory_space=pltpu.VMEM)] * len(aux),
        out_specs=out_specs,
        scratch_shapes=[
            pltpu.VMEM((mp_size, share, depth), BF16),
            pltpu.VMEM((2, step, depth), BF16),
            *buffers,
            pltpu.SemaphoreType.DMA((2 + mp_size * len(lefts),)),
            *sems,
        ],
        compiler_params=pltpu.CompilerParams(
            collective_id=collective_id, has_side_effects=True, vmem_limit_bytes=VMEM_LIMIT
        ),
    )(*lefts, weight, *aux)


def weight_grad_kernel(plan, *refs):
    n_right, tile, half, first_column, n_into, steps, mp_size = plan
    left_ref, rights, refs = refs[0], refs[1 : 1 + n_right], refs[1 + n_right + n_into :]
    out_ref, refs = refs[0], refs[1:]
    if steps:
        steps_ref, gathered, refs = left_ref, refs[: len(steps)], refs[len(steps) :]
        own_rows, row_sems, refs = refs[0], refs[1 : 1 + len(steps)], refs[1 + len(steps) :]
        left_ref = gathered[0]
    left, right, sent, arrived, own, result, in_sem, swap_sem, out_sem = refs
    dp, seq, mp = lax.axis_index("dp"), lax.axis_index("seq"), lax.axis_index("mp")
    other = (1 - dp, seq, mp)

    def peer(k):
        return (dp, seq, flipped(mp, k))

    if steps:
        rows_load = pltpu.make_async_copy(
            steps_ref.at[pl.ds(steps[0], len(steps))], own_rows, in_sem.at[4]
        )
        rows_load.start()
    lefts = []
    for i, side in enumerate((1 - dp, dp)):
        columns = pl.ds(pl.multiple_of(side * half, LANES), half)
        lefts.append(pltpu.make_async_copy(left_ref.at[:, columns], left.at[i], in_sem.at[2 + i]))
    sources = []
    for ref in rights:
        for first in range(0, ref.shape[1], tile):
            sources.append(ref.at[:, pl.ds(first, tile)])
    tiles = len(sources)
    loads = [
        pltpu.make_async_copy(source, right.at[t % 2], in_sem.at[t % 2])
        for t, source in enumerate(sources)
    ]
    loads[0].start()
    barrier = pltpu.get_barrier_semaphore()
    pl.semaphore_signal(barrier, inc=1, device_id=other, device_id_type=MESH)
    if steps:
        for k in range(1, mp_size):
            pl.semaphore_signal(barrier, inc=1, device_id=peer(k), device_id_type=MESH)
    pl.semaphore_wait(barrier, mp_size if steps else 1)
    if steps:
        rows_load.wait()
        share = own_rows.shape[1]
        keeps = [
            pltpu.make_async_copy(own_rows.at[n], gathered[n].at[pl.ds(0, share)], in_sem.at[4 + n])
            for n in range(len(steps))
        ]
        for copy in keeps:
            copy.start()
        pass_on, end_rows = row_gather(own_rows.at[0], gathered[0], mp_size, peer, row_sems[0])
        pass_on()
        end_rows()
        keeps[0].wait()
        rest = [
            row_gather(own_rows.at[n], gathered[n], mp_size, peer, row_sems[n])
            for n in range(1, len(steps))
        ]
    for copy in lefts:
        copy.start()
    swaps, stores = [], []

    def finish(t):
        swaps[t].wait_recv()
        if t >= 2:
            stores[t - 2].wait()
        result[t % 2] = (own[t % 2] + arrived[t].astype(F32)).astype(BF16)
        stores.append(
            pltpu.make_async_copy(
                result.at[t % 2],
                out_ref.at[:, pl.ds(first_column + t * tile, tile)],
                out_sem.at[t % 2],
            )
        )
        stores[t].start()

    for t in range(tiles):
        loads[t].wait()
        if t + 1 < tiles:
            loads[t + 1].start()
        if t == 0:
            lefts[0].wait()
        sent[t] = dot_tn(left[0], right[t % 2]).astype(BF16)
        swaps.append(remote_copy(sent.at[t], arrived.at[t], swap_sem, (t,), other))
        if t == 0:
            lefts[1].wait()
        own[t % 2] = dot_tn(left[1], right[t % 2])
        if t >= 1:
            finish(t - 1)
        if t == tiles // 2 and steps:
            for pass_on, _ in rest:
                pass_on()
    finish(tiles - 1)
    for store in stores[-2:]:
        store.wait()
    for swap in swaps:
        swap.wait_send()
    if steps:
        for copy in keeps[1:]:
            copy.wait()
        for _, end_rows in rest:
            end_rows()


def weight_grad(left, rights, collective_id, into=None, columns=0, steps=(), mp_size=1):
    rows, width = rights[0].shape[0], left.shape[-1]
    half = width // 2
    total = sum(right.shape[1] for right in rights)
    tile = next(
        t
        for t in (768, 512, 384, 256, LANES)
        if total >= 2 * t and all(right.shape[1] % t == 0 for right in rights)
    )
    tiles = total // tile
    first = 0 if into is None else into.shape[1] - total
    earlier = () if into is None else (into,)
    out_shape = [jax.ShapeDtypeStruct((half, first + total + columns), BF16)]
    scratch = []
    if steps:
        out_shape += [jax.ShapeDtypeStruct((rows, width), BF16)] * len(steps)
        scratch = [pltpu.VMEM((len(steps), *left.shape[1:]), BF16)]
        scratch += [pltpu.SemaphoreType.DMA((2, max(6, mp_size)))] * len(steps)
    plan = (len(rights), tile, half, first, len(earlier), tuple(steps), mp_size)
    results = pl.pallas_call(
        functools.partial(weight_grad_kernel, plan),
        out_shape=out_shape,
        in_specs=[pl.BlockSpec(memory_space=pl.ANY)] * (1 + len(rights) + len(earlier)),
        out_specs=[pl.BlockSpec(memory_space=pl.ANY)] * len(out_shape),
        input_output_aliases={} if into is None else {1 + len(rights): 0},
        scratch_shapes=[
            *scratch,
            pltpu.VMEM((2, rows, half), BF16),
            pltpu.VMEM((2, rows, tile), BF16),
            pltpu.VMEM((tiles, half, tile), BF16),
            pltpu.VMEM((tiles, half, tile), BF16),
            pltpu.VMEM((2, half, tile), F32),
            pltpu.VMEM((2, half, tile), BF16),
            pltpu.SemaphoreType.DMA((4 + max(1, len(steps)),)),
            pltpu.SemaphoreType.DMA((2, tiles)),
            pltpu.SemaphoreType.DMA((2,)),
        ],
        compiler_params=pltpu.CompilerParams(
            collective_id=collective_id, has_side_effects=True, vmem_limit_bytes=VMEM_LIMIT
        ),
    )(left, *rights, *earlier)
    return results if steps else results[0]


def ffw_kernel(plan, normed_ref, gate_up_ref, shard_ref, resid_ref, cotangent_ref, gain_ref, *refs):
    mp_size, seq_size, share, step, row_step, tile = plan
    output_ref, gain_grad_ref, own_ref, dmixed_ref, hidden_ref, act_ref, slope_ref, down_ref = refs[:8]
    normed, gate_up, hidden, down, staged, *refs = refs[8:]
    buffers, refs = refs[:5], refs[5:]
    load_sem, store_sem, local_sem, line_sem, pair_sem, sum_sem, row_sem = refs
    steps, _, units = down.shape
    piece = step // (2 * seq_size)
    far = seq_size - 1
    dp, seq, mp = lax.axis_index("dp"), lax.axis_index("seq"), lax.axis_index("mp")
    sibling = (1 - dp, seq, mp)

    def peer(k):
        return (dp, seq, flipped(mp, k))

    def block(t, at):
        first = pl.multiple_of((dp * seq_size + at) * piece, piece)
        return down.at[t, pl.ds(first, piece)]

    start, share_piece, arrival, complete, drain = travel(block, line_sem, pair_sem, seq_size)
    normed_load = pltpu.make_async_copy(normed_ref, normed, local_sem.at[0])
    normed_load.start()
    shard_loads = [
        pltpu.make_async_copy(
            shard_ref.at[pl.ds(t * piece, piece)], block(t, seq), local_sem.at[1 + t]
        )
        for t in range(steps)
    ]
    for load in shard_loads:
        load.start()

    def loads(i, slot):
        return [
            pltpu.make_async_copy(
                gate_up_ref.at[:, pl.ds(pl.multiple_of(side * units + i * tile, LANES), tile)],
                gate_up.at[slot, side],
                load_sem.at[slot, side],
            )
            for side in range(2)
        ]

    def stores(i, slot):
        columns = pl.ds(pl.multiple_of(i * tile, LANES), tile)
        return [
            pltpu.make_async_copy(staged.at[slot, 0], act_ref.at[:, columns], store_sem.at[slot, 0]),
            pltpu.make_async_copy(staged.at[slot, 1], slope_ref.at[:, columns], store_sem.at[slot, 1]),
        ]

    for load in loads(0, 0):
        load.start()
    barrier = pltpu.get_barrier_semaphore()
    for k in range(1, mp_size):
        pl.semaphore_signal(barrier, inc=1, device_id=peer(k), device_id_type=MESH)
    pl.semaphore_signal(barrier, inc=1, device_id=sibling, device_id_type=MESH)
    for way in range(2):
        @pl.when(seq < far if way == 0 else seq > 0)
        def _(way=way):
            pl.semaphore_signal(
                barrier, inc=1, device_id=(dp, seq + 1 - 2 * way, mp), device_id_type=MESH
            )

    line_peers = (seq + far) // seq_size + (2 * far - seq) // seq_size
    pl.semaphore_wait(barrier, mp_size + line_peers)

    for t in range(steps):
        shard_loads[t].wait()
        start(t)
    for t in range(steps):
        share_piece(t)
    normed_load.wait()
    arrivals = [(t, distance) for distance in range(1, seq_size) for t in range(steps)]
    tiles = units // tile
    early = [(2 * n + 2, event) for n, event in enumerate(arrivals) if 2 * n + 2 < tiles]
    late = arrivals[len(early) :]

    def units_at(i, carry):
        slot = lax.rem(i, 2)
        for load in loads(i, slot):
            load.wait()

        @pl.when(i + 1 < tiles)
        def _():
            for load in loads(i + 1, 1 - slot):
                load.start()

        @pl.when(i >= 2)
        def _():
            for store in stores(i - 2, slot):
                store.wait()

        gate = dot_nn(normed[...], gate_up[slot, 0])
        up = dot_nn(normed[...], gate_up[slot, 1])
        squared = gate * gate
        bend = jnp.tanh(GELU_SCALE * gate * (1.0 + GELU_CUBE * squared))
        side = 0.5 * (1.0 + bend)
        act = gate * side
        slope = side + (0.5 * GELU_SCALE) * gate * (1.0 - bend * bend) * (1.0 + 3.0 * GELU_CUBE * squared)
        staged[slot, 0] = act.astype(BF16)
        staged[slot, 1] = (slope * up).astype(BF16)
        for store in stores(i, slot):
            store.start()
        product = (act * up).astype(BF16)
        for k in range(mp_size):
            hidden[k, :, pl.ds(pl.multiple_of(i * tile, LANES), tile)] = product[
                k * share : (k + 1) * share
            ]
        for at, event in early:
            @pl.when(i == at)
            def _(event=event):
                arrival(*event)

        return carry

    lax.fori_loop(0, tiles, units_at, 0)
    for i in range(max(0, tiles - 2), tiles):
        for store in stores(i, i % 2):
            store.wait()
    hidden_stores = [
        pltpu.make_async_copy(hidden.at[k], hidden_ref.at[pl.ds(k * share, share)], local_sem.at[1 + k])
        for k in range(mp_size)
    ]
    for store in hidden_stores:
        store.start()
    down_stores = [
        pltpu.make_async_copy(
            down.at[t], down_ref.at[pl.ds(t * step, step)], local_sem.at[1 + mp_size + t]
        )
        for t in range(steps)
    ]
    waiting = list(late)

    def ready(t):
        while (t, far) in waiting:
            arrival(*waiting.pop(0))
        complete(t)
        down_stores[t].start()

    def parts_at(t, k):
        return dot_nt(hidden[k], down[t])

    finish_rows(
        ready,
        parts_at,
        (mp_size, share, step, row_step),
        (after_ffw, (resid_ref, cotangent_ref, gain_ref), (output_ref, gain_grad_ref), dmixed_ref),
        peer,
        buffers,
        (sum_sem, row_sem, local_sem.at[0]),
    )
    own_store = pltpu.make_async_copy(buffers[1], own_ref, local_sem.at[0])
    own_store.start()
    for store in hidden_stores + down_stores:
        store.wait()
    own_store.wait()
    for t in range(steps):
        drain(t)


def ffw(normed, gate_up_w, down_shard, resid, cotangent, gain, sizes, collective_id):
    dp_size, seq_size, mp_size = sizes
    span, width = normed.shape
    units = gate_up_w.shape[1] // 2
    share = span // mp_size
    step, row_step, buffers, sems = row_plan(width, share, mp_size)
    steps = width // step
    buffers[1] = pltpu.VMEM((steps, share, step), BF16)
    tile = 256 if units % 256 == 0 else LANES
    plan = (mp_size, seq_size, share, step, row_step, tile)
    per_unit = jax.ShapeDtypeStruct((span, units), BF16)
    return pl.pallas_call(
        functools.partial(ffw_kernel, plan),
        out_shape=(
            jax.ShapeDtypeStruct((share, width), BF16),
            jax.ShapeDtypeStruct((8, width), F32),
            jax.ShapeDtypeStruct((steps, share, step), BF16),
            jax.ShapeDtypeStruct((span, step), BF16),
            per_unit,
            per_unit,
            per_unit,
            jax.ShapeDtypeStruct((width, units), BF16),
        ),
        in_specs=[pl.BlockSpec(memory_space=pl.ANY)] * 3 + [pl.BlockSpec(memory_space=pltpu.VMEM)] * 3,
        out_specs=(pl.BlockSpec(memory_space=pltpu.VMEM),) * 2 + (pl.BlockSpec(memory_space=pl.ANY),) * 6,
        scratch_shapes=[
            pltpu.VMEM((span, width), BF16),
            pltpu.VMEM((2, 2, width, tile), BF16),
            pltpu.VMEM((mp_size, share, units), BF16),
            pltpu.VMEM((steps, step, units), BF16),
            pltpu.VMEM((2, 2, span, tile), BF16),
            *buffers,
            pltpu.SemaphoreType.DMA((2, 2)),
            pltpu.SemaphoreType.DMA((2, 2)),
            pltpu.SemaphoreType.DMA((1 + mp_size + steps,)),
            pltpu.SemaphoreType.DMA((2, steps, 2, seq_size)),
            pltpu.SemaphoreType.DMA((2, steps, 2, seq_size)),
            *sems,
        ],
        compiler_params=pltpu.CompilerParams(
            collective_id=collective_id, has_side_effects=True, vmem_limit_bytes=VMEM_LIMIT
        ),
    )(normed, gate_up_w, down_shard, resid, cotangent, gain)


def hidden_back_kernel(n_parts, *refs):
    parts, (down_ref, act_ref, slope_ref, dgate_ref, dup_ref) = refs[:n_parts], refs[n_parts:]
    first, dhidden = 0, 0.0
    for part in parts:
        depth = part.shape[1]
        dhidden = dhidden + dot_nn(part[...], down_ref[first : first + depth, :])
        first += depth
    dgate_ref[...] = (dhidden * slope_ref[...].astype(F32)).astype(BF16)
    dup_ref[...] = (dhidden * act_ref[...].astype(F32)).astype(BF16)


def hidden_back(dmixed, down_wt, act, slope):
    rows, depth = dmixed[0].shape
    width, units = down_wt.shape
    tile = 256 if units % 256 == 0 else units
    columns = pl.BlockSpec((rows, tile), lambda i: (0, i))
    return pl.pallas_call(
        functools.partial(hidden_back_kernel, len(dmixed)),
        grid=(units // tile,),
        out_shape=(jax.ShapeDtypeStruct((rows, units), BF16),) * 2,
        in_specs=[pl.BlockSpec((rows, depth), lambda i: (0, 0))] * len(dmixed)
        + [pl.BlockSpec((width, tile), lambda i: (0, i)), columns, columns],
        out_specs=(columns, columns),
        compiler_params=pltpu.CompilerParams(vmem_limit_bytes=VMEM_LIMIT),
    )(*dmixed, down_wt, act, slope)


def fold_rows(x):
    return jnp.sum(x.reshape(x.shape[0] // 8, 8, x.shape[1]), axis=0)


def after_attention(attn, rows, aux, outs):
    tokens, gain_two, gain_three = aux
    attn_out, resid_out = outs
    resid = tokens[rows, :].astype(F32) + attn * rms_scale(attn) * gain_two[...]
    attn_out[rows, :] = attn
    resid_out[rows, :] = resid
    return resid * rms_scale(resid) * gain_three[...]


def after_ffw(mixed, rows, aux, outs):
    resid, cotangent, gain_four = aux
    output, gain_grad = outs
    scale = rms_scale(mixed)
    unit = mixed * scale
    grad_out = cotangent[rows, :].astype(F32)
    output[rows, :] = (resid[rows, :] + unit * gain_four[...]).astype(BF16)
    gain_grad[...] += fold_rows(grad_out * unit)
    return vector_back(grad_out, unit, scale, gain_four[...])


def vector_back(grad_in, unit, scale, gain):
    unit_grad = grad_in * gain
    return scale * (unit_grad - unit * jnp.mean(unit_grad * unit, axis=-1, keepdims=True))


def before_ffw(dnormed_two, rows, aux, outs):
    resid, attn, cotangent, gain_two, gain_three = aux
    dresid_out, gain_two_grad, gain_three_grad = outs
    scale = rms_scale(resid[rows, :])
    unit = resid[rows, :] * scale
    gain_three_grad[...] += fold_rows(dnormed_two * unit)
    dresid = cotangent[rows, :].astype(F32) + vector_back(dnormed_two, unit, scale, gain_three[...])
    dresid_out[rows, :] = dresid
    scale = rms_scale(attn[rows, :])
    unit = attn[rows, :] * scale
    gain_two_grad[...] += fold_rows(dresid * unit)
    return vector_back(dresid, unit, scale, gain_two[...])


def before_attention(dnormed_one, rows, aux, outs):
    tokens, dresid, gain_one = aux
    tokens_grad, gain_grad = outs
    vector = tokens[rows, :].astype(F32)
    scale = rms_scale(vector)
    unit = vector * scale
    gain_grad[...] += fold_rows(dnormed_one * unit)
    back = vector_back(dnormed_one, unit, scale, gain_one[...])
    tokens_grad[rows, :] = (dresid[rows, :] + back).astype(BF16)


def swapped(x, axis, k):
    return lax.ppermute(x, axis, [(i, i ^ k) for i in range(lax.axis_size(axis))])


def shards(
    tokens,
    cotangent,
    pre_attn_gain,
    w_query,
    w_key,
    w_value,
    w_out,
    post_attn_gain,
    pre_ffw_gain,
    w_gate,
    w_up,
    w_down,
    post_ffw_gain,
):
    dp_size, seq_size, mp_size = (lax.axis_size(axis) for axis in ("dp", "seq", "mp"))
    dp, seq, mp = lax.axis_index("dp"), lax.axis_index("seq"), lax.axis_index("mp")
    both = ("dp", "seq")
    heads = w_query.shape[1] // HEAD_DIM
    q_width = heads * HEAD_DIM
    span = tokens.shape[1]
    width = tokens.shape[2]
    share = span // mp_size
    plan = attention_plan(span, seq_size)

    def gather_weight(x):
        return lax.all_gather(x, both, axis=0, tiled=True)

    sizes = (dp_size, seq_size, mp_size)
    gain_rows, own_pair, cosine, sine, normed_one, w_qkv = front(
        tokens[0],
        w_query,
        w_key,
        w_value,
        [pre_attn_gain, post_attn_gain, pre_ffw_gain, post_ffw_gain],
        heads,
        sizes,
    )
    gain_one, gain_two, gain_three, gain_four = (gain_rows[i : i + 1, :width] for i in range(4))
    pairs = lax.all_gather(own_pair, "seq", axis=0, tiled=True)
    w_out_t = carry(after(w_out.T, own_pair), sizes, 30)
    query_lin = dot_nn(after(normed_one, pairs), w_qkv[:, :q_width]).reshape(span, heads, HEAD_DIM)
    queries = rotary(query_lin, cosine[:, None], sine[:, None], 1.0) * HEAD_DIM ** (-0.5)
    queries = queries.astype(BF16).reshape(span, q_width)

    units = w_gate.shape[1]
    gate_up_w = gather_weight(after(jnp.concatenate([w_gate, w_up], axis=1), pairs, w_out_t))

    attn_o, attn_exact, lse = attend(queries, pairs, plan)
    own_first = mp * share
    tokens_own = lax.dynamic_slice_in_dim(tokens[0], own_first, share, 0)
    cotangent_own = lax.dynamic_slice_in_dim(cotangent[0], own_first, share, 0)

    def by_owner(x):
        return jnp.concatenate(
            [lax.dynamic_slice_in_dim(x, (mp ^ k) * share, share, 0) for k in range(mp_size)], axis=0
        )

    attn, resid, normed_two = sum_rows(
        (attn_o,),
        w_out_t,
        after_attention,
        (tokens_own, gain_two, gain_three),
        ((share, F32), (share, F32)),
        True,
        True,
        mp_size,
        3,
    )
    shard_count = dp_size * seq_size
    steps = width // row_plan(width, share, mp_size)[0]

    def to_steps(x):
        return jnp.swapaxes(x.reshape(x.shape[0], shard_count, steps, -1), 1, 2).reshape(x.shape)

    def to_shards(x):
        return jnp.swapaxes(x.reshape(x.shape[0], steps, shard_count, -1), 1, 2).reshape(x.shape)

    output, grad_gain_four, dmixed_own, dmixed_first, hidden, gate_act, slope, down_wt = ffw(
        normed_two,
        gate_up_w,
        w_down.T,
        to_steps(resid),
        to_steps(cotangent_own),
        to_steps(gain_four),
        sizes,
        4,
    )
    output = to_shards(output)
    grad_gain_four = to_shards(grad_gain_four)

    def spread(x):
        return lax.psum_scatter(x, "seq", scatter_dimension=0, tiled=True)

    grad_sums = [weight_grad(dmixed_first, (hidden,), 20)]
    grad_sum, *arrived = weight_grad(
        after(dmixed_own, grad_sums[0]),
        (hidden,),
        21,
        columns=units * (steps - 2),
        steps=tuple(range(1, steps)),
        mp_size=mp_size,
    )
    for t in range(2, steps):
        grad_sum = weight_grad(
            arrived[t - 1], (hidden,), 20 + t, into=grad_sum, columns=units * (steps - 1 - t)
        )
    grad_sums.append(grad_sum)
    dmixed_low = [dmixed_first, *arrived]
    grad_down_first = spread(grad_sums[0])
    grad_down_rest = spread(after(grad_sums[-1], grad_down_first))
    grad_down = [grad_down_first] + [
        grad_down_rest[:, t * units : (t + 1) * units] for t in range(steps - 1)
    ]
    grad_down = jnp.concatenate(grad_down, axis=0).astype(F32).T
    dgate_low, dup_low = hidden_back(
        (after(dmixed_low[0], grad_sum), *dmixed_low[1:]), down_wt, gate_act, slope
    )
    grad_gate_up_sum = weight_grad(normed_two, (dgate_low, dup_low), 8)
    dresid, grad_gain_two, grad_gain_three, dattn_low = sum_rows(
        (after(dgate_low, grad_down_rest, grad_gate_up_sum), dup_low),
        gate_up_w,
        before_ffw,
        (resid, attn, cotangent_own, gain_two, gain_three),
        ((share, F32), (8, F32), (8, F32)),
        True,
        False,
        mp_size,
        5,
    )
    grad_gate_up = spread(after(grad_gate_up_sum, grad_down_rest))

    dattn_o = by_owner(dot_nn(dattn_low, w_out_t)).astype(BF16)
    dquery, dpairs = attend_back(queries, dattn_o, attn_exact, lse, pairs, plan)
    grad_out_sum = weight_grad(dattn_low, (by_owner(attn_o),), 9)
    dquery = dquery.reshape(span, heads, HEAD_DIM)
    dquery_low = (
        rotary(dquery * HEAD_DIM ** (-0.5), cosine[:, None], sine[:, None], -1.0).reshape(span, q_width).astype(BF16)
    )
    grad_q_sum = weight_grad(normed_one, (dquery_low,), 10, columns=2 * HEAD_DIM)
    own_grads = spread(after(dpairs, grad_gate_up, grad_out_sum, grad_q_sum)).astype(F32)
    grad_gate = grad_gate_up[:, :units].astype(F32)
    grad_up = grad_gate_up[:, units:].astype(F32)
    own_grads = after(own_grads, grad_gate, grad_up, grad_down)
    dkey_rot = own_grads[:, :HEAD_DIM]
    dkey_low = rotary(dkey_rot, cosine, sine, -1.0).astype(BF16)
    dvalue_low = own_grads[:, HEAD_DIM:].astype(BF16)
    dkv_low = jnp.concatenate([dkey_low, dvalue_low], axis=1)
    grad_qkv_sum = weight_grad(normed_one, (dkv_low,), 11, into=grad_q_sum)
    grad_qkv = spread(grad_qkv_sum)
    tokens_grad, grad_gain_one = sum_rows(
        (dquery_low, after(dkv_low, grad_qkv_sum)),
        w_qkv,
        before_attention,
        (tokens_own, dresid, gain_one),
        ((share, BF16), (8, F32)),
        False,
        True,
        mp_size,
        6,
    )

    grad_out_t = spread(after(grad_out_sum, grad_qkv, tokens_grad))
    gain_grads, grad_key, grad_value = last_sums(
        [
            jnp.sum(grad, axis=0)
            for grad in (grad_gain_one, grad_gain_two, grad_gain_three, grad_gain_four)
        ],
        grad_qkv[:, q_width:],
        w_key.shape[1],
        heads,
        sizes,
    )
    grad_key, grad_value = grad_key.astype(F32), grad_value.astype(F32)
    grad_out_t = after(grad_out_t, grad_key, grad_value)
    return (
        output[None],
        tokens_grad[None],
        gain_grads[0],
        after(grad_qkv, grad_key)[:, :q_width].astype(F32),
        grad_key,
        grad_value,
        grad_out_t.astype(F32).T,
        gain_grads[1],
        gain_grads[2],
        grad_gate,
        grad_up,
        grad_down,
        gain_grads[3],
    )


def solution(mesh):
    weight = P(("dp", "seq"), "mp")
    whole_rows = P(("dp", "seq"), None)
    columns = P("mp", ("dp", "seq"))
    gain = P(("dp", "seq"))
    tokens = P("dp", "seq", None)
    rows = P("dp", ("seq", "mp"), None)
    in_specs = (
        tokens,
        tokens,
        gain,
        weight,
        whole_rows,
        whole_rows,
        columns,
        gain,
        gain,
        weight,
        weight,
        columns,
        gain,
    )
    out_specs = (
        rows,
        rows,
        gain,
        weight,
        whole_rows,
        whole_rows,
        columns,
        gain,
        gain,
        weight,
        weight,
        columns,
        gain,
    )
    return jax.shard_map(shards, mesh=mesh, in_specs=in_specs, out_specs=out_specs, check_vma=False)
```
